256 devices in a mesh: group: 8 (over y, core), dev: 32 (over x, z).
Axes of the slice: x: 4, y: 4, z: 8, core: 2. Of those that a mesh axis runs over, the one named last changes fastest.
Arguments:
- residual: float32 [192, 768, 144], P('group', 'dev'), may hold values from -6 to 6
- fdm_vectors: float32 [3, 8, 8, 98304], P(None, None, None, ('group', 'dev')), may hold values from -2 to 2
- fdm_values: float32 [3, 8, 98304], P(None, None, ('group', 'dev')), may hold values from 0.1 to 10
- corner_slot: int32 [8, 98304], P(None, ('group', 'dev')), may hold values from 0 to 624, as said below
- x_local: float32 [163840, 128], P(('group', 'dev')), may hold values from -0.07848767 to 0.07848767
- x_middle: float32 [163840, 128], P(('group', 'dev')), may hold values from -0.033 to 0.033
- x_top: float32 [163840, 128], P(('group', 'dev')), may hold values from -0.019621918 to 0.019621918
Outputs:
- preconditioned: float32 [192, 768, 144], P('group', 'dev')
The draws below stay inside these ranges and needn't reach their ends.
Inputs may be any that keep to these rules, and one draw needn't show every extreme that they name: `corner_slot`: within a block the corners of its 384 elements that coincide share one slot and distinct vertices of the block have distinct slots; the 625 vertices of each block take the slots 0 to 624 in an order drawn per block.
All inputs are finite; a program needn't handle non-finite values.
Results may differ from the reference program's by a relative error of at most 0.0001.
Values sent between devices are 32-bit elements; how exact they have to be, the bound alone decides.
A program may use at most 64 MiB of HBM per device.

```python
import math
import jax
import jax.numpy as jnp
from jax import lax

BX = 4
BY = 4
BZ = 24
N_LOC = 128
N_MID = 128
N_TOP = 128
E_DEV = 384
ELEMS = 98304
NXG = 192
NYG = 768
NZG = 144
NVERT = 625
NV_PAD = 640
N_GROUP = 8
N_DEV = 32
DEVICES = 256


def draw_corner_slot(key, part):
    key = jax.random.fold_in(key, 11)
    blocks = ELEMS // E_DEV
    element = jnp.arange(E_DEV, dtype=jnp.int32)
    along_z = element % BZ
    along_y = element // BZ % BY
    along_x = element // (BZ * BY)
    corner = jnp.arange(8, dtype=jnp.int32)
    corner_x = corner // 4
    corner_y = corner // 2 % 2
    corner_z = corner % 2
    vertex = ((along_x[None, :] + corner_x[:, None]) * (BY + 1) + (along_y[None, :] + corner_y[:, None])) * (BZ + 1) + along_z[None, :] + corner_z[:, None]

    def shuffle(subkey):
        return jax.random.permutation(subkey, NVERT).astype(jnp.int32)
    orders = jax.vmap(shuffle)(jax.random.split(key, blocks))
    slots_all = orders[:, vertex]
    return jnp.transpose(slots_all, (1, 0, 2)).reshape(8, ELEMS).astype(jnp.int32)


def shard_levels(own_key, extent, cuts, smallest, high):
    gain = 1.0
    for dim, shards_of in cuts:
        steps = jax.random.uniform(jax.random.fold_in(jax.random.fold_in(own_key, 6), dim), (shards_of,), jnp.float32, smallest / len(cuts), high / len(cuts))
        gain = gain * jnp.repeat(jnp.exp(steps), extent[dim] // shards_of).reshape((-1,) + (1,) * (len(extent) - 1 - dim))
    return gain


def noise(rng, dims, scale, reach, pieces=(), kind=jnp.bfloat16):
    entries = scale * jax.random.normal(rng, dims, jnp.float32)
    if pieces:
        entries = entries * shard_levels(rng, dims, pieces, -0.22, 0.18)
    return jnp.clip(entries, -reach, reach).astype(kind)


def setup_inputs(seed: int = 0) -> dict:
    streams_of = jax.random.split(jax.random.key(seed), 8)
    return {
        "residual": noise(streams_of[0], (NXG, NYG, NZG), 1.0, 6.0, ((0, 8), (1, 32)), jnp.float32),
        "fdm_vectors": noise(streams_of[1], (3, 8, 8, ELEMS), 8 ** -0.5, 2.0, ((3, 256),), jnp.float32),
        "fdm_values": jnp.clip(jnp.exp(math.log(10.0) - 4.6051702 * jax.random.uniform(streams_of[2], (3, 8, ELEMS), jnp.float32) ** shard_levels(streams_of[2], (3, 8, ELEMS), ((2, 256),), -0.2, 0.2)), 0.1, 10.0),
        "corner_slot": draw_corner_slot(jax.random.fold_in(streams_of[7], 71), 0),
        "x_local": noise(streams_of[4], (DEVICES * NV_PAD, N_LOC), (0.22 * (N_LOC * NVERT) ** -0.25), 0.07848767, ((0, 256),), jnp.float32),
        "x_middle": noise(streams_of[5], (DEVICES * NV_PAD, N_MID), (0.22 * (N_MID * NVERT * N_DEV) ** -0.25), 0.033, ((0, 256),), jnp.float32),
        "x_top": noise(streams_of[6], (DEVICES * NV_PAD, N_TOP), (0.22 * (N_TOP * NVERT * DEVICES) ** -0.25), 0.019621918, ((0, 256),), jnp.float32),
    }


PRECISE = lax.Precision.HIGHEST


def corner_weights():
    spots = (jnp.arange(6, dtype=jnp.float32) + 0.5) / 6.0
    return jnp.stack([1.0 - spots, spots])


def windows(padded, count_x, count_y, count_z):
    def take_every(source, elements):
        return jnp.stack([lax.slice_in_dim(source, offset, offset + 6 * (elements - 1) + 1, stride=6, axis=2) for offset in range(8)])
    return take_every(take_every(take_every(padded, count_z), count_y), count_x)


def spread(stacked, elements):
    trailing = stacked.shape[1:]
    merged = trailing[:2] + (6 * elements,) + trailing[3:]
    zeroes = jnp.zeros_like(stacked[0])
    lower = jnp.stack([stacked[offset] for offset in range(6)], axis=3).reshape(merged)
    upper = jnp.stack([stacked[6], stacked[7], zeroes, zeroes, zeroes, zeroes], axis=3).reshape(merged)
    low_pads = [(0, 0)] * len(trailing)
    low_pads[2] = (0, 2)
    up_pads = [(0, 0)] * len(trailing)
    up_pads[2] = (6, 0)
    upper = lax.slice_in_dim(jnp.pad(upper, up_pads), 0, 6 * elements + 2, axis=2)
    return jnp.pad(lower, low_pads) + upper


def local_solve(window, vectors, values):
    vec_x, vec_y, vec_z = vectors[0], vectors[1], vectors[2]
    section = jnp.einsum('aie,abce->ibce', vec_x, window, precision=PRECISE)
    section = jnp.einsum('bje,ibce->ijce', vec_y, section, precision=PRECISE)
    section = jnp.einsum('cke,ijce->ijke', vec_z, section, precision=PRECISE)
    divisor = values[0][:, None, None, :] + values[1][None, :, None, :] + values[2][None, None, :, :]
    section = section / divisor
    section = jnp.einsum('aie,ijke->ajke', vec_x, section, precision=PRECISE)
    section = jnp.einsum('bje,ajke->abke', vec_y, section, precision=PRECISE)
    section = jnp.einsum('cke,abke->abce', vec_z, section, precision=PRECISE)
    return section


def corner_values(block, weights):
    count_x, count_y, count_z = block.shape[0] // 6, block.shape[1] // 6, block.shape[2] // 6
    cells = block.reshape(count_x, 6, count_y, 6, count_z, 6)
    values = jnp.einsum('xi,yj,zk,aibjck->xyzabc', weights, weights, weights, cells, precision=PRECISE)
    return values.reshape(8, count_x * count_y * count_z)


def prolong(corner, weights, count_x, count_y, count_z):
    cube = corner.reshape(2, 2, 2, count_x, count_y, count_z)
    field = jnp.einsum('xi,yj,zk,xyzabc->aibjck', weights, weights, weights, cube, precision=PRECISE)
    return field.reshape(6 * count_x, 6 * count_y, 6 * count_z)


def reference(residual, fdm_vectors, fdm_values, corner_slot, x_local, x_middle, x_top):
    weights = corner_weights()
    padded = jnp.pad(residual, 1)
    window_shape = (6 * BX + 2, 6 * BY + 2, 6 * BZ + 2)
    accum_start = jnp.zeros_like(padded)
    rows_start = jnp.zeros((DEVICES, NV_PAD), jnp.float32)

    def visit(block_index, carry):
        accum, rows = carry
        block_id = jnp.asarray(block_index).astype(jnp.int32)
        anchor = ((block_id // N_DEV) * (6 * BX), (block_id % N_DEV) * (6 * BY), jnp.int32(0))
        block = lax.dynamic_slice(padded, anchor, window_shape)
        first = block_id * E_DEV
        vectors = lax.dynamic_slice_in_dim(fdm_vectors, first, E_DEV, 3)
        values = lax.dynamic_slice_in_dim(fdm_values, first, E_DEV, 2)
        slot_table = lax.dynamic_slice_in_dim(corner_slot, first, E_DEV, 1)
        stacked = windows(block, BX, BY, BZ).reshape(8, 8, 8, E_DEV)
        solved = local_solve(stacked, vectors, values).reshape(8, 8, 8, BX, BY, BZ)
        contrib = spread(spread(spread(solved, BX), BY), BZ)
        accum = lax.dynamic_update_slice(accum, lax.dynamic_slice(accum, anchor, window_shape) + contrib, anchor)
        corners = corner_values(block[1:-1, 1:-1, 1:-1], weights)
        restricted = jax.ops.segment_sum(corners.reshape(-1), slot_table.reshape(-1), num_segments=NV_PAD)
        rows = lax.dynamic_update_slice(rows, restricted[None, :], (block_id, jnp.int32(0)))
        return accum, rows

    accum, restricted = lax.fori_loop(0, DEVICES, visit, (accum_start, rows_start))
    fine_part = accum[1:-1, 1:-1, 1:-1]
    factor_low = x_local.reshape(DEVICES, NV_PAD, N_LOC)
    factor_mid = x_middle.reshape(DEVICES, NV_PAD, N_MID)
    factor_top = x_top.reshape(DEVICES, NV_PAD, N_TOP)
    y_local = jnp.einsum('dv,dvn->dn', restricted, factor_low, precision=PRECISE)
    y_middle = jnp.einsum('dv,dvn->dn', restricted, factor_mid, precision=PRECISE).reshape(N_GROUP, N_DEV, N_MID).sum(axis=1)
    y_top = jnp.einsum('dv,dvn->n', restricted, factor_top, precision=PRECISE)
    coarse = jnp.einsum('dvn,dn->dv', factor_low, y_local, precision=PRECISE)
    coarse = coarse + jnp.einsum('dvn,dn->dv', factor_mid, jnp.repeat(y_middle, N_DEV, axis=0), precision=PRECISE)
    coarse = coarse + jnp.einsum('dvn,n->dv', factor_top, y_top, precision=PRECISE)
    slot_blocks = corner_slot.reshape(8, DEVICES, E_DEV).transpose(1, 0, 2).reshape(DEVICES, 8 * E_DEV)
    corner_coarse = jnp.take_along_axis(coarse, slot_blocks, axis=1).reshape(DEVICES, 8, E_DEV)
    fields = lax.map(lambda corner: prolong(corner, weights, BX, BY, BZ), corner_coarse)
    coarse_field = fields.reshape(N_GROUP, N_DEV, 6 * BX, 6 * BY, 6 * BZ).transpose(0, 2, 1, 3, 4).reshape(NXG, NYG, NZG)
    return fine_part + coarse_field
```

```python
import functools

import jax
import jax.numpy as jnp
import ml_dtypes
import numpy as np
from jax import lax
from jax.experimental import pallas as pl
from jax.experimental.pallas import tpu as pltpu
from jax.sharding import PartitionSpec as P

F32 = jnp.float32
BF16 = jnp.bfloat16
MESH = pl.DeviceIdType.MESH

BX, BY, BZ = 4, 4, 24
NX, NY, NZ = 6 * BX, 6 * BY, 6 * BZ
ELEMENTS = BX * BY * BZ
ROWS = 32
PLANES = NX + 2
LANES = 640
COARSE = 640
SIDES = ((1, 0), (-1, 0), (0, 1), (0, -1), (1, 1), (1, -1), (-1, 1), (-1, -1))


def row_of(y):
    return {0: 24, 25: 25}.get(y, y - 1)


def tables():
    bf16 = ml_dtypes.bfloat16
    pick_z = np.zeros((8 * BZ, NZ), np.float32)
    for l in range(BZ):
        for c in range(8):
            z = 6 * l + c - 1
            if 0 <= z < NZ:
                pick_z[8 * l + c, z] = 1
    pick_y = np.zeros((128, 128), np.float32)
    for i in range(4):
        for b in range(8):
            for j in range(4):
                pick_y[i * 32 + row_of(6 * j + b), i * 32 + b * 4 + j] = 1
    order = np.zeros((ELEMENTS, ELEMENTS), np.float32)
    for i in range(BX):
        for j in range(BY):
            for l in range(BZ):
                order[(i * BY + j) * BZ + l, l // 8 * 128 + i * 32 + l % 8 * 4 + j] = 1

    def hats(elements):
        weights = np.zeros((6 * elements, elements + 1), np.float32)
        for e in range(elements):
            for m in range(6):
                weights[6 * e + m, e] = 11 - 2 * m
                weights[6 * e + m, e + 1] = 2 * m + 1
        return weights

    hat_x, hat_y, hat_z = hats(BX), hats(BY), hats(BZ)
    hat_xy = np.zeros((NX, ROWS, 32), np.float32)
    hat_xy[:, :NY, :25] = np.einsum("xv,yw->xyvw", hat_x, hat_y).reshape(NX, NY, 25)
    hat_xy = hat_xy.reshape(NX * ROWS, 32)
    hat_zw = np.zeros((NZ, LANES), np.float32)
    is_xy = np.zeros((32, LANES), np.float32)
    pick_e = np.zeros((ELEMENTS, LANES), np.float32)
    is_corner = np.zeros((8, LANES), np.float32)
    for vx in range(5):
        for vy in range(5):
            for vz in range(25):
                w = (vx * 5 + vy) * 25 + vz
                hat_zw[:, w] = hat_z[:, vz]
                is_xy[vx * 5 + vy, w] = 1
                i, j, l = min(vx, 3), min(vy, 3), min(vz, 23)
                pick_e[(i * BY + j) * BZ + l, w] = 1
                is_corner[4 * (vx - i) + 2 * (vy - j) + (vz - l), w] = 1
    return (
        pick_z.astype(bf16),
        pick_z.T.copy().astype(bf16),
        pick_y.astype(bf16),
        order.astype(bf16),
        hat_xy.astype(bf16),
        hat_xy.T.copy().astype(bf16),
        hat_zw.astype(bf16),
        pick_e.astype(bf16),
        is_xy,
        is_corner,
    )


def split(value):
    high = value.astype(BF16)
    return high, (value - high.astype(F32)).astype(BF16)


def mm(a, b):
    return lax.dot_general(a, b, (((1,), (0,)), ((), ())), preferred_element_type=F32)


def mm_t(a, b):
    return lax.dot_general(a, b, (((1,), (1,)), ((), ())), preferred_element_type=F32)


def swap_chunks(pieces, masks):
    pieces = list(pieces)
    for bit in range(3):
        shift = 4 << bit
        mask = masks[bit]
        for low in range(8):
            if low >> bit & 1:
                continue
            high = low | 1 << bit
            x, y = pieces[low], pieces[high]
            pieces[low] = jnp.where(mask, pltpu.roll(y, shift, 1), x)
            pieces[high] = jnp.where(mask, y, pltpu.roll(x, 128 - shift, 1))
    return pieces


def kernel(
    n_group,
    n_dev,
    residual,
    vectors_in,
    values_in,
    slot_in,
    x_local_in,
    x_middle_in,
    x_top_in,
    pick_z_in,
    pick_zt_in,
    pick_y_in,
    order_in,
    hat_xy_in,
    hat_xyt_in,
    hat_zw_in,
    pick_e_in,
    is_xy_in,
    is_corner_in,
    out,
    block,
    vectors_raw,
    values_raw,
    slot,
    x_local,
    x_middle,
    x_top,
    pick_z,
    pick_zt,
    pick_y,
    order,
    hat_xy,
    hat_xyt,
    hat_zw,
    pick_e,
    is_xy,
    is_corner,
    vectors,
    values,
    window,
    stage,
    solved,
    total,
    y_pack,
    c_pack,
    x_halo,
    y_halo,
    c_halo,
    x_rim,
    y_rim,
    c_rim,
    small,
    vertex_row,
    vertex_col,
    y_rows,
    sent,
    got_z,
    got_x,
    got_g,
    load_sem,
    halo_send,
    halo_recv,
    rim_send,
    rim_recv,
    sum_send,
    sum_recv,
    out_sem,
):
    group = lax.axis_index("group")
    dev = lax.axis_index("dev")
    n_low = min(8, n_dev)
    n_high = n_dev // n_low
    high, low = dev // n_low, dev % n_low

    def beside(step_x, step_y):
        return ((group + step_x + n_group) % n_group, (dev + step_y + n_dev) % n_dev)

    def came(step_x, step_y):
        from_x, from_y = group - step_x, dev - step_y
        return (from_x >= 0) & (from_x < n_group) & (from_y >= 0) & (from_y < n_dev)

    peers_z = [(group, high * n_low + (low + k) % n_low) for k in range(1, n_low)]
    peers_x = [(group, (high + k) % n_high * n_low + low) for k in range(1, n_high)]
    peers_g = [((group + k) % n_group, dev) for k in range(1, n_group)]

    pairs = [
        (residual, block.at[pl.ds(1, NX), pl.ds(0, NY), :]),
        (hat_xyt_in, hat_xyt),
        (hat_zw_in, hat_zw),
        (is_xy_in, is_xy),
        (slot_in, slot),
        (pick_e_in, pick_e),
        (is_corner_in, is_corner),
        (x_local_in, x_local),
        (x_middle_in, x_middle),
        (x_top_in, x_top),
        (vectors_in, vectors_raw),
        (values_in, values_raw),
        (order_in, order),
        (pick_z_in, pick_z),
        (pick_y_in, pick_y),
        (pick_zt_in, pick_zt),
        (hat_xy_in, hat_xy),
    ]
    loads = [
        pltpu.make_async_copy(source, target, load_sem.at[number])
        for number, (source, target) in enumerate(pairs)
    ]
    for load in loads:
        load.start()

    barrier = pltpu.get_barrier_semaphore()
    partners = [beside(*side) for side in SIDES] + peers_z + peers_x + peers_g
    for partner in partners:
        pl.semaphore_signal(barrier, inc=1, device_id=partner, device_id_type=MESH)

    rows = block.reshape(PLANES * ROWS, NZ)
    total_rows = total.reshape(PLANES * ROWS, NZ)
    empty = jnp.zeros((8, NZ), F32)
    for plane in range(PLANES):
        rows[plane * ROWS + 24 : plane * ROWS + 32, :] = empty

    def send_sides(source, x_planes, y_rows_at, x_into, y_into, c_into, send, recv):
        copies = []
        for number, (step_x, step_y) in enumerate(SIDES):
            plane = x_planes[step_x]
            row = y_rows_at[step_y]
            if step_y == 0:
                piece = source.at[pl.ds(plane * ROWS, 24), :]
                into = x_into.at[number]
            elif step_x == 0:
                for x in range(NX):
                    at = (x + 1) * ROWS + row
                    y_pack[number - 2, x : x + 1, :] = source[at : at + 1, :]
                piece = y_pack.at[number - 2]
                into = y_into.at[number - 2]
            else:
                c_pack[number - 4] = jnp.broadcast_to(
                    source[plane * ROWS + row : plane * ROWS + row + 1, :], (8, NZ)
                )
                piece = c_pack.at[number - 4]
                into = c_into.at[number - 4]
            copies.append(
                pltpu.make_async_remote_copy(
                    src_ref=piece,
                    dst_ref=into,
                    send_sem=send.at[number],
                    recv_sem=recv.at[number],
                    device_id=beside(step_x, step_y),
                    device_id_type=MESH,
                )
            )
        return copies

    loads[0].wait()
    halo = send_sides(
        rows, {1: 24, -1: 1, 0: 0}, {1: 23, -1: 0, 0: 0}, x_halo, y_halo, c_halo, halo_send, halo_recv
    )
    pl.semaphore_wait(barrier, len(partners))
    for copy in halo:
        copy.start()

    for load in loads[1:10]:
        load.wait()
    own_high, own_low = split(rows[ROWS : ROWS * (NX + 1), :])
    on_xy = mm(hat_xyt[...], own_high) + mm(hat_xyt[...], own_low)
    on_xy_high, on_xy_low = split(on_xy)
    on_vertex = mm(on_xy_high, hat_zw[...]) + mm(on_xy_low, hat_zw[...])
    at_vertex = jnp.sum(on_vertex * is_xy[...], axis=0, keepdims=True) * (1.0 / 1728.0)

    slots = slot[...]
    parts = jnp.concatenate([(slots >> 5).astype(F32), (slots & 31).astype(F32)], axis=0)
    picked = mm(parts.astype(BF16), pick_e[...])
    upper = jnp.sum(picked[0:8] * is_corner[...], axis=0, keepdims=True)
    lower = jnp.sum(picked[8:16] * is_corner[...], axis=0, keepdims=True)
    count = lax.broadcasted_iota(jnp.int32, (32, LANES), 0).astype(F32)
    is_upper = jnp.where(count == upper, 1.0, 0.0)
    is_lower = jnp.where(count == lower, 1.0, 0.0).astype(BF16)
    by_high, by_low = split(is_upper * at_vertex)
    small[...] = mm_t(by_high, is_lower) + mm_t(by_low, is_lower)

    eye = jnp.where(
        lax.broadcasted_iota(jnp.int32, (32, 32), 0) == lax.broadcasted_iota(jnp.int32, (32, 32), 1),
        1.0,
        0.0,
    )
    y_sums = [jnp.zeros((8, 128), F32) for _ in range(3)]
    for part in range(COARSE // 32):
        column = jnp.sum(small[part : part + 1, :] * eye, axis=1, keepdims=True)
        for level, factor in enumerate((x_local, x_middle, x_top)):
            weighted = column * factor[32 * part : 32 * part + 32, :]
            y_sums[level] = y_sums[level] + (
                (weighted[0:8] + weighted[8:16]) + (weighted[16:24] + weighted[24:32])
            )
    y_local, y_middle, y_top = [jnp.sum(value, axis=0, keepdims=True) for value in y_sums]
    row_number = lax.broadcasted_iota(jnp.int32, (8, 128), 0)
    y_rows[...] = jnp.broadcast_to(y_local, (8, 128))
    sent[0] = jnp.where(row_number == 0, y_middle, y_top)

    def send_sums(stage_number, peers, into, first):
        copies = []
        for k, peer in enumerate(peers):
            copies.append(
                pltpu.make_async_remote_copy(
                    src_ref=sent.at[stage_number],
                    dst_ref=into.at[k],
                    send_sem=sum_send.at[first + k],
                    recv_sem=sum_recv.at[first + k],
                    device_id=peer,
                    device_id_type=MESH,
                )
            )
        for copy in copies:
            copy.start()
        return copies

    def take_sums(copies, stage_number, into):
        for copy in copies:
            copy.wait()
        value = sent[stage_number]
        for k in range(len(copies)):
            value = value + into[k]
        return value

    first_sums = send_sums(0, peers_z, got_z, 0)

    for load in loads[10:]:
        load.wait()
    raw = jnp.concatenate([vectors_raw[...], values_raw[...]], axis=0)
    raw_high, raw_rest = split(raw)
    ordered = mm(raw_high, order[...]) + mm(raw_rest, order[...])
    for tile in range(3):
        vectors[tile] = ordered[0:192, 128 * tile : 128 * tile + 128]
        values[tile] = ordered[192:216, 128 * tile : 128 * tile + 128]

    for copy in halo:
        copy.wait()
    for number, (step_x, step_y) in enumerate(SIDES):
        inside = jnp.where(came(step_x, step_y), 1.0, 0.0)
        plane = {1: 0, -1: PLANES - 1}.get(step_x)
        row = {1: 24, -1: 25}.get(step_y)
        if step_y == 0:
            rows[plane * ROWS : plane * ROWS + 24, :] = x_halo[number] * inside
        elif step_x == 0:
            for x in range(NX):
                at = (x + 1) * ROWS + row
                rows[at : at + 1, :] = y_halo[number - 2, x : x + 1, :] * inside
        else:
            rows[plane * ROWS + row : plane * ROWS + row + 1, :] = (
                c_halo[number - 4, 0:1, :] * inside
            )

    lane = lax.broadcasted_iota(jnp.int32, (8, 128), 1)
    masks = [(lane >> (2 + bit)) & 1 == 1 for bit in range(3)]

    def make_windows(a, carry):
        planes = [
            rows[pl.ds(pl.multiple_of((6 * i + a) * ROWS, ROWS), ROWS), :] for i in range(BX)
        ]
        plane_high, plane_low = split(jnp.concatenate(planes, axis=0))
        along_high = mm_t(pick_z[...], plane_high).astype(BF16)
        along_low = mm_t(pick_z[...], plane_low).astype(BF16)
        picked = mm(along_high, pick_y[...]) + mm(along_low, pick_y[...])
        for tile in range(3):
            first = tile * 64
            pieces = swap_chunks(
                [picked[first + 8 * l : first + 8 * l + 8, :] for l in range(8)], masks
            )
            for b in range(8):
                window[tile, a, b] = pieces[b]
        return carry

    lax.fori_loop(0, 8, make_windows, 0)

    def bcast(ref, tile, row):
        return ref[tile, pl.ds(row, 8, stride=0), :]

    def solve(tile, carry):
        for b in (0, 4):
            fields = [window[tile, a, b : b + 4] for a in range(8)]
            for p in range(8):
                value = None
                for a in range(8):
                    term = bcast(vectors, tile, a * 8 + p) * fields[a]
                    value = term if value is None else value + term
                stage[p, b : b + 4] = value

        def middle(p, carry):
            fields = [stage[p, b] for b in range(8)]
            turned = []
            for q in range(8):
                value = None
                for b in range(8):
                    term = bcast(vectors, tile, 64 + b * 8 + q) * fields[b]
                    value = term if value is None else value + term
                turned.append(value)
            along = [vectors[tile, 128 + 8 * c : 136 + 8 * c, :] for c in range(8)]
            scale = bcast(values, tile, p) + values[tile, 16:24, :]
            divided = []
            for q in range(8):
                value = None
                for c in range(8):
                    term = along[c] * turned[q][c : c + 1, :]
                    value = term if value is None else value + term
                divided.append(value / (scale + bcast(values, tile, 8 + q)))
            across = [vectors[tile, pl.ds(128 + s, 8, stride=8), :] for s in range(8)]
            back = []
            for q in range(8):
                value = None
                for s in range(8):
                    term = across[s] * divided[q][s : s + 1, :]
                    value = term if value is None else value + term
                back.append(value)
            for b in range(8):
                value = None
                for q in range(8):
                    term = bcast(vectors, tile, 64 + b * 8 + q) * back[q]
                    value = term if value is None else value + term
                stage[p, b] = value
            return carry

        lax.fori_loop(0, 8, middle, 0)
        for b in (0, 4):
            fields = [stage[p, b : b + 4] for p in range(8)]
            for a in range(8):
                value = None
                for p in range(8):
                    term = bcast(vectors, tile, a * 8 + p) * fields[p]
                    value = term if value is None else value + term
                solved[tile, a, b : b + 4] = value
        return carry

    lax.fori_loop(0, 1, solve, 0)
    sent[1] = take_sums(first_sums, 0, got_z)
    second_sums = send_sums(1, peers_x, got_x, 8)
    lax.fori_loop(1, 2, solve, 0)
    row_sum = take_sums(second_sums, 1, got_x)
    sent[2] = row_sum
    third_sums = send_sums(2, peers_g, got_g, 16)
    lax.fori_loop(2, 3, solve, 0)
    y_all = take_sums(third_sums, 2, got_g)

    y_local = y_rows[0:1, :]
    y_middle = sent[2, 0:1, :]
    y_top = y_all[1:2, :]
    for part in range(COARSE // 32):
        here = slice(32 * part, 32 * part + 32)
        terms = x_local[here, :] * y_local + x_middle[here, :] * y_middle + x_top[here, :] * y_top
        column = jnp.sum(terms, axis=1, keepdims=True)
        vertex_col[part : part + 1, :] = jnp.sum(column * eye, axis=0, keepdims=True)
    vertex_col[20:32, :] = jnp.zeros((12, 32), F32)
    coarse_high, coarse_low = split(vertex_col[...])
    spread_out = mm(coarse_high, is_lower) + mm(coarse_low, is_lower)
    at_vertex = jnp.sum(spread_out * is_upper, axis=0, keepdims=True) * (1.0 / 1728.0)
    vertex_high, vertex_low = split(is_xy[...] * at_vertex)
    on_xy = mm_t(vertex_high, hat_zw[...]) + mm_t(vertex_low, hat_zw[...])
    vertex_row[...] = on_xy

    def add_up(a):
        pieces = []
        for tile in range(3):
            pieces.extend(swap_chunks([solved[tile, a, b] for b in range(8)], masks))
        piece_high, piece_low = split(jnp.concatenate(pieces, axis=0))
        along = mm(pick_zt[...], piece_high) + mm(pick_zt[...], piece_low)
        along_high, along_low = split(along)
        return mm_t(pick_y[...], along_high) + mm_t(pick_y[...], along_low)

    def store_sums(a, carry):
        value = add_up(a)
        for i in range(BX):
            total_rows[pl.ds(pl.multiple_of((6 * i + a) * ROWS, ROWS), ROWS), :] = value[
                32 * i : 32 * i + 32, :
            ]
        return carry

    lax.fori_loop(0, 6, store_sums, 0)
    for a in (6, 7):
        value = add_up(a)
        for i in range(BX):
            here = slice((6 * i + a) * ROWS, (6 * i + a + 1) * ROWS)
            piece = value[32 * i : 32 * i + 32, :]
            total_rows[here, :] = piece if i == BX - 1 else total_rows[here, :] + piece

    rim = send_sides(
        total_rows,
        {1: PLANES - 1, -1: 0, 0: 0},
        {1: 25, -1: 24, 0: 0},
        x_rim,
        y_rim,
        c_rim,
        rim_send,
        rim_recv,
    )
    for copy in rim:
        copy.start()

    field_high, field_low = split(vertex_row[...])
    field = mm(hat_xy[...], field_high) + mm(hat_xy[...], field_low)
    own = slice(ROWS, ROWS * (NX + 1))
    for x in range(NX):
        here = slice((x + 1) * ROWS, (x + 1) * ROWS + 24)
        total_rows[here, :] = total_rows[here, :] + field[x * ROWS : x * ROWS + 24, :]

    for copy in rim:
        copy.wait()
    for number, (step_x, step_y) in enumerate(SIDES):
        inside = jnp.where(came(step_x, step_y), 1.0, 0.0)
        plane = {1: 1, -1: PLANES - 2}.get(step_x)
        row = {1: 0, -1: 23}.get(step_y)
        if step_y == 0:
            here = slice(plane * ROWS, plane * ROWS + 24)
            total_rows[here, :] = total_rows[here, :] + x_rim[number] * inside
        elif step_x == 0:
            for x in range(NX):
                here = slice((x + 1) * ROWS + row, (x + 1) * ROWS + row + 1)
                total_rows[here, :] = total_rows[here, :] + y_rim[number - 2, x : x + 1, :] * inside
        else:
            here = slice(plane * ROWS + row, plane * ROWS + row + 1)
            total_rows[here, :] = total_rows[here, :] + c_rim[number - 4, 0:1, :] * inside

    store = pltpu.make_async_copy(total.at[pl.ds(1, NX), pl.ds(0, NY), :], out, out_sem)
    store.start()
    store.wait()


def local(residual, fdm_vectors, fdm_values, corner_slot, x_local, x_middle, x_top):
    n_group, n_dev = lax.axis_size("group"), lax.axis_size("dev")
    consts = tables()
    arguments = (
        residual,
        fdm_vectors.reshape(192, ELEMENTS),
        fdm_values.reshape(24, ELEMENTS),
        corner_slot,
        x_local,
        x_middle,
        x_top,
    ) + tuple(jnp.asarray(value) for value in consts)
    vmem = [pltpu.VMEM(value.shape, value.dtype) for value in arguments[1:]]
    n_sides = len(SIDES)
    scratch = (
        [pltpu.VMEM((PLANES, ROWS, NZ), F32)]
        + vmem
        + [
            pltpu.VMEM((3, 192, 128), F32),
            pltpu.VMEM((3, 24, 128), F32),
            pltpu.VMEM((3, 8, 8, 8, 128), F32),
            pltpu.VMEM((8, 8, 8, 128), F32),
            pltpu.VMEM((3, 8, 8, 8, 128), F32),
            pltpu.VMEM((PLANES, ROWS, NZ), F32),
            pltpu.VMEM((2, 24, NZ), F32),
            pltpu.VMEM((4, 8, NZ), F32),
            pltpu.VMEM((2, 24, NZ), F32),
            pltpu.VMEM((2, 24, NZ), F32),
            pltpu.VMEM((4, 8, NZ), F32),
            pltpu.VMEM((2, 24, NZ), F32),
            pltpu.VMEM((2, 24, NZ), F32),
            pltpu.VMEM((4, 8, NZ), F32),
            pltpu.VMEM((32, 32), F32),
            pltpu.VMEM((32, NZ), F32),
            pltpu.VMEM((32, 32), F32),
            pltpu.VMEM((8, 128), F32),
            pltpu.VMEM((3, 8, 128), F32),
            pltpu.VMEM((8, 8, 128), F32),
            pltpu.VMEM((8, 8, 128), F32),
            pltpu.VMEM((8, 8, 128), F32),
            pltpu.SemaphoreType.DMA((len(arguments),)),
            pltpu.SemaphoreType.DMA((n_sides,)),
            pltpu.SemaphoreType.DMA((n_sides,)),
            pltpu.SemaphoreType.DMA((n_sides,)),
            pltpu.SemaphoreType.DMA((n_sides,)),
            pltpu.SemaphoreType.DMA((24,)),
            pltpu.SemaphoreType.DMA((24,)),
            pltpu.SemaphoreType.DMA,
        ]
    )
    return pl.pallas_call(
        functools.partial(kernel, n_group, n_dev),
        out_shape=jax.ShapeDtypeStruct((NX, NY, NZ), F32),
        in_specs=[pl.BlockSpec(memory_space=pl.ANY)] * len(arguments),
        out_specs=pl.BlockSpec(memory_space=pl.ANY),
        scratch_shapes=scratch,
        compiler_params=pltpu.CompilerParams(
            collective_id=0, has_side_effects=True, vmem_limit_bytes=48 * 1024 * 1024
        ),
    )(*arguments)


def solution(mesh):
    return jax.shard_map(
        local,
        mesh=mesh,
        in_specs=(
            P("group", "dev", None),
            P(None, None, None, ("group", "dev")),
            P(None, None, ("group", "dev")),
            P(None, ("group", "dev")),
            P(("group", "dev"), None),
            P(("group", "dev"), None),
            P(("group", "dev"), None),
        ),
        out_specs=P("group", "dev", None),
        check_vma=False,
    )
```

```python
import functools

import jax
import jax.numpy as jnp
import ml_dtypes
import numpy as np
from jax import lax
from jax.experimental import pallas as pl
from jax.experimental.pallas import tpu as pltpu
from jax.sharding import PartitionSpec as P

F32 = jnp.float32
BF16 = jnp.bfloat16
MESH = pl.DeviceIdType.MESH

BX, BY, BZ = 4, 4, 24
NX, NY, NZ = 6 * BX, 6 * BY, 6 * BZ
ELEMENTS = BX * BY * BZ
ROWS = 32
PLANES = NX + 2
LANES = 640
COARSE = 640
SIDES = ((1, 0), (-1, 0), (0, 1), (0, -1), (1, 1), (1, -1), (-1, 1), (-1, -1))


def row_of(y):
    return {0: 24, 25: 25}.get(y, y - 1)


def tables():
    bf16 = ml_dtypes.bfloat16
    pick_z = np.zeros((8 * BZ, NZ), np.float32)
    for l in range(BZ):
        for c in range(8):
            z = 6 * l + c - 1
            if 0 <= z < NZ:
                pick_z[8 * l + c, z] = 1
    pick_y = np.zeros((128, 128), np.float32)
    for i in range(4):
        for b in range(8):
            for j in range(4):
                pick_y[i * 32 + row_of(6 * j + b), i * 32 + b * 4 + j] = 1
    order = np.zeros((ELEMENTS, ELEMENTS), np.float32)
    for i in range(BX):
        for j in range(BY):
            for l in range(BZ):
                order[(i * BY + j) * BZ + l, l // 8 * 128 + i * 32 + l % 8 * 4 + j] = 1

    def hats(elements):
        weights = np.zeros((6 * elements, elements + 1), np.float32)
        for e in range(elements):
            for m in range(6):
                weights[6 * e + m, e] = 11 - 2 * m
                weights[6 * e + m, e + 1] = 2 * m + 1
        return weights

    hat_x, hat_y, hat_z = hats(BX), hats(BY), hats(BZ)
    hat_xy = np.zeros((NX, ROWS, 32), np.float32)
    hat_xy[:, :NY, :25] = np.einsum("xv,yw->xyvw", hat_x, hat_y).reshape(NX, NY, 25)
    hat_xy = hat_xy.reshape(NX * ROWS, 32)
    hat_zw = np.zeros((NZ, LANES), np.float32)
    is_xy = np.zeros((32, LANES), np.float32)
    pick_e = np.zeros((ELEMENTS, LANES), np.float32)
    is_corner = np.zeros((8, LANES), np.float32)
    for vx in range(5):
        for vy in range(5):
            for vz in range(25):
                w = (vx * 5 + vy) * 25 + vz
                hat_zw[:, w] = hat_z[:, vz]
                is_xy[vx * 5 + vy, w] = 1
                i, j, l = min(vx, 3), min(vy, 3), min(vz, 23)
                pick_e[(i * BY + j) * BZ + l, w] = 1
                is_corner[4 * (vx - i) + 2 * (vy - j) + (vz - l), w] = 1
    return (
        pick_z.astype(bf16),
        pick_z.T.copy().astype(bf16),
        pick_y.astype(bf16),
        order.astype(bf16),
        hat_xy.astype(bf16),
        hat_xy.T.copy().astype(bf16),
        hat_zw.astype(bf16),
        pick_e.astype(bf16),
        is_xy,
        is_corner,
    )


def split(value):
    high = value.astype(BF16)
    return high, (value - high.astype(F32)).astype(BF16)


def mm(a, b):
    return lax.dot_general(a, b, (((1,), (0,)), ((), ())), preferred_element_type=F32)


def mm_t(a, b):
    return lax.dot_general(a, b, (((1,), (1,)), ((), ())), preferred_element_type=F32)


def swap_chunks(pieces, masks):
    pieces = list(pieces)
    for bit in range(3):
        shift = 4 << bit
        mask = masks[bit]
        for low in range(8):
            if low >> bit & 1:
                continue
            high = low | 1 << bit
            x, y = pieces[low], pieces[high]
            pieces[low] = jnp.where(mask, pltpu.roll(y, shift, 1), x)
            pieces[high] = jnp.where(mask, y, pltpu.roll(x, 128 - shift, 1))
    return pieces


def kernel(
    n_group,
    n_dev,
    residual,
    vectors_in,
    values_in,
    slot_in,
    x_local_in,
    x_middle_in,
    x_top_in,
    pick_z_in,
    pick_zt_in,
    pick_y_in,
    order_in,
    hat_xy_in,
    hat_xyt_in,
    hat_zw_in,
    pick_e_in,
    is_xy_in,
    is_corner_in,
    out,
    block,
    vectors_raw,
    values_raw,
    slot,
    x_local,
    x_middle,
    x_top,
    pick_z,
    pick_zt,
    pick_y,
    order,
    hat_xy,
    hat_xyt,
    hat_zw,
    pick_e,
    is_xy,
    is_corner,
    vectors,
    values,
    window,
    stage,
    solved,
    total,
    y_pack,
    c_pack,
    x_halo,
    y_halo,
    c_halo,
    x_rim,
    y_rim,
    c_rim,
    small,
    vertex_row,
    vertex_col,
    y_rows,
    sent,
    got_z,
    got_x,
    got_g,
    load_sem,
    halo_send,
    halo_recv,
    rim_send,
    rim_recv,
    sum_send,
    sum_recv,
    out_sem,
):
    group = lax.axis_index("group")
    dev = lax.axis_index("dev")
    n_low = min(8, n_dev)
    n_high = n_dev // n_low
    high, low = dev // n_low, dev % n_low

    def beside(step_x, step_y):
        return ((group + step_x + n_group) % n_group, (dev + step_y + n_dev) % n_dev)

    def came(step_x, step_y):
        from_x, from_y = group - step_x, dev - step_y
        return (from_x >= 0) & (from_x < n_group) & (from_y >= 0) & (from_y < n_dev)

    peers_z = [(group, high * n_low + (low + k) % n_low) for k in range(1, n_low)]
    peers_x = [(group, (high + k) % n_high * n_low + low) for k in range(1, n_high)]
    peers_g = [((group + k) % n_group, dev) for k in range(1, n_group)]

    pairs = [
        (residual, block.at[pl.ds(1, NX), pl.ds(0, NY), :]),
        (hat_xyt_in, hat_xyt),
        (hat_zw_in, hat_zw),
        (is_xy_in, is_xy),
        (slot_in, slot),
        (pick_e_in, pick_e),
        (is_corner_in, is_corner),
        (x_local_in, x_local),
        (x_middle_in, x_middle),
        (x_top_in, x_top),
        (vectors_in, vectors_raw),
        (values_in, values_raw),
        (order_in, order),
        (pick_z_in, pick_z),
        (pick_y_in, pick_y),
        (pick_zt_in, pick_zt),
        (hat_xy_in, hat_xy),
    ]
    loads = [
        pltpu.make_async_copy(source, target, load_sem.at[number])
        for number, (source, target) in enumerate(pairs)
    ]
    for load in loads:
        load.start()

    barrier = pltpu.get_barrier_semaphore()
    partners = [beside(*side) for side in SIDES] + peers_z + peers_x + peers_g
    for partner in partners:
        pl.semaphore_signal(barrier, inc=1, device_id=partner, device_id_type=MESH)

    rows = block.reshape(PLANES * ROWS, NZ)
    total_rows = total.reshape(PLANES * ROWS, NZ)
    empty = jnp.zeros((8, NZ), F32)
    for plane in range(PLANES):
        rows[plane * ROWS + 24 : plane * ROWS + 32, :] = empty

    def send_sides(source, x_planes, y_rows_at, x_into, y_into, c_into, send, recv):
        copies = []
        for number, (step_x, step_y) in enumerate(SIDES):
            plane = x_planes[step_x]
            row = y_rows_at[step_y]
            if step_y == 0:
                piece = source.at[pl.ds(plane * ROWS, 24), :]
                into = x_into.at[number]
            elif step_x == 0:
                for x in range(NX):
                    at = (x + 1) * ROWS + row
                    y_pack[number - 2, x : x + 1, :] = source[at : at + 1, :]
                piece = y_pack.at[number - 2]
                into = y_into.at[number - 2]
            else:
                c_pack[number - 4] = jnp.broadcast_to(
                    source[plane * ROWS + row : plane * ROWS + row + 1, :], (8, NZ)
                )
                piece = c_pack.at[number - 4]
                into = c_into.at[number - 4]
            copies.append(
                pltpu.make_async_remote_copy(
                    src_ref=piece,
                    dst_ref=into,
                    send_sem=send.at[number],
                    recv_sem=recv.at[number],
                    device_id=beside(step_x, step_y),
                    device_id_type=MESH,
                )
            )
        return copies

    loads[0].wait()
    halo = send_sides(
        rows, {1: 24, -1: 1, 0: 0}, {1: 23, -1: 0, 0: 0}, x_halo, y_halo, c_halo, halo_send, halo_recv
    )
    pl.semaphore_wait(barrier, len(partners))
    for copy in halo:
        copy.start()

    for load in loads[1:10]:
        load.wait()
    own_high, own_low = split(rows[ROWS : ROWS * (NX + 1), :])
    on_xy = mm(hat_xyt[...], own_high) + mm(hat_xyt[...], own_low)
    on_xy_high, on_xy_low = split(on_xy)
    on_vertex = mm(on_xy_high, hat_zw[...]) + mm(on_xy_low, hat_zw[...])
    at_vertex = jnp.sum(on_vertex * is_xy[...], axis=0, keepdims=True) * (1.0 / 1728.0)

    slots = slot[...]
    parts = jnp.concatenate([(slots >> 5).astype(F32), (slots & 31).astype(F32)], axis=0)
    picked = mm(parts.astype(BF16), pick_e[...])
    upper = jnp.sum(picked[0:8] * is_corner[...], axis=0, keepdims=True)
    lower = jnp.sum(picked[8:16] * is_corner[...], axis=0, keepdims=True)
    count = lax.broadcasted_iota(jnp.int32, (32, LANES), 0).astype(F32)
    is_upper = jnp.where(count == upper, 1.0, 0.0)
    is_lower = jnp.where(count == lower, 1.0, 0.0).astype(BF16)
    by_high, by_low = split(is_upper * at_vertex)
    small[...] = mm_t(by_high, is_lower) + mm_t(by_low, is_lower)

    eye = jnp.where(
        lax.broadcasted_iota(jnp.int32, (32, 32), 0) == lax.broadcasted_iota(jnp.int32, (32, 32), 1),
        1.0,
        0.0,
    )
    y_sums = [jnp.zeros((8, 128), F32) for _ in range(3)]
    for part in range(COARSE // 32):
        column = jnp.sum(small[part : part + 1, :] * eye, axis=1, keepdims=True)
        for level, factor in enumerate((x_local, x_middle, x_top)):
            weighted = column * factor[32 * part : 32 * part + 32, :]
            y_sums[level] = y_sums[level] + (
                (weighted[0:8] + weighted[8:16]) + (weighted[16:24] + weighted[24:32])
            )
    y_local, y_middle, y_top = [jnp.sum(value, axis=0, keepdims=True) for value in y_sums]
    row_number = lax.broadcasted_iota(jnp.int32, (8, 128), 0)
    y_rows[...] = jnp.broadcast_to(y_local, (8, 128))
    sent[0] = jnp.where(row_number == 0, y_middle, y_top)

    def send_sums(stage_number, peers, into, first):
        copies = []
        for k, peer in enumerate(peers):
            copies.append(
                pltpu.make_async_remote_copy(
                    src_ref=sent.at[stage_number],
                    dst_ref=into.at[k],
                    send_sem=sum_send.at[first + k],
                    recv_sem=sum_recv.at[first + k],
                    device_id=peer,
                    device_id_type=MESH,
                )
            )
        for copy in copies:
            copy.start()
        return copies

    def take_sums(copies, stage_number, into):
        for copy in copies:
            copy.wait()
        value = sent[stage_number]
        for k in range(len(copies)):
            value = value + into[k]
        return value

    first_sums = send_sums(0, peers_z, got_z, 0)

    for load in loads[10:]:
        load.wait()
    raw = jnp.concatenate([vectors_raw[...], values_raw[...]], axis=0)
    raw_high, raw_rest = split(raw)
    ordered = mm(raw_high, order[...]) + mm(raw_rest, order[...])
    for tile in range(3):
        vectors[tile] = ordered[0:192, 128 * tile : 128 * tile + 128]
        values[tile] = ordered[192:216, 128 * tile : 128 * tile + 128]

    for copy in halo:
        copy.wait()
    for number, (step_x, step_y) in enumerate(SIDES):
        inside = jnp.where(came(step_x, step_y), 1.0, 0.0)
        plane = {1: 0, -1: PLANES - 1}.get(step_x)
        row = {1: 24, -1: 25}.get(step_y)
        if step_y == 0:
            rows[plane * ROWS : plane * ROWS + 24, :] = x_halo[number] * inside
        elif step_x == 0:
            for x in range(NX):
                at = (x + 1) * ROWS + row
                rows[at : at + 1, :] = y_halo[number - 2, x : x + 1, :] * inside
        else:
            rows[plane * ROWS + row : plane * ROWS + row + 1, :] = (
                c_halo[number - 4, 0:1, :] * inside
            )

    lane = lax.broadcasted_iota(jnp.int32, (8, 128), 1)
    masks = [(lane >> (2 + bit)) & 1 == 1 for bit in range(3)]

    def make_windows(a, carry):
        planes = [
            rows[pl.ds(pl.multiple_of((6 * i + a) * ROWS, ROWS), ROWS), :] for i in range(BX)
        ]
        plane_high, plane_low = split(jnp.concatenate(planes, axis=0))
        along_high = mm_t(pick_z[...], plane_high).astype(BF16)
        along_low = mm_t(pick_z[...], plane_low).astype(BF16)
        picked = mm(along_high, pick_y[...]) + mm(along_low, pick_y[...])
        for tile in range(3):
            first = tile * 64
            pieces = swap_chunks(
                [picked[first + 8 * l : first + 8 * l + 8, :] for l in range(8)], masks
            )
            for b in range(8):
                window[tile, a, b] = pieces[b]
        return carry

    lax.fori_loop(0, 8, make_windows, 0)

    def bcast(ref, tile, row):
        return ref[tile, pl.ds(row, 8, stride=0), :]

    def solve(tile, carry):
        for b in (0, 4):
            fields = [window[tile, a, b : b + 4] for a in range(8)]
            for p in range(8):
                value = None
                for a in range(8):
                    term = bcast(vectors, tile, a * 8 + p) * fields[a]
                    value = term if value is None else value + term
                stage[p, b : b + 4] = value

        def middle(p, carry):
            fields = [stage[p, b] for b in range(8)]
            turned = []
            for q in range(8):
                value = None
                for b in range(8):
                    term = bcast(vectors, tile, 64 + b * 8 + q) * fields[b]
                    value = term if value is None else value + term
                turned.append(value)
            along = [vectors[tile, 128 + 8 * c : 136 + 8 * c, :] for c in range(8)]
            scale = bcast(values, tile, p) + values[tile, 16:24, :]
            divided = []
            for q in range(8):
                value = None
                for c in range(8):
                    term = along[c] * turned[q][c : c + 1, :]
                    value = term if value is None else value + term
                divided.append(value / (scale + bcast(values, tile, 8 + q)))
            across = [vectors[tile, pl.ds(128 + s, 8, stride=8), :] for s in range(8)]
            back = []
            for q in range(8):
                value = None
                for s in range(8):
                    term = across[s] * divided[q][s : s + 1, :]
                    value = term if value is None else value + term
                back.append(value)
            for b in range(8):
                value = None
                for q in range(8):
                    term = bcast(vectors, tile, 64 + b * 8 + q) * back[q]
                    value = term if value is None else value + term
                stage[p, b] = value
            return carry

        lax.fori_loop(0, 8, middle, 0)
        for b in (0, 4):
            fields = [stage[p, b : b + 4] for p in range(8)]
            for a in range(8):
                value = None
                for p in range(8):
                    term = bcast(vectors, tile, a * 8 + p) * fields[p]
                    value = term if value is None else value + term
                solved[tile, a, b : b + 4] = value
        return carry

    lax.fori_loop(0, 1, solve, 0)
    sent[1] = take_sums(first_sums, 0, got_z)
    second_sums = send_sums(1, peers_x, got_x, 8)
    lax.fori_loop(1, 2, solve, 0)
    row_sum = take_sums(second_sums, 1, got_x)
    sent[2] = row_sum
    third_sums = send_sums(2, peers_g, got_g, 16)
    lax.fori_loop(2, 3, solve, 0)
    y_all = take_sums(third_sums, 2, got_g)

    y_local = y_rows[0:1, :]
    y_middle = sent[2, 0:1, :]
    y_top = y_all[1:2, :]
    for part in range(COARSE // 32):
        here = slice(32 * part, 32 * part + 32)
        terms = x_local[here, :] * y_local + x_middle[here, :] * y_middle + x_top[here, :] * y_top
        column = jnp.sum(terms, axis=1, keepdims=True)
        vertex_col[part : part + 1, :] = jnp.sum(column * eye, axis=0, keepdims=True)
    vertex_col[20:32, :] = jnp.zeros((12, 32), F32)
    coarse_high, coarse_low = split(vertex_col[...])
    spread_out = mm(coarse_high, is_lower) + mm(coarse_low, is_lower)
    at_vertex = jnp.sum(spread_out * is_upper, axis=0, keepdims=True) * (1.0 / 1728.0)
    vertex_high, vertex_low = split(is_xy[...] * at_vertex)
    on_xy = mm_t(vertex_high, hat_zw[...]) + mm_t(vertex_low, hat_zw[...])
    vertex_row[...] = on_xy

    def add_up(a):
        pieces = []
        for tile in range(3):
            pieces.extend(swap_chunks([solved[tile, a, b] for b in range(8)], masks))
        piece_high, piece_low = split(jnp.concatenate(pieces, axis=0))
        along = mm(pick_zt[...], piece_high) + mm(pick_zt[...], piece_low)
        along_high, along_low = split(along)
        return mm_t(pick_y[...], along_high) + mm_t(pick_y[...], along_low)

    def store_sums(a, carry):
        value = add_up(a)
        for i in range(BX):
            total_rows[pl.ds(pl.multiple_of((6 * i + a) * ROWS, ROWS), ROWS), :] = value[
                32 * i : 32 * i + 32, :
            ]
        return carry

    lax.fori_loop(0, 6, store_sums, 0)
    for a in (6, 7):
        value = add_up(a)
        for i in range(BX):
            here = slice((6 * i + a) * ROWS, (6 * i + a + 1) * ROWS)
            piece = value[32 * i : 32 * i + 32, :]
            total_rows[here, :] = piece if i == BX - 1 else total_rows[here, :] + piece

    rim = send_sides(
        total_rows,
        {1: PLANES - 1, -1: 0, 0: 0},
        {1: 25, -1: 24, 0: 0},
        x_rim,
        y_rim,
        c_rim,
        rim_send,
        rim_recv,
    )
    for copy in rim:
        copy.start()

    field_high, field_low = split(vertex_row[...])
    field = mm(hat_xy[...], field_high) + mm(hat_xy[...], field_low)
    own = slice(ROWS, ROWS * (NX + 1))
    for x in range(NX):
        here = slice((x + 1) * ROWS, (x + 1) * ROWS + 24)
        total_rows[here, :] = total_rows[here, :] + field[x * ROWS : x * ROWS + 24, :]

    for copy in rim:
        copy.wait()
    for number, (step_x, step_y) in enumerate(SIDES):
        inside = jnp.where(came(step_x, step_y), 1.0, 0.0)
        plane = {1: 1, -1: PLANES - 2}.get(step_x)
        row = {1: 0, -1: 23}.get(step_y)
        if step_y == 0:
            here = slice(plane * ROWS, plane * ROWS + 24)
            total_rows[here, :] = total_rows[here, :] + x_rim[number] * inside
        elif step_x == 0:
            for x in range(NX):
                here = slice((x + 1) * ROWS + row, (x + 1) * ROWS + row + 1)
                total_rows[here, :] = total_rows[here, :] + y_rim[number - 2, x : x + 1, :] * inside
        else:
            here = slice(plane * ROWS + row, plane * ROWS + row + 1)
            total_rows[here, :] = total_rows[here, :] + c_rim[number - 4, 0:1, :] * inside

    store = pltpu.make_async_copy(total.at[pl.ds(1, NX), pl.ds(0, NY), :], out, out_sem)
    store.start()
    store.wait()


def local(residual, fdm_vectors, fdm_values, corner_slot, x_local, x_middle, x_top):
    n_group, n_dev = lax.axis_size("group"), lax.axis_size("dev")
    consts = tables()
    arguments = (
        residual,
        fdm_vectors.reshape(192, ELEMENTS),
        fdm_values.reshape(24, ELEMENTS),
        corner_slot,
        x_local,
        x_middle,
        x_top,
    ) + tuple(jnp.asarray(value) for value in consts)
    vmem = [pltpu.VMEM(value.shape, value.dtype) for value in arguments[1:]]
    n_sides = len(SIDES)
    scratch = (
        [pltpu.VMEM((PLANES, ROWS, NZ), F32)]
        + vmem
        + [
            pltpu.VMEM((3, 192, 128), F32),
            pltpu.VMEM((3, 24, 128), F32),
            pltpu.VMEM((3, 8, 8, 8, 128), F32),
            pltpu.VMEM((8, 8, 8, 128), F32),
            pltpu.VMEM((3, 8, 8, 8, 128), F32),
            pltpu.VMEM((PLANES, ROWS, NZ), F32),
            pltpu.VMEM((2, 24, NZ), F32),
            pltpu.VMEM((4, 8, NZ), F32),
            pltpu.VMEM((2, 24, NZ), F32),
            pltpu.VMEM((2, 24, NZ), F32),
            pltpu.VMEM((4, 8, NZ), F32),
            pltpu.VMEM((2, 24, NZ), F32),
            pltpu.VMEM((2, 24, NZ), F32),
            pltpu.VMEM((4, 8, NZ), F32),
            pltpu.VMEM((32, 32), F32),
            pltpu.VMEM((32, NZ), F32),
            pltpu.VMEM((32, 32), F32),
            pltpu.VMEM((8, 128), F32),
            pltpu.VMEM((3, 8, 128), F32),
            pltpu.VMEM((8, 8, 128), F32),
            pltpu.VMEM((8, 8, 128), F32),
            pltpu.VMEM((8, 8, 128), F32),
            pltpu.SemaphoreType.DMA((len(arguments),)),
            pltpu.SemaphoreType.DMA((n_sides,)),
            pltpu.SemaphoreType.DMA((n_sides,)),
            pltpu.SemaphoreType.DMA((n_sides,)),
            pltpu.SemaphoreType.DMA((n_sides,)),
            pltpu.SemaphoreType.DMA((24,)),
            pltpu.SemaphoreType.DMA((24,)),
            pltpu.SemaphoreType.DMA,
        ]
    )
    return pl.pallas_call(
        functools.partial(kernel, n_group, n_dev),
        out_shape=jax.ShapeDtypeStruct((NX, NY, NZ), F32),
        in_specs=[pl.BlockSpec(memory_space=pl.ANY)] * len(arguments),
        out_specs=pl.BlockSpec(memory_space=pl.ANY),
        scratch_shapes=scratch,
        compiler_params=pltpu.CompilerParams(
            collective_id=0, has_side_effects=True, vmem_limit_bytes=56 * 1024 * 1024
        ),
    )(*arguments)


def solution(mesh):
    return jax.shard_map(
        local,
        mesh=mesh,
        in_specs=(
            P("group", "dev", None),
            P(None, None, None, ("group", "dev")),
            P(None, None, ("group", "dev")),
            P(None, ("group", "dev")),
            P(("group", "dev"), None),
            P(("group", "dev"), None),
            P(("group", "dev"), None),
        ),
        out_specs=P("group", "dev", None),
        check_vma=False,
    )
```

```python
import functools

import jax
import jax.numpy as jnp
import ml_dtypes
import numpy as np
from jax import lax
from jax.experimental import pallas as pl
from jax.experimental.pallas import tpu as pltpu
from jax.sharding import PartitionSpec as P

F32 = jnp.float32
BF16 = jnp.bfloat16
MESH = pl.DeviceIdType.MESH

BX, BY, BZ = 4, 4, 24
NX, NY, NZ = 6 * BX, 6 * BY, 6 * BZ
ELEMENTS = BX * BY * BZ
ROWS = 32
PLANES = NX + 2
LANES = 640
COARSE = 640
SIDES = ((1, 0), (-1, 0), (0, 1), (0, -1), (1, 1), (1, -1), (-1, 1), (-1, -1))


def row_of(y):
    return {0: 24, 25: 25}.get(y, y - 1)


def tables():
    bf16 = ml_dtypes.bfloat16
    pick_z = np.zeros((8 * BZ, NZ), np.float32)
    for l in range(BZ):
        for c in range(8):
            z = 6 * l + c - 1
            if 0 <= z < NZ:
                pick_z[8 * l + c, z] = 1
    pick_y = np.zeros((128, 128), np.float32)
    for i in range(4):
        for b in range(8):
            for j in range(4):
                pick_y[i * 32 + row_of(6 * j + b), i * 32 + b * 4 + j] = 1
    order = np.zeros((ELEMENTS, ELEMENTS), np.float32)
    for i in range(BX):
        for j in range(BY):
            for l in range(BZ):
                order[(i * BY + j) * BZ + l, l // 8 * 128 + i * 32 + l % 8 * 4 + j] = 1

    def hats(elements):
        weights = np.zeros((6 * elements, elements + 1), np.float32)
        for e in range(elements):
            for m in range(6):
                weights[6 * e + m, e] = 11 - 2 * m
                weights[6 * e + m, e + 1] = 2 * m + 1
        return weights

    hat_x, hat_y, hat_z = hats(BX), hats(BY), hats(BZ)
    hat_xy = np.zeros((NX, ROWS, 32), np.float32)
    hat_xy[:, :NY, :25] = np.einsum("xv,yw->xyvw", hat_x, hat_y).reshape(NX, NY, 25)
    hat_xy = hat_xy.reshape(NX * ROWS, 32)
    hat_zw = np.zeros((NZ, LANES), np.float32)
    is_xy = np.zeros((32, LANES), np.float32)
    pick_e = np.zeros((ELEMENTS, LANES), np.float32)
    is_corner = np.zeros((8, LANES), np.float32)
    for vx in range(5):
        for vy in range(5):
            for vz in range(25):
                w = (vx * 5 + vy) * 25 + vz
                hat_zw[:, w] = hat_z[:, vz]
                is_xy[vx * 5 + vy, w] = 1
                i, j, l = min(vx, 3), min(vy, 3), min(vz, 23)
                pick_e[(i * BY + j) * BZ + l, w] = 1
                is_corner[4 * (vx - i) + 2 * (vy - j) + (vz - l), w] = 1
    return (
        pick_z.astype(bf16),
        pick_z.T.copy().astype(bf16),
        pick_y.astype(bf16),
        order.astype(bf16),
        hat_xy.astype(bf16),
        hat_xy.T.copy().astype(bf16),
        hat_zw.astype(bf16),
        pick_e.astype(bf16),
        is_xy,
        is_corner,
    )


def split(value):
    high = value.astype(BF16)
    return high, (value - high.astype(F32)).astype(BF16)


def mm(a, b):
    return lax.dot_general(a, b, (((1,), (0,)), ((), ())), preferred_element_type=F32)


def mm_t(a, b):
    return lax.dot_general(a, b, (((1,), (1,)), ((), ())), preferred_element_type=F32)


def swap_chunks(pieces, masks):
    pieces = list(pieces)
    for bit in range(3):
        shift = 4 << bit
        mask = masks[bit]
        for low in range(8):
            if low >> bit & 1:
                continue
            high = low | 1 << bit
            x, y = pieces[low], pieces[high]
            pieces[low] = jnp.where(mask, pltpu.roll(y, shift, 1), x)
            pieces[high] = jnp.where(mask, y, pltpu.roll(x, 128 - shift, 1))
    return pieces


def kernel(
    n_group,
    n_dev,
    residual,
    vectors_in,
    values_in,
    slot_in,
    x_local_in,
    x_middle_in,
    x_top_in,
    pick_z_in,
    pick_zt_in,
    pick_y_in,
    order_in,
    hat_xy_in,
    hat_xyt_in,
    hat_zw_in,
    pick_e_in,
    is_xy_in,
    is_corner_in,
    out,
    block,
    vectors_raw,
    values_raw,
    slot,
    x_local,
    x_middle,
    x_top,
    pick_z,
    pick_zt,
    pick_y,
    order,
    hat_xy,
    hat_xyt,
    hat_zw,
    pick_e,
    is_xy,
    is_corner,
    vectors,
    values,
    window,
    stage,
    solved,
    total,
    y_pack,
    c_pack,
    x_halo,
    y_halo,
    c_halo,
    x_rim,
    y_rim,
    c_rim,
    small,
    vertex_row,
    vertex_col,
    y_rows,
    sent,
    got_z,
    got_x,
    got_g,
    load_sem,
    halo_send,
    halo_recv,
    rim_send,
    rim_recv,
    sum_send,
    sum_recv,
):
    group = lax.axis_index("group")
    dev = lax.axis_index("dev")
    n_low = min(8, n_dev)
    n_high = n_dev // n_low
    high, low = dev // n_low, dev % n_low

    def beside(step_x, step_y):
        return ((group + step_x + n_group) % n_group, (dev + step_y + n_dev) % n_dev)

    def came(step_x, step_y):
        from_x, from_y = group - step_x, dev - step_y
        return (from_x >= 0) & (from_x < n_group) & (from_y >= 0) & (from_y < n_dev)

    peers_z = [(group, high * n_low + (low + k) % n_low) for k in range(1, n_low)]
    peers_x = [(group, (high + k) % n_high * n_low + low) for k in range(1, n_high)]
    peers_g = [((group + k) % n_group, dev) for k in range(1, n_group)]

    pairs = [
        (residual, block.at[pl.ds(1, NX), pl.ds(0, NY), :]),
        (hat_xyt_in, hat_xyt),
        (hat_zw_in, hat_zw),
        (is_xy_in, is_xy),
        (slot_in, slot),
        (pick_e_in, pick_e),
        (is_corner_in, is_corner),
        (x_local_in, x_local),
        (x_middle_in, x_middle),
        (x_top_in, x_top),
        (vectors_in, vectors_raw),
        (values_in, values_raw),
        (order_in, order),
        (pick_z_in, pick_z),
        (pick_y_in, pick_y),
        (pick_zt_in, pick_zt),
        (hat_xy_in, hat_xy),
    ]
    loads = [
        pltpu.make_async_copy(source, target, load_sem.at[number])
        for number, (source, target) in enumerate(pairs)
    ]
    for load in loads:
        load.start()

    barrier = pltpu.get_barrier_semaphore()
    partners = [beside(*side) for side in SIDES] + peers_z + peers_x + peers_g
    for partner in partners:
        pl.semaphore_signal(barrier, inc=1, device_id=partner, device_id_type=MESH)

    rows = block.reshape(PLANES * ROWS, NZ)
    total_rows = total.reshape(PLANES * ROWS, NZ)
    empty = jnp.zeros((8, NZ), F32)
    for plane in range(PLANES):
        rows[plane * ROWS + 24 : plane * ROWS + 32, :] = empty

    def send_sides(source, x_planes, y_rows_at, x_into, y_into, c_into, send, recv):
        copies = []
        for number, (step_x, step_y) in enumerate(SIDES):
            plane = x_planes[step_x]
            row = y_rows_at[step_y]
            if step_y == 0:
                piece = source.at[pl.ds(plane * ROWS, 24), :]
                into = x_into.at[number]
            elif step_x == 0:
                for x in range(NX):
                    at = (x + 1) * ROWS + row
                    y_pack[number - 2, x : x + 1, :] = source[at : at + 1, :]
                piece = y_pack.at[number - 2]
                into = y_into.at[number - 2]
            else:
                c_pack[number - 4] = jnp.broadcast_to(
                    source[plane * ROWS + row : plane * ROWS + row + 1, :], (8, NZ)
                )
                piece = c_pack.at[number - 4]
                into = c_into.at[number - 4]
            copies.append(
                pltpu.make_async_remote_copy(
                    src_ref=piece,
                    dst_ref=into,
                    send_sem=send.at[number],
                    recv_sem=recv.at[number],
                    device_id=beside(step_x, step_y),
                    device_id_type=MESH,
                )
            )
        return copies

    loads[0].wait()
    halo = send_sides(
        rows, {1: 24, -1: 1, 0: 0}, {1: 23, -1: 0, 0: 0}, x_halo, y_halo, c_halo, halo_send, halo_recv
    )
    pl.semaphore_wait(barrier, len(partners))
    for copy in halo:
        copy.start()

    for load in loads[1:10]:
        load.wait()
    own_high, own_low = split(rows[ROWS : ROWS * (NX + 1), :])
    on_xy = mm(hat_xyt[...], own_high) + mm(hat_xyt[...], own_low)
    on_xy_high, on_xy_low = split(on_xy)
    on_vertex = mm(on_xy_high, hat_zw[...]) + mm(on_xy_low, hat_zw[...])
    at_vertex = jnp.sum(on_vertex * is_xy[...], axis=0, keepdims=True) * (1.0 / 1728.0)

    slots = slot[...]
    parts = jnp.concatenate([(slots >> 5).astype(F32), (slots & 31).astype(F32)], axis=0)
    picked = mm(parts.astype(BF16), pick_e[...])
    upper = jnp.sum(picked[0:8] * is_corner[...], axis=0, keepdims=True)
    lower = jnp.sum(picked[8:16] * is_corner[...], axis=0, keepdims=True)
    count = lax.broadcasted_iota(jnp.int32, (32, LANES), 0).astype(F32)
    is_upper = jnp.where(count == upper, 1.0, 0.0)
    is_lower = jnp.where(count == lower, 1.0, 0.0).astype(BF16)
    by_high, by_low = split(is_upper * at_vertex)
    small[...] = mm_t(by_high, is_lower) + mm_t(by_low, is_lower)

    eye = jnp.where(
        lax.broadcasted_iota(jnp.int32, (32, 32), 0) == lax.broadcasted_iota(jnp.int32, (32, 32), 1),
        1.0,
        0.0,
    )
    y_sums = [jnp.zeros((8, 128), F32) for _ in range(3)]
    for part in range(COARSE // 32):
        column = jnp.sum(small[part : part + 1, :] * eye, axis=1, keepdims=True)
        for level, factor in enumerate((x_local, x_middle, x_top)):
            weighted = column * factor[32 * part : 32 * part + 32, :]
            y_sums[level] = y_sums[level] + (
                (weighted[0:8] + weighted[8:16]) + (weighted[16:24] + weighted[24:32])
            )
    y_local, y_middle, y_top = [jnp.sum(value, axis=0, keepdims=True) for value in y_sums]
    row_number = lax.broadcasted_iota(jnp.int32, (8, 128), 0)
    y_rows[...] = jnp.broadcast_to(y_local, (8, 128))
    sent[0] = jnp.where(row_number == 0, y_middle, y_top)

    def send_sums(stage_number, peers, into, first):
        copies = []
        for k, peer in enumerate(peers):
            copies.append(
                pltpu.make_async_remote_copy(
                    src_ref=sent.at[stage_number],
                    dst_ref=into.at[k],
                    send_sem=sum_send.at[first + k],
                    recv_sem=sum_recv.at[first + k],
                    device_id=peer,
                    device_id_type=MESH,
                )
            )
        for copy in copies:
            copy.start()
        return copies

    def take_sums(copies, stage_number, into):
        for copy in copies:
            copy.wait()
        value = sent[stage_number]
        for k in range(len(copies)):
            value = value + into[k]
        return value

    first_sums = send_sums(0, peers_z, got_z, 0)

    for load in loads[10:]:
        load.wait()
    raw = jnp.concatenate([vectors_raw[...], values_raw[...]], axis=0)
    raw_high, raw_rest = split(raw)
    ordered = mm(raw_high, order[...]) + mm(raw_rest, order[...])
    for tile in range(3):
        vectors[tile] = ordered[0:192, 128 * tile : 128 * tile + 128]
        values[tile] = ordered[192:216, 128 * tile : 128 * tile + 128]

    for copy in halo:
        copy.wait()
    for number, (step_x, step_y) in enumerate(SIDES):
        inside = jnp.where(came(step_x, step_y), 1.0, 0.0)
        plane = {1: 0, -1: PLANES - 1}.get(step_x)
        row = {1: 24, -1: 25}.get(step_y)
        if step_y == 0:
            rows[plane * ROWS : plane * ROWS + 24, :] = x_halo[number] * inside
        elif step_x == 0:
            for x in range(NX):
                at = (x + 1) * ROWS + row
                rows[at : at + 1, :] = y_halo[number - 2, x : x + 1, :] * inside
        else:
            rows[plane * ROWS + row : plane * ROWS + row + 1, :] = (
                c_halo[number - 4, 0:1, :] * inside
            )

    lane = lax.broadcasted_iota(jnp.int32, (8, 128), 1)
    masks = [(lane >> (2 + bit)) & 1 == 1 for bit in range(3)]

    def make_windows(a, carry):
        planes = [
            rows[pl.ds(pl.multiple_of((6 * i + a) * ROWS, ROWS), ROWS), :] for i in range(BX)
        ]
        plane_high, plane_low = split(jnp.concatenate(planes, axis=0))
        along_high = mm_t(pick_z[...], plane_high).astype(BF16)
        along_low = mm_t(pick_z[...], plane_low).astype(BF16)
        picked = mm(along_high, pick_y[...]) + mm(along_low, pick_y[...])
        for tile in range(3):
            first = tile * 64
            pieces = swap_chunks(
                [picked[first + 8 * l : first + 8 * l + 8, :] for l in range(8)], masks
            )
            for b in range(8):
                window[tile, a, b] = pieces[b]
        return carry

    lax.fori_loop(0, 8, make_windows, 0, unroll=8)

    def bcast(ref, tile, row):
        return ref[tile, pl.ds(row, 8, stride=0), :]

    def solve(tile, carry):
        for b in (0, 4):
            fields = [window[tile, a, b : b + 4] for a in range(8)]
            for p in range(8):
                value = None
                for a in range(8):
                    term = bcast(vectors, tile, a * 8 + p) * fields[a]
                    value = term if value is None else value + term
                stage[p, b : b + 4] = value

        def middle(p, carry):
            fields = [stage[p, b] for b in range(8)]
            turned = []
            for q in range(8):
                value = None
                for b in range(8):
                    term = bcast(vectors, tile, 64 + b * 8 + q) * fields[b]
                    value = term if value is None else value + term
                turned.append(value)
            along = [vectors[tile, 128 + 8 * c : 136 + 8 * c, :] for c in range(8)]
            scale = bcast(values, tile, p) + values[tile, 16:24, :]
            divided = []
            for q in range(8):
                value = None
                for c in range(8):
                    term = along[c] * turned[q][c : c + 1, :]
                    value = term if value is None else value + term
                divided.append(value / (scale + bcast(values, tile, 8 + q)))
            across = [vectors[tile, pl.ds(128 + s, 8, stride=8), :] for s in range(8)]
            back = []
            for q in range(8):
                value = None
                for s in range(8):
                    term = across[s] * divided[q][s : s + 1, :]
                    value = term if value is None else value + term
                back.append(value)
            for b in range(8):
                value = None
                for q in range(8):
                    term = bcast(vectors, tile, 64 + b * 8 + q) * back[q]
                    value = term if value is None else value + term
                stage[p, b] = value
            return carry

        lax.fori_loop(0, 8, middle, 0)
        for b in (0, 4):
            fields = [stage[p, b : b + 4] for p in range(8)]
            for a in range(8):
                value = None
                for p in range(8):
                    term = bcast(vectors, tile, a * 8 + p) * fields[p]
                    value = term if value is None else value + term
                solved[tile, a, b : b + 4] = value
        return carry

    lax.fori_loop(0, 1, solve, 0)
    sent[1] = take_sums(first_sums, 0, got_z)
    second_sums = send_sums(1, peers_x, got_x, 8)
    lax.fori_loop(1, 2, solve, 0)
    row_sum = take_sums(second_sums, 1, got_x)
    sent[2] = row_sum
    third_sums = send_sums(2, peers_g, got_g, 16)
    lax.fori_loop(2, 3, solve, 0)
    y_all = take_sums(third_sums, 2, got_g)

    y_local = y_rows[0:1, :]
    y_middle = sent[2, 0:1, :]
    y_top = y_all[1:2, :]
    for part in range(COARSE // 32):
        here = slice(32 * part, 32 * part + 32)
        terms = x_local[here, :] * y_local + x_middle[here, :] * y_middle + x_top[here, :] * y_top
        column = jnp.sum(terms, axis=1, keepdims=True)
        vertex_col[part : part + 1, :] = jnp.sum(column * eye, axis=0, keepdims=True)
    vertex_col[20:32, :] = jnp.zeros((12, 32), F32)
    coarse_high, coarse_low = split(vertex_col[...])
    spread_out = mm(coarse_high, is_lower) + mm(coarse_low, is_lower)
    at_vertex = jnp.sum(spread_out * is_upper, axis=0, keepdims=True) * (1.0 / 1728.0)
    vertex_high, vertex_low = split(is_xy[...] * at_vertex)
    on_xy = mm_t(vertex_high, hat_zw[...]) + mm_t(vertex_low, hat_zw[...])
    vertex_row[...] = on_xy

    def add_up(a):
        pieces = []
        for tile in range(3):
            pieces.extend(swap_chunks([solved[tile, a, b] for b in range(8)], masks))
        piece_high, piece_low = split(jnp.concatenate(pieces, axis=0))
        along = mm(pick_zt[...], piece_high) + mm(pick_zt[...], piece_low)
        along_high, along_low = split(along)
        return mm_t(pick_y[...], along_high) + mm_t(pick_y[...], along_low)

    def store_sums(a, carry):
        value = add_up(a)
        for i in range(BX):
            total_rows[pl.ds(pl.multiple_of((6 * i + a) * ROWS, ROWS), ROWS), :] = value[
                32 * i : 32 * i + 32, :
            ]
        return carry

    lax.fori_loop(0, 6, store_sums, 0, unroll=6)
    for a in (6, 7):
        value = add_up(a)
        for i in range(BX):
            here = slice((6 * i + a) * ROWS, (6 * i + a + 1) * ROWS)
            piece = value[32 * i : 32 * i + 32, :]
            total_rows[here, :] = piece if i == BX - 1 else total_rows[here, :] + piece

    rim = send_sides(
        total_rows,
        {1: PLANES - 1, -1: 0, 0: 0},
        {1: 25, -1: 24, 0: 0},
        x_rim,
        y_rim,
        c_rim,
        rim_send,
        rim_recv,
    )
    for copy in rim:
        copy.start()

    field_high, field_low = split(vertex_row[...])
    field = mm(hat_xy[...], field_high) + mm(hat_xy[...], field_low)
    for x in range(NX):
        at = (x + 1) * ROWS
        out[x] = total_rows[at : at + NY, :] + field[x * ROWS : x * ROWS + NY, :]

    for copy in rim:
        copy.wait()
    for number, (step_x, step_y) in enumerate(SIDES):
        inside = jnp.where(came(step_x, step_y), 1.0, 0.0)
        x = {1: 0, -1: NX - 1}.get(step_x)
        y = {1: 0, -1: NY - 1}.get(step_y)
        if step_y == 0:
            out[x] = out[x] + x_rim[number] * inside
        elif step_x == 0:
            for x in range(NX):
                out[x, y : y + 1, :] = (
                    out[x, y : y + 1, :] + y_rim[number - 2, x : x + 1, :] * inside
                )
        else:
            out[x, y : y + 1, :] = out[x, y : y + 1, :] + c_rim[number - 4, 0:1, :] * inside


def local(residual, fdm_vectors, fdm_values, corner_slot, x_local, x_middle, x_top):
    n_group, n_dev = lax.axis_size("group"), lax.axis_size("dev")
    consts = tables()
    arguments = (
        residual,
        fdm_vectors.reshape(192, ELEMENTS),
        fdm_values.reshape(24, ELEMENTS),
        corner_slot,
        x_local,
        x_middle,
        x_top,
    ) + tuple(jnp.asarray(value) for value in consts)
    vmem = [pltpu.VMEM(value.shape, value.dtype) for value in arguments[1:]]
    n_sides = len(SIDES)
    scratch = (
        [pltpu.VMEM((PLANES, ROWS, NZ), F32)]
        + vmem
        + [
            pltpu.VMEM((3, 192, 128), F32),
            pltpu.VMEM((3, 24, 128), F32),
            pltpu.VMEM((3, 8, 8, 8, 128), F32),
            pltpu.VMEM((8, 8, 8, 128), F32),
            pltpu.VMEM((3, 8, 8, 8, 128), F32),
            pltpu.VMEM((PLANES, ROWS, NZ), F32),
            pltpu.VMEM((2, 24, NZ), F32),
            pltpu.VMEM((4, 8, NZ), F32),
            pltpu.VMEM((2, 24, NZ), F32),
            pltpu.VMEM((2, 24, NZ), F32),
            pltpu.VMEM((4, 8, NZ), F32),
            pltpu.VMEM((2, 24, NZ), F32),
            pltpu.VMEM((2, 24, NZ), F32),
            pltpu.VMEM((4, 8, NZ), F32),
            pltpu.VMEM((32, 32), F32),
            pltpu.VMEM((32, NZ), F32),
            pltpu.VMEM((32, 32), F32),
            pltpu.VMEM((8, 128), F32),
            pltpu.VMEM((3, 8, 128), F32),
            pltpu.VMEM((8, 8, 128), F32),
            pltpu.VMEM((8, 8, 128), F32),
            pltpu.VMEM((8, 8, 128), F32),
            pltpu.SemaphoreType.DMA((len(arguments),)),
            pltpu.SemaphoreType.DMA((n_sides,)),
            pltpu.SemaphoreType.DMA((n_sides,)),
            pltpu.SemaphoreType.DMA((n_sides,)),
            pltpu.SemaphoreType.DMA((n_sides,)),
            pltpu.SemaphoreType.DMA((24,)),
            pltpu.SemaphoreType.DMA((24,)),
        ]
    )
    return pl.pallas_call(
        functools.partial(kernel, n_group, n_dev),
        out_shape=pltpu.VMEM((NX, NY, NZ), F32),
        in_specs=[pl.BlockSpec(memory_space=pl.ANY)] * len(arguments),
        out_specs=pl.BlockSpec(memory_space=pltpu.VMEM),
        scratch_shapes=scratch,
        compiler_params=pltpu.CompilerParams(
            collective_id=0, has_side_effects=True, vmem_limit_bytes=40 * 1024 * 1024
        ),
    )(*[pltpu.with_memory_space_constraint(value, pltpu.HBM) for value in arguments])


def solution(mesh):
    return jax.shard_map(
        local,
        mesh=mesh,
        in_specs=(
            P("group", "dev", None),
            P(None, None, None, ("group", "dev")),
            P(None, None, ("group", "dev")),
            P(None, ("group", "dev")),
            P(("group", "dev"), None),
            P(("group", "dev"), None),
            P(("group", "dev"), None),
        ),
        out_specs=P("group", "dev", None),
        check_vma=False,
    )
```

```python
import functools

import jax
import jax.numpy as jnp
import ml_dtypes
import numpy as np
from jax import lax
from jax.experimental import pallas as pl
from jax.experimental.pallas import tpu as pltpu
from jax.sharding import PartitionSpec as P

F32 = jnp.float32
BF16 = jnp.bfloat16
MESH = pl.DeviceIdType.MESH

BX, BY, BZ = 4, 4, 24
NX, NY, NZ = 6 * BX, 6 * BY, 6 * BZ
ELEMENTS = BX * BY * BZ
ROWS = 32
PLANES = NX + 2
LANES = 640
COARSE = 640
SIDES = ((1, 0), (-1, 0), (0, 1), (0, -1), (1, 1), (1, -1), (-1, 1), (-1, -1))


def row_of(y):
    return {0: 24, 25: 25}.get(y, y - 1)


def tables():
    bf16 = ml_dtypes.bfloat16
    pick_z = np.zeros((8 * BZ, NZ), np.float32)
    for l in range(BZ):
        for c in range(8):
            z = 6 * l + c - 1
            if 0 <= z < NZ:
                pick_z[8 * l + c, z] = 1
    pick_y = np.zeros((128, 128), np.float32)
    for i in range(4):
        for b in range(8):
            for j in range(4):
                pick_y[i * 32 + row_of(6 * j + b), i * 32 + b * 4 + j] = 1
    order = np.zeros((ELEMENTS, ELEMENTS), np.float32)
    for i in range(BX):
        for j in range(BY):
            for l in range(BZ):
                order[(i * BY + j) * BZ + l, l // 8 * 128 + i * 32 + l % 8 * 4 + j] = 1

    def hats(elements):
        weights = np.zeros((6 * elements, elements + 1), np.float32)
        for e in range(elements):
            for m in range(6):
                weights[6 * e + m, e] = 11 - 2 * m
                weights[6 * e + m, e + 1] = 2 * m + 1
        return weights

    hat_x, hat_y, hat_z = hats(BX), hats(BY), hats(BZ)
    hat_xy = np.zeros((NX, ROWS, 32), np.float32)
    hat_xy[:, :NY, :25] = np.einsum("xv,yw->xyvw", hat_x, hat_y).reshape(NX, NY, 25)
    hat_xy = hat_xy.reshape(NX * ROWS, 32)
    hat_zw = np.zeros((NZ, LANES), np.float32)
    is_xy = np.zeros((32, LANES), np.float32)
    pick_e = np.zeros((ELEMENTS, LANES), np.float32)
    is_corner = np.zeros((8, LANES), np.float32)
    for vx in range(5):
        for vy in range(5):
            for vz in range(25):
                w = (vx * 5 + vy) * 25 + vz
                hat_zw[:, w] = hat_z[:, vz]
                is_xy[vx * 5 + vy, w] = 1
                i, j, l = min(vx, 3), min(vy, 3), min(vz, 23)
                pick_e[(i * BY + j) * BZ + l, w] = 1
                is_corner[4 * (vx - i) + 2 * (vy - j) + (vz - l), w] = 1
    return (
        pick_z.astype(bf16),
        pick_z.T.copy().astype(bf16),
        np.concatenate([pick_y, pick_y], axis=0).astype(bf16),
        np.concatenate([pick_y, pick_y], axis=1).astype(bf16),
        order.astype(bf16),
        hat_xy.astype(bf16),
        hat_xy.T.copy().astype(bf16),
        hat_zw.astype(bf16),
        pick_e.astype(bf16),
        is_xy,
        is_corner,
    )


def split(value):
    high = value.astype(BF16)
    return high, (value - high.astype(F32)).astype(BF16)


def mm(a, b):
    return lax.dot_general(a, b, (((1,), (0,)), ((), ())), preferred_element_type=F32)


def mm_t(a, b):
    return lax.dot_general(a, b, (((1,), (1,)), ((), ())), preferred_element_type=F32)


def swap_chunks(pieces, masks):
    pieces = list(pieces)
    for bit in range(3):
        shift = 4 << bit
        mask = masks[bit]
        for low in range(8):
            if low >> bit & 1:
                continue
            high = low | 1 << bit
            x, y = pieces[low], pieces[high]
            pieces[low] = jnp.where(mask, pltpu.roll(y, shift, 1), x)
            pieces[high] = jnp.where(mask, y, pltpu.roll(x, 128 - shift, 1))
    return pieces


def kernel(
    n_group,
    n_dev,
    residual,
    vectors_in,
    values_in,
    slot_in,
    x_local_in,
    x_middle_in,
    x_top_in,
    pick_z_in,
    pick_zt_in,
    pick_y_in,
    pick_yt_in,
    order_in,
    hat_xy_in,
    hat_xyt_in,
    hat_zw_in,
    pick_e_in,
    is_xy_in,
    is_corner_in,
    out,
    block,
    vectors_raw,
    values_raw,
    slot,
    x_local,
    x_middle,
    x_top,
    pick_z,
    pick_zt,
    pick_y,
    pick_yt,
    order,
    hat_xy,
    hat_xyt,
    hat_zw,
    pick_e,
    is_xy,
    is_corner,
    vectors,
    values,
    window,
    stage,
    solved,
    total,
    y_pack,
    c_pack,
    x_halo,
    y_halo,
    c_halo,
    x_rim,
    y_rim,
    c_rim,
    small,
    vertex_col,
    y_rows,
    sent,
    got_z,
    got_x,
    got_g,
    load_sem,
    halo_send,
    halo_recv,
    rim_send,
    rim_recv,
    sum_send,
    sum_recv,
):
    group = lax.axis_index("group")
    dev = lax.axis_index("dev")
    n_low = min(8, n_dev)
    n_high = n_dev // n_low
    high, low = dev // n_low, dev % n_low

    def beside(step_x, step_y):
        return ((group + step_x + n_group) % n_group, (dev + step_y + n_dev) % n_dev)

    def came(step_x, step_y):
        from_x, from_y = group - step_x, dev - step_y
        return (from_x >= 0) & (from_x < n_group) & (from_y >= 0) & (from_y < n_dev)

    peers_z = [(group, high * n_low + (low + k) % n_low) for k in range(1, n_low)]
    peers_x = [(group, (high + k) % n_high * n_low + low) for k in range(1, n_high)]
    peers_g = [((group + k) % n_group, dev) for k in range(1, n_group)]

    pairs = [
        (residual, block.at[pl.ds(1, NX), pl.ds(0, NY), :]),
        (hat_xyt_in, hat_xyt),
        (hat_zw_in, hat_zw),
        (is_xy_in, is_xy),
        (slot_in, slot),
        (pick_e_in, pick_e),
        (is_corner_in, is_corner),
        (x_local_in, x_local),
        (x_middle_in, x_middle),
        (x_top_in, x_top),
        (vectors_in, vectors_raw),
        (values_in, values_raw),
        (order_in, order),
        (pick_z_in, pick_z),
        (pick_y_in, pick_y),
        (pick_yt_in, pick_yt),
        (pick_zt_in, pick_zt),
        (hat_xy_in, hat_xy),
    ]
    loads = [
        pltpu.make_async_copy(source, target, load_sem.at[number])
        for number, (source, target) in enumerate(pairs)
    ]
    for load in loads:
        load.start()

    barrier = pltpu.get_barrier_semaphore()
    partners = [beside(*side) for side in SIDES] + peers_z + peers_x + peers_g
    for partner in partners:
        pl.semaphore_signal(barrier, inc=1, device_id=partner, device_id_type=MESH)

    rows = block.reshape(PLANES * ROWS, NZ)
    total_rows = total.reshape(PLANES * ROWS, NZ)
    empty = jnp.zeros((8, NZ), F32)
    for plane in range(PLANES):
        rows[plane * ROWS + 24 : plane * ROWS + 32, :] = empty

    def send_sides(source, x_planes, y_rows_at, x_into, y_into, c_into, send, recv):
        copies = []
        for number, (step_x, step_y) in enumerate(SIDES):
            plane = x_planes[step_x]
            row = y_rows_at[step_y]
            if step_y == 0:
                piece = source.at[pl.ds(plane * ROWS, 24), :]
                into = x_into.at[number]
            elif step_x == 0:
                for x in range(NX):
                    at = (x + 1) * ROWS + row
                    y_pack[number - 2, x : x + 1, :] = source[at : at + 1, :]
                piece = y_pack.at[number - 2]
                into = y_into.at[number - 2]
            else:
                c_pack[number - 4] = jnp.broadcast_to(
                    source[plane * ROWS + row : plane * ROWS + row + 1, :], (8, NZ)
                )
                piece = c_pack.at[number - 4]
                into = c_into.at[number - 4]
            copies.append(
                pltpu.make_async_remote_copy(
                    src_ref=piece,
                    dst_ref=into,
                    send_sem=send.at[number],
                    recv_sem=recv.at[number],
                    device_id=beside(step_x, step_y),
                    device_id_type=MESH,
                )
            )
        return copies

    loads[0].wait()
    halo = send_sides(
        rows, {1: 24, -1: 1, 0: 0}, {1: 23, -1: 0, 0: 0}, x_halo, y_halo, c_halo, halo_send, halo_recv
    )
    pl.semaphore_wait(barrier, len(partners))
    for copy in halo:
        copy.start()

    for load in loads[1:10]:
        load.wait()
    own_high, own_low = split(rows[ROWS : ROWS * (NX + 1), :])
    on_xy = mm(hat_xyt[...], own_high) + mm(hat_xyt[...], own_low)
    on_xy_high, on_xy_low = split(on_xy)
    on_vertex = mm(on_xy_high, hat_zw[...]) + mm(on_xy_low, hat_zw[...])
    at_vertex = jnp.sum(on_vertex * is_xy[...], axis=0, keepdims=True) * (1.0 / 1728.0)

    slots = slot[...]
    parts = jnp.concatenate([(slots >> 5).astype(F32), (slots & 31).astype(F32)], axis=0)
    picked = mm(parts.astype(BF16), pick_e[...])
    upper = jnp.sum(picked[0:8] * is_corner[...], axis=0, keepdims=True)
    lower = jnp.sum(picked[8:16] * is_corner[...], axis=0, keepdims=True)
    count = lax.broadcasted_iota(jnp.int32, (32, LANES), 0).astype(F32)
    is_upper = jnp.where(count == upper, 1.0, 0.0)
    is_lower = jnp.where(count == lower, 1.0, 0.0).astype(BF16)
    by_high, by_low = split(is_upper * at_vertex)
    small[...] = mm_t(by_high, is_lower) + mm_t(by_low, is_lower)

    eye = jnp.where(
        lax.broadcasted_iota(jnp.int32, (32, 32), 0) == lax.broadcasted_iota(jnp.int32, (32, 32), 1),
        1.0,
        0.0,
    )
    y_sums = [jnp.zeros((8, 128), F32) for _ in range(3)]
    for part in range(COARSE // 32):
        column = jnp.sum(small[part : part + 1, :] * eye, axis=1, keepdims=True)
        for level, factor in enumerate((x_local, x_middle, x_top)):
            weighted = column * factor[32 * part : 32 * part + 32, :]
            y_sums[level] = y_sums[level] + (
                (weighted[0:8] + weighted[8:16]) + (weighted[16:24] + weighted[24:32])
            )
    y_local, y_middle, y_top = [jnp.sum(value, axis=0, keepdims=True) for value in y_sums]
    row_number = lax.broadcasted_iota(jnp.int32, (8, 128), 0)
    y_rows[...] = jnp.broadcast_to(y_local, (8, 128))
    sent[0] = jnp.where(row_number == 0, y_middle, y_top)

    def send_sums(stage_number, peers, into, first):
        copies = []
        for k, peer in enumerate(peers):
            copies.append(
                pltpu.make_async_remote_copy(
                    src_ref=sent.at[stage_number],
                    dst_ref=into.at[k],
                    send_sem=sum_send.at[first + k],
                    recv_sem=sum_recv.at[first + k],
                    device_id=peer,
                    device_id_type=MESH,
                )
            )
        for copy in copies:
            copy.start()
        return copies

    def take_sums(copies, stage_number, into):
        for copy in copies:
            copy.wait()
        value = sent[stage_number]
        for k in range(len(copies)):
            value = value + into[k]
        return value

    first_sums = send_sums(0, peers_z, got_z, 0)

    for load in loads[10:]:
        load.wait()
    raw = jnp.concatenate([vectors_raw[...], values_raw[...]], axis=0)
    raw_high, raw_rest = split(raw)
    ordered = mm(raw_high, order[...]) + mm(raw_rest, order[...])
    for tile in range(3):
        vectors[tile] = ordered[0:192, 128 * tile : 128 * tile + 128]
        values[tile] = ordered[192:216, 128 * tile : 128 * tile + 128]

    for copy in halo:
        copy.wait()
    for number, (step_x, step_y) in enumerate(SIDES):
        inside = jnp.where(came(step_x, step_y), 1.0, 0.0)
        plane = {1: 0, -1: PLANES - 1}.get(step_x)
        row = {1: 24, -1: 25}.get(step_y)
        if step_y == 0:
            rows[plane * ROWS : plane * ROWS + 24, :] = x_halo[number] * inside
        elif step_x == 0:
            for x in range(NX):
                at = (x + 1) * ROWS + row
                rows[at : at + 1, :] = y_halo[number - 2, x : x + 1, :] * inside
        else:
            rows[plane * ROWS + row : plane * ROWS + row + 1, :] = (
                c_halo[number - 4, 0:1, :] * inside
            )

    lane = lax.broadcasted_iota(jnp.int32, (8, 128), 1)
    masks = [(lane >> (2 + bit)) & 1 == 1 for bit in range(3)]

    def make_windows(a, carry):
        planes = [
            rows[pl.ds(pl.multiple_of((6 * i + a) * ROWS, ROWS), ROWS), :] for i in range(BX)
        ]
        both = jnp.concatenate(split(jnp.concatenate(planes, axis=0)), axis=0)
        along = mm_t(pick_z[...], both).astype(BF16)
        picked = mm(along, pick_y[...])
        for tile in range(3):
            first = tile * 64
            pieces = swap_chunks(
                [picked[first + 8 * l : first + 8 * l + 8, :] for l in range(8)], masks
            )
            for b in range(8):
                window[tile, a, b] = pieces[b]
        return carry

    lax.fori_loop(0, 8, make_windows, 0, unroll=8)

    def bcast(ref, tile, row):
        return ref[tile, pl.ds(row, 8, stride=0), :]

    def solve(tile, carry):
        for b in (0, 4):
            fields = [window[tile, a, b : b + 4] for a in range(8)]
            for p in range(8):
                value = None
                for a in range(8):
                    term = bcast(vectors, tile, a * 8 + p) * fields[a]
                    value = term if value is None else value + term
                stage[p, b : b + 4] = value

        def middle(p, carry):
            fields = [stage[p, b] for b in range(8)]
            turned = []
            for q in range(8):
                value = None
                for b in range(8):
                    term = bcast(vectors, tile, 64 + b * 8 + q) * fields[b]
                    value = term if value is None else value + term
                turned.append(value)
            along = [vectors[tile, 128 + 8 * c : 136 + 8 * c, :] for c in range(8)]
            scale = bcast(values, tile, p) + values[tile, 16:24, :]
            divided = []
            for q in range(8):
                value = None
                for c in range(8):
                    term = along[c] * turned[q][c : c + 1, :]
                    value = term if value is None else value + term
                divided.append(value / (scale + bcast(values, tile, 8 + q)))
            across = [vectors[tile, pl.ds(128 + s, 8, stride=8), :] for s in range(8)]
            back = []
            for q in range(8):
                value = None
                for s in range(8):
                    term = across[s] * divided[q][s : s + 1, :]
                    value = term if value is None else value + term
                back.append(value)
            for b in range(8):
                value = None
                for q in range(8):
                    term = bcast(vectors, tile, 64 + b * 8 + q) * back[q]
                    value = term if value is None else value + term
                stage[p, b] = value
            return carry

        lax.fori_loop(0, 8, middle, 0)
        for b in (0, 4):
            fields = [stage[p, b : b + 4] for p in range(8)]
            for a in range(8):
                value = None
                for p in range(8):
                    term = bcast(vectors, tile, a * 8 + p) * fields[p]
                    value = term if value is None else value + term
                solved[tile, a, b : b + 4] = value
        return carry

    lax.fori_loop(0, 1, solve, 0)
    sent[1] = take_sums(first_sums, 0, got_z)
    second_sums = send_sums(1, peers_x, got_x, 8)
    lax.fori_loop(1, 2, solve, 0)
    row_sum = take_sums(second_sums, 1, got_x)
    sent[2] = row_sum
    third_sums = send_sums(2, peers_g, got_g, 16)
    lax.fori_loop(2, 3, solve, 0)
    def add_up(a):
        pieces = []
        for tile in range(3):
            pieces.extend(swap_chunks([solved[tile, a, b] for b in range(8)], masks))
        both = jnp.concatenate(split(jnp.concatenate(pieces, axis=0)), axis=1)
        along = mm(pick_zt[...], both)
        along = along[:, 0:128] + along[:, 128:256]
        return mm_t(pick_yt[...], jnp.concatenate(split(along), axis=1))

    def store_sums(a, carry):
        value = add_up(a)
        for i in range(BX):
            total_rows[pl.ds(pl.multiple_of((6 * i + a) * ROWS, ROWS), ROWS), :] = value[
                32 * i : 32 * i + 32, :
            ]
        return carry

    lax.fori_loop(0, 6, store_sums, 0, unroll=6)
    for a in (6, 7):
        value = add_up(a)
        for i in range(BX):
            here = slice((6 * i + a) * ROWS, (6 * i + a + 1) * ROWS)
            piece = value[32 * i : 32 * i + 32, :]
            total_rows[here, :] = piece if i == BX - 1 else total_rows[here, :] + piece

    rim = send_sides(
        total_rows,
        {1: PLANES - 1, -1: 0, 0: 0},
        {1: 25, -1: 24, 0: 0},
        x_rim,
        y_rim,
        c_rim,
        rim_send,
        rim_recv,
    )
    for copy in rim:
        copy.start()

    y_all = take_sums(third_sums, 2, got_g)

    y_local = y_rows[0:1, :]
    y_middle = sent[2, 0:1, :]
    y_top = y_all[1:2, :]
    for part in range(COARSE // 32):
        here = slice(32 * part, 32 * part + 32)
        terms = x_local[here, :] * y_local + x_middle[here, :] * y_middle + x_top[here, :] * y_top
        column = jnp.sum(terms, axis=1, keepdims=True)
        vertex_col[part : part + 1, :] = jnp.sum(column * eye, axis=0, keepdims=True)
    vertex_col[20:32, :] = jnp.zeros((12, 32), F32)
    coarse_high, coarse_low = split(vertex_col[...])
    spread_out = mm(coarse_high, is_lower) + mm(coarse_low, is_lower)
    at_vertex = jnp.sum(spread_out * is_upper, axis=0, keepdims=True) * (1.0 / 1728.0)
    vertex_high, vertex_low = split(is_xy[...] * at_vertex)
    on_xy = mm_t(vertex_high, hat_zw[...]) + mm_t(vertex_low, hat_zw[...])
    field_high, field_low = split(on_xy)
    field = mm(hat_xy[...], field_high) + mm(hat_xy[...], field_low)
    for x in range(NX):
        at = (x + 1) * ROWS
        out[x] = total_rows[at : at + NY, :] + field[x * ROWS : x * ROWS + NY, :]

    for copy in rim:
        copy.wait()
    for number, (step_x, step_y) in enumerate(SIDES):
        inside = jnp.where(came(step_x, step_y), 1.0, 0.0)
        x = {1: 0, -1: NX - 1}.get(step_x)
        y = {1: 0, -1: NY - 1}.get(step_y)
        if step_y == 0:
            out[x] = out[x] + x_rim[number] * inside
        elif step_x == 0:
            for x in range(NX):
                out[x, y : y + 1, :] = (
                    out[x, y : y + 1, :] + y_rim[number - 2, x : x + 1, :] * inside
                )
        else:
            out[x, y : y + 1, :] = out[x, y : y + 1, :] + c_rim[number - 4, 0:1, :] * inside


def local(residual, fdm_vectors, fdm_values, corner_slot, x_local, x_middle, x_top):
    n_group, n_dev = lax.axis_size("group"), lax.axis_size("dev")
    consts = tables()
    arguments = (
        residual,
        fdm_vectors.reshape(192, ELEMENTS),
        fdm_values.reshape(24, ELEMENTS),
        corner_slot,
        x_local,
        x_middle,
        x_top,
    ) + tuple(jnp.asarray(value) for value in consts)
    vmem = [pltpu.VMEM(value.shape, value.dtype) for value in arguments[1:]]
    n_sides = len(SIDES)
    scratch = (
        [pltpu.VMEM((PLANES, ROWS, NZ), F32)]
        + vmem
        + [
            pltpu.VMEM((3, 192, 128), F32),
            pltpu.VMEM((3, 24, 128), F32),
            pltpu.VMEM((3, 8, 8, 8, 128), F32),
            pltpu.VMEM((8, 8, 8, 128), F32),
            pltpu.VMEM((3, 8, 8, 8, 128), F32),
            pltpu.VMEM((PLANES, ROWS, NZ), F32),
            pltpu.VMEM((2, 24, NZ), F32),
            pltpu.VMEM((4, 8, NZ), F32),
            pltpu.VMEM((2, 24, NZ), F32),
            pltpu.VMEM((2, 24, NZ), F32),
            pltpu.VMEM((4, 8, NZ), F32),
            pltpu.VMEM((2, 24, NZ), F32),
            pltpu.VMEM((2, 24, NZ), F32),
            pltpu.VMEM((4, 8, NZ), F32),
            pltpu.VMEM((32, 32), F32),
            pltpu.VMEM((32, 32), F32),
            pltpu.VMEM((8, 128), F32),
            pltpu.VMEM((3, 8, 128), F32),
            pltpu.VMEM((8, 8, 128), F32),
            pltpu.VMEM((8, 8, 128), F32),
            pltpu.VMEM((8, 8, 128), F32),
            pltpu.SemaphoreType.DMA((len(arguments),)),
            pltpu.SemaphoreType.DMA((n_sides,)),
            pltpu.SemaphoreType.DMA((n_sides,)),
            pltpu.SemaphoreType.DMA((n_sides,)),
            pltpu.SemaphoreType.DMA((n_sides,)),
            pltpu.SemaphoreType.DMA((24,)),
            pltpu.SemaphoreType.DMA((24,)),
        ]
    )
    return pl.pallas_call(
        functools.partial(kernel, n_group, n_dev),
        out_shape=pltpu.VMEM((NX, NY, NZ), F32),
        in_specs=[pl.BlockSpec(memory_space=pl.ANY)] * len(arguments),
        out_specs=pl.BlockSpec(memory_space=pltpu.VMEM),
        scratch_shapes=scratch,
        compiler_params=pltpu.CompilerParams(
            collective_id=0, has_side_effects=True, vmem_limit_bytes=40 * 1024 * 1024
        ),
    )(*[pltpu.with_memory_space_constraint(value, pltpu.HBM) for value in arguments])


def solution(mesh):
    return jax.shard_map(
        local,
        mesh=mesh,
        in_specs=(
            P("group", "dev", None),
            P(None, None, None, ("group", "dev")),
            P(None, None, ("group", "dev")),
            P(None, ("group", "dev")),
            P(("group", "dev"), None),
            P(("group", "dev"), None),
            P(("group", "dev"), None),
        ),
        out_specs=P("group", "dev", None),
        check_vma=False,
    )
```

```python
import functools

import jax
import jax.numpy as jnp
import ml_dtypes
import numpy as np
from jax import lax
from jax.experimental import pallas as pl
from jax.experimental.pallas import tpu as pltpu
from jax.sharding import PartitionSpec as P

F32 = jnp.float32
BF16 = jnp.bfloat16
MESH = pl.DeviceIdType.MESH

BX, BY, BZ = 4, 4, 24
NX, NY, NZ = 6 * BX, 6 * BY, 6 * BZ
ELEMENTS = BX * BY * BZ
ROWS = 32
PLANES = NX + 2
LANES = 640
COARSE = 640
SIDES = ((1, 0), (-1, 0), (0, 1), (0, -1), (1, 1), (1, -1), (-1, 1), (-1, -1))


def row_of(y):
    return {0: 24, 25: 25}.get(y, y - 1)


def tables():
    bf16 = ml_dtypes.bfloat16
    pick_z = np.zeros((8 * BZ, NZ), np.float32)
    for l in range(BZ):
        for c in range(8):
            z = 6 * l + c - 1
            if 0 <= z < NZ:
                pick_z[8 * l + c, z] = 1
    pick_y = np.zeros((128, 128), np.float32)
    for i in range(4):
        for b in range(8):
            for j in range(4):
                pick_y[i * 32 + row_of(6 * j + b), i * 32 + b * 4 + j] = 1
    order = np.zeros((ELEMENTS, ELEMENTS), np.float32)
    for i in range(BX):
        for j in range(BY):
            for l in range(BZ):
                order[(i * BY + j) * BZ + l, l // 8 * 128 + i * 32 + l % 8 * 4 + j] = 1

    def hats(elements):
        weights = np.zeros((6 * elements, elements + 1), np.float32)
        for e in range(elements):
            for m in range(6):
                weights[6 * e + m, e] = 11 - 2 * m
                weights[6 * e + m, e + 1] = 2 * m + 1
        return weights

    hat_x, hat_y, hat_z = hats(BX), hats(BY), hats(BZ)
    hat_xy = np.zeros((NX, ROWS, 32), np.float32)
    hat_xy[:, :NY, :25] = np.einsum("xv,yw->xyvw", hat_x, hat_y).reshape(NX, NY, 25)
    hat_xy = hat_xy.reshape(NX * ROWS, 32)
    hat_zw = np.zeros((NZ, LANES), np.float32)
    is_xy = np.zeros((32, LANES), np.float32)
    pick_e = np.zeros((ELEMENTS, LANES), np.float32)
    is_corner = np.zeros((8, LANES), np.float32)
    for vx in range(5):
        for vy in range(5):
            for vz in range(25):
                w = (vx * 5 + vy) * 25 + vz
                hat_zw[:, w] = hat_z[:, vz]
                is_xy[vx * 5 + vy, w] = 1
                i, j, l = min(vx, 3), min(vy, 3), min(vz, 23)
                pick_e[(i * BY + j) * BZ + l, w] = 1
                is_corner[4 * (vx - i) + 2 * (vy - j) + (vz - l), w] = 1
    return (
        pick_z.astype(bf16),
        pick_z.T.copy().astype(bf16),
        np.concatenate([pick_y, pick_y], axis=0).astype(bf16),
        np.concatenate([pick_y, pick_y], axis=1).astype(bf16),
        order.astype(bf16),
        hat_xy.astype(bf16),
        hat_xy.T.copy().astype(bf16),
        hat_zw.astype(bf16),
        pick_e.astype(bf16),
        is_xy,
        is_corner,
    )


def split(value):
    high = value.astype(BF16)
    return high, (value - high.astype(F32)).astype(BF16)


def mm(a, b):
    return lax.dot_general(a, b, (((1,), (0,)), ((), ())), preferred_element_type=F32)


def mm_t(a, b):
    return lax.dot_general(a, b, (((1,), (1,)), ((), ())), preferred_element_type=F32)


def swap_chunks(pieces, masks):
    pieces = list(pieces)
    for bit in range(3):
        shift = 4 << bit
        mask = masks[bit]
        for low in range(8):
            if low >> bit & 1:
                continue
            high = low | 1 << bit
            x, y = pieces[low], pieces[high]
            pieces[low] = jnp.where(mask, pltpu.roll(y, shift, 1), x)
            pieces[high] = jnp.where(mask, y, pltpu.roll(x, 128 - shift, 1))
    return pieces


def kernel(
    n_group,
    n_dev,
    residual,
    vectors_in,
    values_in,
    slot_in,
    x_local_in,
    x_middle_in,
    x_top_in,
    pick_z_in,
    pick_zt_in,
    pick_y_in,
    pick_yt_in,
    order_in,
    hat_xy_in,
    hat_xyt_in,
    hat_zw_in,
    pick_e_in,
    is_xy_in,
    is_corner_in,
    out,
    block,
    vectors_raw,
    values_raw,
    slot,
    x_local,
    x_middle,
    x_top,
    pick_z,
    pick_zt,
    pick_y,
    pick_yt,
    order,
    hat_xy,
    hat_xyt,
    hat_zw,
    pick_e,
    is_xy,
    is_corner,
    vectors,
    values,
    window,
    stage,
    solved,
    total,
    y_halo_pack,
    c_halo_pack,
    y_rim_pack,
    c_rim_pack,
    x_halo,
    y_halo,
    c_halo,
    x_rim,
    y_rim,
    c_rim,
    small,
    vertex_col,
    y_rows,
    sent,
    got_z,
    got_x,
    got_g,
    load_sem,
    halo_send,
    halo_recv,
    rim_send,
    rim_recv,
    sum_send,
    sum_recv,
):
    group = lax.axis_index("group")
    dev = lax.axis_index("dev")
    n_low = min(8, n_dev)
    n_high = n_dev // n_low
    high, low = dev // n_low, dev % n_low

    def beside(step_x, step_y):
        return ((group + step_x + n_group) % n_group, (dev + step_y + n_dev) % n_dev)

    def came(step_x, step_y):
        from_x, from_y = group - step_x, dev - step_y
        return (from_x >= 0) & (from_x < n_group) & (from_y >= 0) & (from_y < n_dev)

    def goes(step_x, step_y):
        return came(-step_x, -step_y)

    peers_z = [(group, high * n_low + (low + k) % n_low) for k in range(1, n_low)]
    peers_x = [(group, (high + k) % n_high * n_low + low) for k in range(1, n_high)]
    peers_g = [((group + k) % n_group, dev) for k in range(1, n_group)]

    pairs = [
        (residual, block.at[pl.ds(1, NX), pl.ds(0, NY), :]),
        (hat_xyt_in, hat_xyt),
        (hat_zw_in, hat_zw),
        (is_xy_in, is_xy),
        (slot_in, slot),
        (pick_e_in, pick_e),
        (is_corner_in, is_corner),
        (x_local_in, x_local),
        (x_middle_in, x_middle),
        (x_top_in, x_top),
        (vectors_in, vectors_raw),
        (values_in, values_raw),
        (order_in, order),
        (pick_z_in, pick_z),
        (pick_y_in, pick_y),
        (pick_yt_in, pick_yt),
        (pick_zt_in, pick_zt),
        (hat_xy_in, hat_xy),
    ]
    loads = [
        pltpu.make_async_copy(source, target, load_sem.at[number])
        for number, (source, target) in enumerate(pairs)
    ]
    for load in loads:
        load.start()

    barrier = pltpu.get_barrier_semaphore()
    partners = peers_z + peers_x + peers_g
    greeted = len(partners)
    for side in SIDES:
        greeted = greeted + goes(*side).astype(jnp.int32)

        @pl.when(goes(*side))
        def _(side=side):
            pl.semaphore_signal(barrier, inc=1, device_id=beside(*side), device_id_type=MESH)

    for partner in partners:
        pl.semaphore_signal(barrier, inc=1, device_id=partner, device_id_type=MESH)

    rows = block.reshape(PLANES * ROWS, NZ)
    total_rows = total.reshape(PLANES * ROWS, NZ)
    empty = jnp.zeros((8, NZ), F32)
    for plane in range(PLANES):
        for part in range(0 if plane in (0, PLANES - 1) else 24, ROWS, 8):
            rows[plane * ROWS + part : plane * ROWS + part + 8, :] = empty

    def send_sides(source, x_planes, y_rows_at, packs, x_into, y_into, c_into, send, recv):
        copies = []
        y_pack, c_pack = packs
        for number, (step_x, step_y) in enumerate(SIDES):
            plane = x_planes[step_x]
            row = y_rows_at[step_y]
            if step_y == 0:
                piece = source.at[pl.ds(plane * ROWS, 24), :]
                into = x_into.at[number]
            elif step_x == 0:
                for x in range(NX):
                    at = (x + 1) * ROWS + row
                    y_pack[number - 2, x : x + 1, :] = source[at : at + 1, :]
                piece = y_pack.at[number - 2]
                into = y_into.at[number - 2]
            else:
                c_pack[number - 4] = source[plane * ROWS + row : plane * ROWS + row + 1, :]
                piece = c_pack.at[number - 4]
                into = c_into.at[number - 4]
            copies.append(
                pltpu.make_async_remote_copy(
                    src_ref=piece,
                    dst_ref=into,
                    send_sem=send.at[number],
                    recv_sem=recv.at[number],
                    device_id=beside(step_x, step_y),
                    device_id_type=MESH,
                )
            )
        return copies

    loads[0].wait()
    halo = send_sides(
        rows,
        {1: 24, -1: 1, 0: 0},
        {1: 23, -1: 0, 0: 0},
        (y_halo_pack, c_halo_pack),
        x_halo,
        y_halo,
        c_halo,
        halo_send,
        halo_recv,
    )
    pl.semaphore_wait(barrier, greeted)

    def start_sides(copies):
        for side, copy in zip(SIDES, copies):
            pl.when(goes(*side))(copy.start)

    start_sides(halo)

    for load in loads[1:10]:
        load.wait()
    own_high, own_low = split(rows[ROWS : ROWS * (NX + 1), :])
    on_xy = mm(hat_xyt[...], own_high) + mm(hat_xyt[...], own_low)
    on_xy_high, on_xy_low = split(on_xy)
    on_vertex = mm(on_xy_high, hat_zw[...]) + mm(on_xy_low, hat_zw[...])
    at_vertex = jnp.sum(on_vertex * is_xy[...], axis=0, keepdims=True) * (1.0 / 1728.0)

    slots = slot[...]
    parts = jnp.concatenate([(slots >> 5).astype(F32), (slots & 31).astype(F32)], axis=0)
    picked = mm(parts.astype(BF16), pick_e[...])
    upper = jnp.sum(picked[0:8] * is_corner[...], axis=0, keepdims=True)
    lower = jnp.sum(picked[8:16] * is_corner[...], axis=0, keepdims=True)
    count = lax.broadcasted_iota(jnp.int32, (32, LANES), 0).astype(F32)
    is_upper = jnp.where(count == upper, 1.0, 0.0)
    is_lower = jnp.where(count == lower, 1.0, 0.0).astype(BF16)
    by_high, by_low = split(is_upper * at_vertex)
    small[...] = mm_t(by_high, is_lower) + mm_t(by_low, is_lower)

    eye = jnp.where(
        lax.broadcasted_iota(jnp.int32, (32, 32), 0) == lax.broadcasted_iota(jnp.int32, (32, 32), 1),
        1.0,
        0.0,
    )
    y_sums = [jnp.zeros((8, 128), F32) for _ in range(3)]
    for part in range(COARSE // 32):
        column = jnp.sum(small[part : part + 1, :] * eye, axis=1, keepdims=True)
        for level, factor in enumerate((x_local, x_middle, x_top)):
            weighted = column * factor[32 * part : 32 * part + 32, :]
            y_sums[level] = y_sums[level] + (
                (weighted[0:8] + weighted[8:16]) + (weighted[16:24] + weighted[24:32])
            )
    y_local, y_middle, y_top = [jnp.sum(value, axis=0, keepdims=True) for value in y_sums]
    row_number = lax.broadcasted_iota(jnp.int32, (8, 128), 0)
    y_rows[...] = jnp.broadcast_to(y_local, (8, 128))
    sent[0] = jnp.where(row_number == 0, y_middle, y_top)

    def send_sums(stage_number, peers, into, first):
        copies = []
        for k, peer in enumerate(peers):
            copies.append(
                pltpu.make_async_remote_copy(
                    src_ref=sent.at[stage_number],
                    dst_ref=into.at[k],
                    send_sem=sum_send.at[first + k],
                    recv_sem=sum_recv.at[first + k],
                    device_id=peer,
                    device_id_type=MESH,
                )
            )
        for copy in copies:
            copy.start()
        return copies

    def take_sums(copies, stage_number, into):
        for copy in copies:
            copy.wait_recv()
        value = sent[stage_number]
        for k in range(len(copies)):
            value = value + into[k]
        return value

    first_sums = send_sums(0, peers_z, got_z, 0)

    for load in loads[10:]:
        load.wait()
    raw = jnp.concatenate([vectors_raw[...], values_raw[...]], axis=0)
    raw_high, raw_rest = split(raw)
    ordered = mm(raw_high, order[...]) + mm(raw_rest, order[...])
    for tile in range(3):
        vectors[tile] = ordered[0:192, 128 * tile : 128 * tile + 128]
        values[tile] = ordered[192:216, 128 * tile : 128 * tile + 128]

    for number, (step_x, step_y) in enumerate(SIDES):
        plane = {1: 0, -1: PLANES - 1}.get(step_x)
        row = {1: 24, -1: 25}.get(step_y)

        @pl.when(came(step_x, step_y))
        def _(number=number, step_x=step_x, step_y=step_y, plane=plane, row=row):
            halo[number].wait_recv()
            if step_y == 0:
                rows[plane * ROWS : plane * ROWS + 24, :] = x_halo[number]
            elif step_x == 0:
                for x in range(NX):
                    at = (x + 1) * ROWS + row
                    rows[at : at + 1, :] = y_halo[number - 2, x : x + 1, :]
            else:
                rows[plane * ROWS + row : plane * ROWS + row + 1, :] = c_halo[number - 4]

    lane = lax.broadcasted_iota(jnp.int32, (8, 128), 1)
    masks = [(lane >> (2 + bit)) & 1 == 1 for bit in range(3)]

    def make_windows(a, carry):
        planes = [
            rows[pl.ds(pl.multiple_of((6 * i + a) * ROWS, ROWS), ROWS), :] for i in range(BX)
        ]
        both = jnp.concatenate(split(jnp.concatenate(planes, axis=0)), axis=0)
        along = mm_t(pick_z[...], both).astype(BF16)
        picked = mm(along, pick_y[...])
        for tile in range(3):
            first = tile * 64
            pieces = swap_chunks(
                [picked[first + 8 * l : first + 8 * l + 8, :] for l in range(8)], masks
            )
            for b in range(8):
                window[tile, a, b] = pieces[b]
        return carry

    lax.fori_loop(0, 8, make_windows, 0, unroll=8)

    def bcast(ref, tile, row):
        return ref[tile, pl.ds(row, 8, stride=0), :]

    def solve(tile, carry):
        for b in (0, 4):
            fields = [window[tile, a, b : b + 4] for a in range(8)]
            for p in range(8):
                value = None
                for a in range(8):
                    term = bcast(vectors, tile, a * 8 + p) * fields[a]
                    value = term if value is None else value + term
                stage[p, b : b + 4] = value

        def middle(p, carry):
            fields = [stage[p, b] for b in range(8)]
            turned = []
            for q in range(8):
                value = None
                for b in range(8):
                    term = bcast(vectors, tile, 64 + b * 8 + q) * fields[b]
                    value = term if value is None else value + term
                turned.append(value)
            along = [vectors[tile, 128 + 8 * c : 136 + 8 * c, :] for c in range(8)]
            scale = bcast(values, tile, p) + values[tile, 16:24, :]
            divided = []
            for q in range(8):
                value = None
                for c in range(8):
                    term = along[c] * turned[q][c : c + 1, :]
                    value = term if value is None else value + term
                divided.append(value / (scale + bcast(values, tile, 8 + q)))
            across = [vectors[tile, pl.ds(128 + s, 8, stride=8), :] for s in range(8)]
            back = []
            for q in range(8):
                value = None
                for s in range(8):
                    term = across[s] * divided[q][s : s + 1, :]
                    value = term if value is None else value + term
                back.append(value)
            for b in range(8):
                value = None
                for q in range(8):
                    term = bcast(vectors, tile, 64 + b * 8 + q) * back[q]
                    value = term if value is None else value + term
                stage[p, b] = value
            return carry

        lax.fori_loop(0, 8, middle, 0)
        for b in (0, 4):
            fields = [stage[p, b : b + 4] for p in range(8)]
            for a in range(8):
                value = None
                for p in range(8):
                    term = bcast(vectors, tile, a * 8 + p) * fields[p]
                    value = term if value is None else value + term
                solved[tile, a, b : b + 4] = value
        return carry

    lax.fori_loop(0, 1, solve, 0)
    sent[1] = take_sums(first_sums, 0, got_z)
    second_sums = send_sums(1, peers_x, got_x, 8)
    lax.fori_loop(1, 2, solve, 0)
    lax.fori_loop(2, 3, solve, 0)
    sent[2] = take_sums(second_sums, 1, got_x)
    third_sums = send_sums(2, peers_g, got_g, 16)
    def add_up(a):
        pieces = []
        for tile in range(3):
            pieces.extend(swap_chunks([solved[tile, a, b] for b in range(8)], masks))
        both = jnp.concatenate(split(jnp.concatenate(pieces, axis=0)), axis=1)
        along = mm(pick_zt[...], both)
        along = along[:, 0:128] + along[:, 128:256]
        return mm_t(pick_yt[...], jnp.concatenate(split(along), axis=1))

    def store_sums(a, carry):
        value = add_up(a)
        for i in range(BX):
            total_rows[pl.ds(pl.multiple_of((6 * i + a) * ROWS, ROWS), ROWS), :] = value[
                32 * i : 32 * i + 32, :
            ]
        return carry

    lax.fori_loop(0, 6, store_sums, 0, unroll=6)
    for a in (6, 7):
        value = add_up(a)
        for i in range(BX):
            here = slice((6 * i + a) * ROWS, (6 * i + a + 1) * ROWS)
            piece = value[32 * i : 32 * i + 32, :]
            total_rows[here, :] = piece if i == BX - 1 else total_rows[here, :] + piece

    rim = send_sides(
        total_rows,
        {1: PLANES - 1, -1: 0, 0: 0},
        {1: 25, -1: 24, 0: 0},
        (y_rim_pack, c_rim_pack),
        x_rim,
        y_rim,
        c_rim,
        rim_send,
        rim_recv,
    )
    start_sides(rim)

    y_all = take_sums(third_sums, 2, got_g)

    y_local = y_rows[0:1, :]
    y_middle = sent[2, 0:1, :]
    y_top = y_all[1:2, :]
    for part in range(COARSE // 32):
        here = slice(32 * part, 32 * part + 32)
        terms = x_local[here, :] * y_local + x_middle[here, :] * y_middle + x_top[here, :] * y_top
        column = jnp.sum(terms, axis=1, keepdims=True)
        vertex_col[part : part + 1, :] = jnp.sum(column * eye, axis=0, keepdims=True)
    vertex_col[20:32, :] = jnp.zeros((12, 32), F32)
    coarse_high, coarse_low = split(vertex_col[...])
    spread_out = mm(coarse_high, is_lower) + mm(coarse_low, is_lower)
    at_vertex = jnp.sum(spread_out * is_upper, axis=0, keepdims=True) * (1.0 / 1728.0)
    vertex_high, vertex_low = split(is_xy[...] * at_vertex)
    on_xy = mm_t(vertex_high, hat_zw[...]) + mm_t(vertex_low, hat_zw[...])
    field_high, field_low = split(on_xy)
    field = mm(hat_xy[...], field_high) + mm(hat_xy[...], field_low)
    for x in range(NX):
        at = (x + 1) * ROWS
        out[x] = total_rows[at : at + NY, :] + field[x * ROWS : x * ROWS + NY, :]

    for number, (step_x, step_y) in enumerate(SIDES):
        x = {1: 0, -1: NX - 1}.get(step_x)
        y = {1: 0, -1: NY - 1}.get(step_y)

        @pl.when(came(step_x, step_y))
        def _(number=number, step_x=step_x, step_y=step_y, x=x, y=y):
            rim[number].wait_recv()
            if step_y == 0:
                out[x] = out[x] + x_rim[number]
            elif step_x == 0:
                for x in range(NX):
                    out[x, y : y + 1, :] = out[x, y : y + 1, :] + y_rim[number - 2, x : x + 1, :]
            else:
                out[x, y : y + 1, :] = out[x, y : y + 1, :] + c_rim[number - 4]

    for side, halo_copy, rim_copy in zip(SIDES, halo, rim):

        @pl.when(goes(*side))
        def _(halo_copy=halo_copy, rim_copy=rim_copy):
            halo_copy.wait_send()
            rim_copy.wait_send()

    for copy in first_sums + second_sums + third_sums:
        copy.wait_send()


def local(residual, fdm_vectors, fdm_values, corner_slot, x_local, x_middle, x_top):
    n_group, n_dev = lax.axis_size("group"), lax.axis_size("dev")
    consts = tables()
    arguments = (
        residual,
        fdm_vectors.reshape(192, ELEMENTS),
        fdm_values.reshape(24, ELEMENTS),
        corner_slot,
        x_local,
        x_middle,
        x_top,
    ) + tuple(jnp.asarray(value) for value in consts)
    vmem = [pltpu.VMEM(value.shape, value.dtype) for value in arguments[1:]]
    n_sides = len(SIDES)
    scratch = (
        [pltpu.VMEM((PLANES, ROWS, NZ), F32)]
        + vmem
        + [
            pltpu.VMEM((3, 192, 128), F32),
            pltpu.VMEM((3, 24, 128), F32),
            pltpu.VMEM((3, 8, 8, 8, 128), F32),
            pltpu.VMEM((8, 8, 8, 128), F32),
            pltpu.VMEM((3, 8, 8, 8, 128), F32),
            pltpu.VMEM((PLANES, ROWS, NZ), F32),
            pltpu.VMEM((2, 24, NZ), F32),
            pltpu.VMEM((4, 1, NZ), F32),
            pltpu.VMEM((2, 24, NZ), F32),
            pltpu.VMEM((4, 1, NZ), F32),
            pltpu.VMEM((2, 24, NZ), F32),
            pltpu.VMEM((2, 24, NZ), F32),
            pltpu.VMEM((4, 1, NZ), F32),
            pltpu.VMEM((2, 24, NZ), F32),
            pltpu.VMEM((2, 24, NZ), F32),
            pltpu.VMEM((4, 1, NZ), F32),
            pltpu.VMEM((32, 32), F32),
            pltpu.VMEM((32, 32), F32),
            pltpu.VMEM((8, 128), F32),
            pltpu.VMEM((3, 8, 128), F32),
            pltpu.VMEM((8, 8, 128), F32),
            pltpu.VMEM((8, 8, 128), F32),
            pltpu.VMEM((8, 8, 128), F32),
            pltpu.SemaphoreType.DMA((len(arguments),)),
            pltpu.SemaphoreType.DMA((n_sides,)),
            pltpu.SemaphoreType.DMA((n_sides,)),
            pltpu.SemaphoreType.DMA((n_sides,)),
            pltpu.SemaphoreType.DMA((n_sides,)),
            pltpu.SemaphoreType.DMA((24,)),
            pltpu.SemaphoreType.DMA((24,)),
        ]
    )
    return pl.pallas_call(
        functools.partial(kernel, n_group, n_dev),
        out_shape=pltpu.VMEM((NX, NY, NZ), F32),
        in_specs=[pl.BlockSpec(memory_space=pl.ANY)] * len(arguments),
        out_specs=pl.BlockSpec(memory_space=pltpu.VMEM),
        scratch_shapes=scratch,
        compiler_params=pltpu.CompilerParams(
            collective_id=0, has_side_effects=True, vmem_limit_bytes=40 * 1024 * 1024
        ),
    )(*[pltpu.with_memory_space_constraint(value, pltpu.HBM) for value in arguments])


def solution(mesh):
    return jax.shard_map(
        local,
        mesh=mesh,
        in_specs=(
            P("group", "dev", None),
            P(None, None, None, ("group", "dev")),
            P(None, None, ("group", "dev")),
            P(None, ("group", "dev")),
            P(("group", "dev"), None),
            P(("group", "dev"), None),
            P(("group", "dev"), None),
        ),
        out_specs=P("group", "dev", None),
        check_vma=False,
    )
```

```python
import functools

import jax
import jax.numpy as jnp
import ml_dtypes
import numpy as np
from jax import lax
from jax.experimental import pallas as pl
from jax.experimental.pallas import tpu as pltpu
from jax.sharding import PartitionSpec as P

F32 = jnp.float32
BF16 = jnp.bfloat16
MESH = pl.DeviceIdType.MESH

BX, BY, BZ = 4, 4, 24
NX, NY, NZ = 6 * BX, 6 * BY, 6 * BZ
ELEMENTS = BX * BY * BZ
ROWS = 32
PLANES = NX + 2
LANES = 640
COARSE = 640
SIDES = ((1, 0), (-1, 0), (0, 1), (0, -1), (1, 1), (1, -1), (-1, 1), (-1, -1))


def row_of(y):
    return {0: 24, 25: 25}.get(y, y - 1)


def tables():
    bf16 = ml_dtypes.bfloat16
    pick_z = np.zeros((8 * BZ, NZ), np.float32)
    for l in range(BZ):
        for c in range(8):
            z = 6 * l + c - 1
            if 0 <= z < NZ:
                pick_z[8 * l + c, z] = 1
    pick_y = np.zeros((128, 128), np.float32)
    for i in range(4):
        for b in range(8):
            for j in range(4):
                pick_y[i * 32 + row_of(6 * j + b), i * 32 + b * 4 + j] = 1
    order = np.zeros((ELEMENTS, ELEMENTS), np.float32)
    for i in range(BX):
        for j in range(BY):
            for l in range(BZ):
                order[(i * BY + j) * BZ + l, l // 8 * 128 + i * 32 + l % 8 * 4 + j] = 1

    def hats(elements):
        weights = np.zeros((6 * elements, elements + 1), np.float32)
        for e in range(elements):
            for m in range(6):
                weights[6 * e + m, e] = 11 - 2 * m
                weights[6 * e + m, e + 1] = 2 * m + 1
        return weights

    hat_x, hat_y, hat_z = hats(BX), hats(BY), hats(BZ)
    hat_xy = np.zeros((NX, ROWS, 32), np.float32)
    hat_xy[:, :NY, :25] = np.einsum("xv,yw->xyvw", hat_x, hat_y).reshape(NX, NY, 25)
    hat_xy = hat_xy.reshape(NX * ROWS, 32)
    hat_zw = np.zeros((NZ, LANES), np.float32)
    is_xy = np.zeros((32, LANES), np.float32)
    pick_e = np.zeros((ELEMENTS, LANES), np.float32)
    is_corner = np.zeros((8, LANES), np.float32)
    for vx in range(5):
        for vy in range(5):
            for vz in range(25):
                w = (vx * 5 + vy) * 25 + vz
                hat_zw[:, w] = hat_z[:, vz]
                is_xy[vx * 5 + vy, w] = 1
                i, j, l = min(vx, 3), min(vy, 3), min(vz, 23)
                pick_e[(i * BY + j) * BZ + l, w] = 1
                is_corner[4 * (vx - i) + 2 * (vy - j) + (vz - l), w] = 1
    return (
        pick_z.astype(bf16),
        pick_z.T.copy().astype(bf16),
        np.concatenate([pick_y, pick_y], axis=0).astype(bf16),
        np.concatenate([pick_y, pick_y], axis=1).astype(bf16),
        order.astype(bf16),
        hat_xy.astype(bf16),
        hat_xy.T.copy().astype(bf16),
        hat_zw.astype(bf16),
        pick_e.astype(bf16),
        is_xy,
        is_corner,
    )


def split(value):
    high = value.astype(BF16)
    return high, (value - high.astype(F32)).astype(BF16)


def mm(a, b):
    return lax.dot_general(a, b, (((1,), (0,)), ((), ())), preferred_element_type=F32)


def mm_t(a, b):
    return lax.dot_general(a, b, (((1,), (1,)), ((), ())), preferred_element_type=F32)


def swap_chunks(pieces, masks):
    pieces = list(pieces)
    for bit in range(3):
        shift = 4 << bit
        mask = masks[bit]
        for low in range(8):
            if low >> bit & 1:
                continue
            high = low | 1 << bit
            x, y = pieces[low], pieces[high]
            pieces[low] = jnp.where(mask, pltpu.roll(y, shift, 1), x)
            pieces[high] = jnp.where(mask, y, pltpu.roll(x, 128 - shift, 1))
    return pieces


def kernel(
    n_group,
    n_dev,
    residual,
    vectors_in,
    values_in,
    slot_in,
    x_local_in,
    x_middle_in,
    x_top_in,
    pick_z_in,
    pick_zt_in,
    pick_y_in,
    pick_yt_in,
    order_in,
    hat_xy_in,
    hat_xyt_in,
    hat_zw_in,
    pick_e_in,
    is_xy_in,
    is_corner_in,
    out,
    block,
    vectors_raw,
    values_raw,
    slot,
    x_local,
    x_middle,
    x_top,
    pick_z,
    pick_zt,
    pick_y,
    pick_yt,
    order,
    hat_xy,
    hat_xyt,
    hat_zw,
    pick_e,
    is_xy,
    is_corner,
    vectors,
    values,
    window,
    stage,
    solved,
    total,
    y_halo_pack,
    c_halo_pack,
    y_rim_pack,
    c_rim_pack,
    x_halo,
    y_halo,
    c_halo,
    x_rim,
    y_rim,
    c_rim,
    small,
    vertex_col,
    y_rows,
    sent,
    got_first,
    got_second,
    load_sem,
    halo_send,
    halo_recv,
    rim_send,
    rim_recv,
    first_send,
    first_recv,
    second_send,
    second_recv,
    hello,
):
    group = lax.axis_index("group")
    dev = lax.axis_index("dev")
    n_z = min(8, n_dev)
    n_x, n_y = n_dev // n_z, n_group // 2
    at_x, at_z = dev // n_z, dev % n_z
    at_y, core = group // 2, group % 2

    def beside(step_x, step_y):
        return (group + step_x, dev + step_y)

    def ahead(place, step, size):
        place = place + step
        return jnp.where(place >= size, place - size, place)

    def came(step_x, step_y):
        from_x, from_y = group - step_x, dev - step_y
        return (from_x >= 0) & (from_x < n_group) & (from_y >= 0) & (from_y < n_dev)

    def goes(step_x, step_y):
        return came(-step_x, -step_y)

    peers_first, peers_second = [], []
    for step in range(n_z):
        for other in range(2):
            if step or other:
                to_z = ahead(at_z, step, n_z)
                to_core = 1 - core if other else core
                device = (2 * at_y + to_core, n_z * at_x + to_z)
                later = 2 * to_z + to_core > 2 * at_z + core
                peers_first.append((other == 0, device, later))
    for step in range(n_x):
        for other in range(n_y):
            if step or other:
                to_x, to_y = ahead(at_x, step, n_x), ahead(at_y, other, n_y)
                device = (2 * to_y + core, n_z * to_x + at_z)
                later = n_y * to_x + to_y > n_y * at_x + at_y
                peers_second.append((other == 0, device, later))
    earlier_first = 2 * at_z + core
    earlier_second = n_y * at_x + at_y
    middle_z = (at_z >= 1) & (at_z <= 3)

    pairs = [
        (residual, block.at[pl.ds(1, NX), pl.ds(0, NY), :]),
        (hat_xyt_in, hat_xyt),
        (hat_zw_in, hat_zw),
        (is_xy_in, is_xy),
        (slot_in, slot),
        (pick_e_in, pick_e),
        (is_corner_in, is_corner),
        (x_local_in, x_local),
        (x_middle_in, x_middle),
        (x_top_in, x_top),
        (vectors_in, vectors_raw),
        (values_in, values_raw),
        (order_in, order),
        (pick_z_in, pick_z),
        (pick_y_in, pick_y),
        (pick_yt_in, pick_yt),
        (pick_zt_in, pick_zt),
        (hat_xy_in, hat_xy),
    ]
    loads = [
        pltpu.make_async_copy(source, target, load_sem.at[number])
        for number, (source, target) in enumerate(pairs)
    ]
    for load in loads:
        load.start()

    barrier = pltpu.get_barrier_semaphore()
    greeted = earlier_first + earlier_second
    for side in SIDES:
        greeted = greeted + goes(*side).astype(jnp.int32)

        @pl.when(goes(*side))
        def _(side=side):
            pl.semaphore_signal(barrier, inc=1, device_id=beside(*side), device_id_type=MESH)

    for _, device, later in peers_first + peers_second:

        @pl.when(later)
        def _(device=device):
            pl.semaphore_signal(barrier, inc=1, device_id=device, device_id_type=MESH)

    rows = block.reshape(PLANES * ROWS, NZ)
    total_rows = total.reshape(PLANES * ROWS, NZ)
    empty = jnp.zeros((8, NZ), F32)
    for plane in range(PLANES):
        for part in range(0 if plane in (0, PLANES - 1) else 24, ROWS, 8):
            rows[plane * ROWS + part : plane * ROWS + part + 8, :] = empty

    def send_sides(source, x_planes, y_rows_at, packs, x_into, y_into, c_into, send, recv):
        copies = []
        y_pack, c_pack = packs
        for number, (step_x, step_y) in enumerate(SIDES):
            plane = x_planes[step_x]
            row = y_rows_at[step_y]
            if step_y == 0:
                piece = source.at[pl.ds(plane * ROWS, 24), :]
                into = x_into.at[number]
            elif step_x == 0:
                for x in range(NX):
                    at = (x + 1) * ROWS + row
                    y_pack[number - 2, x : x + 1, :] = source[at : at + 1, :]
                piece = y_pack.at[number - 2]
                into = y_into.at[number - 2]
            else:
                c_pack[number - 4] = source[plane * ROWS + row : plane * ROWS + row + 1, :]
                piece = c_pack.at[number - 4]
                into = c_into.at[number - 4]
            copies.append(
                pltpu.make_async_remote_copy(
                    src_ref=piece,
                    dst_ref=into,
                    send_sem=send.at[number],
                    recv_sem=recv.at[number],
                    device_id=beside(step_x, step_y),
                    device_id_type=MESH,
                )
            )
        return copies

    loads[0].wait()
    halo = send_sides(
        rows,
        {1: 24, -1: 1, 0: 0},
        {1: 23, -1: 0, 0: 0},
        (y_halo_pack, c_halo_pack),
        x_halo,
        y_halo,
        c_halo,
        halo_send,
        halo_recv,
    )
    pl.semaphore_wait(barrier, greeted)

    def start_sides(copies):
        for side, copy in zip(SIDES, copies):
            pl.when(goes(*side))(copy.start)

    start_sides(halo)
    for number, peers in enumerate((peers_first, peers_second)):
        for _, device, later in peers:

            @pl.when(jnp.logical_not(later))
            def _(device=device, number=number):
                pl.semaphore_signal(
                    hello.at[number], inc=1, device_id=device, device_id_type=MESH
                )

    for load in loads[1:10]:
        load.wait()
    own_high, own_low = split(rows[ROWS : ROWS * (NX + 1), :])
    on_xy = mm(hat_xyt[...], own_high) + mm(hat_xyt[...], own_low)
    on_xy_high, on_xy_low = split(on_xy)
    on_vertex = mm(on_xy_high, hat_zw[...]) + mm(on_xy_low, hat_zw[...])
    at_vertex = jnp.sum(on_vertex * is_xy[...], axis=0, keepdims=True) * (1.0 / 1728.0)

    slots = slot[...]
    parts = jnp.concatenate([(slots >> 5).astype(F32), (slots & 31).astype(F32)], axis=0)
    picked = mm(parts.astype(BF16), pick_e[...])
    upper = jnp.sum(picked[0:8] * is_corner[...], axis=0, keepdims=True)
    lower = jnp.sum(picked[8:16] * is_corner[...], axis=0, keepdims=True)
    count = lax.broadcasted_iota(jnp.int32, (32, LANES), 0).astype(F32)
    is_upper = jnp.where(count == upper, 1.0, 0.0)
    is_lower = jnp.where(count == lower, 1.0, 0.0).astype(BF16)
    by_high, by_low = split(is_upper * at_vertex)
    small[...] = mm_t(by_high, is_lower) + mm_t(by_low, is_lower)

    eye = jnp.where(
        lax.broadcasted_iota(jnp.int32, (32, 32), 0) == lax.broadcasted_iota(jnp.int32, (32, 32), 1),
        1.0,
        0.0,
    )
    y_sums = [jnp.zeros((8, 128), F32) for _ in range(3)]
    for part in range(COARSE // 32):
        column = jnp.sum(small[part : part + 1, :] * eye, axis=1, keepdims=True)
        for level, factor in enumerate((x_local, x_middle, x_top)):
            weighted = column * factor[32 * part : 32 * part + 32, :]
            y_sums[level] = y_sums[level] + (
                (weighted[0:8] + weighted[8:16]) + (weighted[16:24] + weighted[24:32])
            )
    y_local, y_middle, y_top = [jnp.sum(value, axis=0, keepdims=True) for value in y_sums]
    row_number = lax.broadcasted_iota(jnp.int32, (8, 128), 0)
    y_rows[...] = jnp.broadcast_to(y_local, (8, 128))
    sent[0] = jnp.where(row_number == 0, y_middle, y_top)[0:2]

    def sums(peers, source, into, send, recv):
        return [
            pltpu.make_async_remote_copy(
                src_ref=source,
                dst_ref=into.at[k],
                send_sem=send.at[k],
                recv_sem=recv.at[k],
                device_id=device,
                device_id_type=MESH,
            )
            for k, (_, device, _) in enumerate(peers)
        ]

    first_sums = sums(peers_first, sent.at[0], got_first, first_send, first_recv)
    second_sums = sums(peers_second, sent.at[1], got_second, second_send, second_recv)

    def take_sums(copies, peers, own, into):
        for copy in copies:
            copy.wait_recv()
        value = sent[own]
        others = jnp.zeros_like(value)
        for k, (same_row, _, _) in enumerate(peers):
            if same_row:
                value = value + into[k]
            else:
                others = others + into[k]
        return jnp.where(row_number[0:2] == 0, value, value + others)

    def hear(number, count):
        @pl.when(count > 0)
        def _():
            pl.semaphore_wait(hello.at[number], count)

    hear(0, len(peers_first) - earlier_first)
    for copy in first_sums:
        copy.start()

    def forward_sums():
        sent[1] = take_sums(first_sums, peers_first, 0, got_first)
        hear(1, len(peers_second) - earlier_second)
        for copy in second_sums:
            copy.start()

    for load in loads[10:]:
        load.wait()
    raw = jnp.concatenate([vectors_raw[...], values_raw[...]], axis=0)
    raw_high, raw_rest = split(raw)
    ordered = mm(raw_high, order[...]) + mm(raw_rest, order[...])
    for tile in range(3):
        vectors[tile] = ordered[0:192, 128 * tile : 128 * tile + 128]
        values[tile] = ordered[192:216, 128 * tile : 128 * tile + 128]

    for number, (step_x, step_y) in enumerate(SIDES):
        plane = {1: 0, -1: PLANES - 1}.get(step_x)
        row = {1: 24, -1: 25}.get(step_y)

        @pl.when(came(step_x, step_y))
        def _(number=number, step_x=step_x, step_y=step_y, plane=plane, row=row):
            halo[number].wait_recv()
            if step_y == 0:
                rows[plane * ROWS : plane * ROWS + 24, :] = x_halo[number]
            elif step_x == 0:
                for x in range(NX):
                    at = (x + 1) * ROWS + row
                    rows[at : at + 1, :] = y_halo[number - 2, x : x + 1, :]
            else:
                rows[plane * ROWS + row : plane * ROWS + row + 1, :] = c_halo[number - 4]

    lane = lax.broadcasted_iota(jnp.int32, (8, 128), 1)
    masks = [(lane >> (2 + bit)) & 1 == 1 for bit in range(3)]

    def make_windows(a, carry):
        planes = [
            rows[pl.ds(pl.multiple_of((6 * i + a) * ROWS, ROWS), ROWS), :] for i in range(BX)
        ]
        both = jnp.concatenate(split(jnp.concatenate(planes, axis=0)), axis=0)
        along = mm_t(pick_z[...], both).astype(BF16)
        picked = mm(along, pick_y[...])
        for tile in range(3):
            first = tile * 64
            pieces = swap_chunks(
                [picked[first + 8 * l : first + 8 * l + 8, :] for l in range(8)], masks
            )
            for b in range(8):
                window[tile, a, b] = pieces[b]
        return carry

    lax.fori_loop(0, 8, make_windows, 0, unroll=8)

    def bcast(ref, tile, row):
        return ref[tile, pl.ds(row, 8, stride=0), :]

    def solve(tile, carry):
        for b in (0, 4):
            fields = [window[tile, a, b : b + 4] for a in range(8)]
            for p in range(8):
                value = None
                for a in range(8):
                    term = bcast(vectors, tile, a * 8 + p) * fields[a]
                    value = term if value is None else value + term
                stage[p, b : b + 4] = value

        def middle(p, carry):
            fields = [stage[p, b] for b in range(8)]
            turned = []
            for q in range(8):
                value = None
                for b in range(8):
                    term = bcast(vectors, tile, 64 + b * 8 + q) * fields[b]
                    value = term if value is None else value + term
                turned.append(value)
            along = [vectors[tile, 128 + 8 * c : 136 + 8 * c, :] for c in range(8)]
            scale = bcast(values, tile, p) + values[tile, 16:24, :]
            divided = []
            for q in range(8):
                value = None
                for c in range(8):
                    term = along[c] * turned[q][c : c + 1, :]
                    value = term if value is None else value + term
                divided.append(value / (scale + bcast(values, tile, 8 + q)))
            across = [vectors[tile, pl.ds(128 + s, 8, stride=8), :] for s in range(8)]
            back = []
            for q in range(8):
                value = None
                for s in range(8):
                    term = across[s] * divided[q][s : s + 1, :]
                    value = term if value is None else value + term
                back.append(value)
            for b in range(8):
                value = None
                for q in range(8):
                    term = bcast(vectors, tile, 64 + b * 8 + q) * back[q]
                    value = term if value is None else value + term
                stage[p, b] = value
            return carry

        lax.fori_loop(0, 8, middle, 0)
        for b in (0, 4):
            fields = [stage[p, b : b + 4] for p in range(8)]
            for a in range(8):
                value = None
                for p in range(8):
                    term = bcast(vectors, tile, a * 8 + p) * fields[p]
                    value = term if value is None else value + term
                solved[tile, a, b : b + 4] = value
        return carry

    lax.fori_loop(0, 2, solve, 0)
    pl.when(jnp.logical_not(middle_z))(forward_sums)
    lax.fori_loop(2, 3, solve, 0)

    def add_up(a):
        pieces = []
        for tile in range(3):
            pieces.extend(swap_chunks([solved[tile, a, b] for b in range(8)], masks))
        both = jnp.concatenate(split(jnp.concatenate(pieces, axis=0)), axis=1)
        along = mm(pick_zt[...], both)
        along = along[:, 0:128] + along[:, 128:256]
        return mm_t(pick_yt[...], jnp.concatenate(split(along), axis=1))

    def store_sums(a, carry):
        value = add_up(a)
        for i in range(BX):
            total_rows[pl.ds(pl.multiple_of((6 * i + a) * ROWS, ROWS), ROWS), :] = value[
                32 * i : 32 * i + 32, :
            ]
        return carry

    lax.fori_loop(0, 6, store_sums, 0, unroll=6)
    for a in (6, 7):
        value = add_up(a)
        for i in range(BX):
            here = slice((6 * i + a) * ROWS, (6 * i + a + 1) * ROWS)
            piece = value[32 * i : 32 * i + 32, :]
            total_rows[here, :] = piece if i == BX - 1 else total_rows[here, :] + piece

    rim = send_sides(
        total_rows,
        {1: PLANES - 1, -1: 0, 0: 0},
        {1: 25, -1: 24, 0: 0},
        (y_rim_pack, c_rim_pack),
        x_rim,
        y_rim,
        c_rim,
        rim_send,
        rim_recv,
    )
    start_sides(rim)

    for x in range(NX):
        at = (x + 1) * ROWS
        out[x] = total_rows[at : at + NY, :]

    def add_coarse():
        y_all = take_sums(second_sums, peers_second, 1, got_second)
        y_local = y_rows[0:1, :]
        y_middle = y_all[0:1, :]
        y_top = y_all[1:2, :]
        for part in range(COARSE // 32):
            here = slice(32 * part, 32 * part + 32)
            terms = x_local[here, :] * y_local + x_middle[here, :] * y_middle + x_top[here, :] * y_top
            column = jnp.sum(terms, axis=1, keepdims=True)
            vertex_col[part : part + 1, :] = jnp.sum(column * eye, axis=0, keepdims=True)
        vertex_col[20:32, :] = jnp.zeros((12, 32), F32)
        coarse_high, coarse_low = split(vertex_col[...])
        spread_out = mm(coarse_high, is_lower) + mm(coarse_low, is_lower)
        at_vertex = jnp.sum(spread_out * is_upper, axis=0, keepdims=True) * (1.0 / 1728.0)
        vertex_high, vertex_low = split(is_xy[...] * at_vertex)
        on_xy = mm_t(vertex_high, hat_zw[...]) + mm_t(vertex_low, hat_zw[...])
        field_high, field_low = split(on_xy)
        field = mm(hat_xy[...], field_high) + mm(hat_xy[...], field_low)
        for x in range(NX):
            out[x] = out[x] + field[x * ROWS : x * ROWS + NY, :]

    def add_rims():
        for number, (step_x, step_y) in enumerate(SIDES):
            x = {1: 0, -1: NX - 1}.get(step_x)
            y = {1: 0, -1: NY - 1}.get(step_y)

            @pl.when(came(step_x, step_y))
            def _(number=number, step_x=step_x, step_y=step_y, x=x, y=y):
                rim[number].wait_recv()
                if step_y == 0:
                    out[x] = out[x] + x_rim[number]
                elif step_x == 0:
                    for x in range(NX):
                        out[x, y : y + 1, :] = (
                            out[x, y : y + 1, :] + y_rim[number - 2, x : x + 1, :]
                        )
                else:
                    out[x, y : y + 1, :] = out[x, y : y + 1, :] + c_rim[number - 4]

    @pl.when(middle_z)
    def _():
        forward_sums()
        add_rims()
        add_coarse()

    @pl.when(jnp.logical_not(middle_z))
    def _():
        add_coarse()
        add_rims()

    for side, halo_copy, rim_copy in zip(SIDES, halo, rim):

        @pl.when(goes(*side))
        def _(halo_copy=halo_copy, rim_copy=rim_copy):
            halo_copy.wait_send()
            rim_copy.wait_send()

    for copy in first_sums + second_sums:
        copy.wait_send()


def local(residual, fdm_vectors, fdm_values, corner_slot, x_local, x_middle, x_top):
    n_group, n_dev = lax.axis_size("group"), lax.axis_size("dev")
    consts = tables()
    arguments = (
        residual,
        fdm_vectors.reshape(192, ELEMENTS),
        fdm_values.reshape(24, ELEMENTS),
        corner_slot,
        x_local,
        x_middle,
        x_top,
    ) + tuple(jnp.asarray(value) for value in consts)
    vmem = [pltpu.VMEM(value.shape, value.dtype) for value in arguments[1:]]
    n_sides = len(SIDES)
    scratch = (
        [pltpu.VMEM((PLANES, ROWS, NZ), F32)]
        + vmem
        + [
            pltpu.VMEM((3, 192, 128), F32),
            pltpu.VMEM((3, 24, 128), F32),
            pltpu.VMEM((3, 8, 8, 8, 128), F32),
            pltpu.VMEM((8, 8, 8, 128), F32),
            pltpu.VMEM((3, 8, 8, 8, 128), F32),
            pltpu.VMEM((PLANES, ROWS, NZ), F32),
            pltpu.VMEM((2, 24, NZ), F32),
            pltpu.VMEM((4, 1, NZ), F32),
            pltpu.VMEM((2, 24, NZ), F32),
            pltpu.VMEM((4, 1, NZ), F32),
            pltpu.VMEM((2, 24, NZ), F32),
            pltpu.VMEM((2, 24, NZ), F32),
            pltpu.VMEM((4, 1, NZ), F32),
            pltpu.VMEM((2, 24, NZ), F32),
            pltpu.VMEM((2, 24, NZ), F32),
            pltpu.VMEM((4, 1, NZ), F32),
            pltpu.VMEM((32, 32), F32),
            pltpu.VMEM((32, 32), F32),
            pltpu.VMEM((8, 128), F32),
            pltpu.VMEM((2, 2, 128), F32),
            pltpu.VMEM((16, 2, 128), F32),
            pltpu.VMEM((16, 2, 128), F32),
            pltpu.SemaphoreType.DMA((len(arguments),)),
            pltpu.SemaphoreType.DMA((n_sides,)),
            pltpu.SemaphoreType.DMA((n_sides,)),
            pltpu.SemaphoreType.DMA((n_sides,)),
            pltpu.SemaphoreType.DMA((n_sides,)),
            pltpu.SemaphoreType.DMA((16,)),
            pltpu.SemaphoreType.DMA((16,)),
            pltpu.SemaphoreType.DMA((16,)),
            pltpu.SemaphoreType.DMA((16,)),
            pltpu.SemaphoreType.REGULAR((2,)),
        ]
    )
    return pl.pallas_call(
        functools.partial(kernel, n_group, n_dev),
        out_shape=pltpu.VMEM((NX, NY, NZ), F32),
        in_specs=[pl.BlockSpec(memory_space=pl.ANY)] * len(arguments),
        out_specs=pl.BlockSpec(memory_space=pltpu.VMEM),
        scratch_shapes=scratch,
        compiler_params=pltpu.CompilerParams(
            collective_id=0, has_side_effects=True, vmem_limit_bytes=40 * 1024 * 1024
        ),
    )(*[pltpu.with_memory_space_constraint(value, pltpu.HBM) for value in arguments])


def solution(mesh):
    return jax.shard_map(
        local,
        mesh=mesh,
        in_specs=(
            P("group", "dev", None),
            P(None, None, None, ("group", "dev")),
            P(None, None, ("group", "dev")),
            P(None, ("group", "dev")),
            P(("group", "dev"), None),
            P(("group", "dev"), None),
            P(("group", "dev"), None),
        ),
        out_specs=P("group", "dev", None),
        check_vma=False,
    )
```

```python
import functools

import jax
import jax.numpy as jnp
import ml_dtypes
import numpy as np
from jax import lax
from jax.experimental import pallas as pl
from jax.experimental.pallas import tpu as pltpu
from jax.sharding import PartitionSpec as P

F32 = jnp.float32
BF16 = jnp.bfloat16
MESH = pl.DeviceIdType.MESH

BX, BY, BZ = 4, 4, 24
NX, NY, NZ = 6 * BX, 6 * BY, 6 * BZ
ELEMENTS = BX * BY * BZ
ROWS = 32
PLANES = NX + 2
LANES = 640
COARSE = 640
SIDES = ((1, 0), (-1, 0), (0, 1), (0, -1), (1, 1), (1, -1), (-1, 1), (-1, -1))


def row_of(y):
    return {0: 24, 25: 25}.get(y, y - 1)


def tables():
    bf16 = ml_dtypes.bfloat16
    pick_z = np.zeros((8 * BZ, NZ), np.float32)
    for l in range(BZ):
        for c in range(8):
            z = 6 * l + c - 1
            if 0 <= z < NZ:
                pick_z[8 * l + c, z] = 1
    pick_y = np.zeros((128, 128), np.float32)
    for i in range(4):
        for b in range(8):
            for j in range(4):
                pick_y[i * 32 + row_of(6 * j + b), i * 32 + b * 4 + j] = 1
    order = np.zeros((ELEMENTS, ELEMENTS), np.float32)
    for i in range(BX):
        for j in range(BY):
            for l in range(BZ):
                order[(i * BY + j) * BZ + l, l // 8 * 128 + i * 32 + l % 8 * 4 + j] = 1

    def hats(elements):
        weights = np.zeros((6 * elements, elements + 1), np.float32)
        for e in range(elements):
            for m in range(6):
                weights[6 * e + m, e] = 11 - 2 * m
                weights[6 * e + m, e + 1] = 2 * m + 1
        return weights

    hat_x, hat_y, hat_z = hats(BX), hats(BY), hats(BZ)
    hat_xy = np.zeros((NX, ROWS, 32), np.float32)
    hat_xy[:, :NY, :25] = np.einsum("xv,yw->xyvw", hat_x, hat_y).reshape(NX, NY, 25)
    hat_xy = hat_xy.reshape(NX * ROWS, 32)
    hat_zw = np.zeros((NZ, LANES), np.float32)
    is_xy = np.zeros((32, LANES), np.float32)
    others = LANES - ELEMENTS
    pick_e = np.zeros((ELEMENTS, others), np.float32)
    is_corner = np.zeros((8, others), np.float32)
    extra = 0
    for vx in range(5):
        for vy in range(5):
            for vz in range(25):
                i, j, l = min(vx, 3), min(vy, 3), min(vz, 23)
                corner = 4 * (vx - i) + 2 * (vy - j) + (vz - l)
                w = (i * BY + j) * BZ + l
                if corner:
                    pick_e[w, extra] = 1
                    is_corner[corner, extra] = 1
                    w = ELEMENTS + extra
                    extra += 1
                hat_zw[:, w] = hat_z[:, vz]
                is_xy[vx * 5 + vy, w] = 1
    return (
        pick_z.astype(bf16),
        pick_z.T.copy().astype(bf16),
        np.concatenate([pick_y, pick_y], axis=0).astype(bf16),
        np.concatenate([pick_y, pick_y], axis=1).astype(bf16),
        order.astype(bf16),
        np.concatenate([hat_xy, hat_xy], axis=1).astype(bf16),
        hat_xy.T.copy().astype(bf16),
        hat_zw.astype(bf16),
        pick_e.astype(bf16),
        is_xy,
        is_corner,
    )


def split(value):
    high = value.astype(BF16)
    return high, (value - high.astype(F32)).astype(BF16)


def mm(a, b):
    return lax.dot_general(a, b, (((1,), (0,)), ((), ())), preferred_element_type=F32)


def mm_rows(a, b, product):
    count = a.shape[0]
    value = product(jnp.concatenate(split(a), axis=0), b)
    return value[:count] + value[count:]


def mm_t(a, b):
    return lax.dot_general(a, b, (((1,), (1,)), ((), ())), preferred_element_type=F32)


def swap_chunks(pieces, masks):
    pieces = list(pieces)
    for bit in range(3):
        shift = 4 << bit
        mask = masks[bit]
        for low in range(8):
            if low >> bit & 1:
                continue
            high = low | 1 << bit
            x, y = pieces[low], pieces[high]
            pieces[low] = jnp.where(mask, pltpu.roll(y, shift, 1), x)
            pieces[high] = jnp.where(mask, y, pltpu.roll(x, 128 - shift, 1))
    return pieces


def kernel(
    n_group,
    n_dev,
    residual,
    vectors_in,
    values_in,
    slot_in,
    x_local_in,
    x_middle_in,
    x_top_in,
    pick_z_in,
    pick_zt_in,
    pick_y_in,
    pick_yt_in,
    order_in,
    hat_xy_in,
    hat_xyt_in,
    hat_zw_in,
    pick_e_in,
    is_xy_in,
    is_corner_in,
    out,
    block,
    vectors_raw,
    values_raw,
    slot,
    x_local,
    x_middle,
    x_top,
    pick_z,
    pick_zt,
    pick_y,
    pick_yt,
    order,
    hat_xy,
    hat_xyt,
    hat_zw,
    pick_e,
    is_xy,
    is_corner,
    vectors,
    values,
    window,
    stage,
    spare,
    solved,
    total,
    y_halo_pack,
    c_halo_pack,
    y_rim_pack,
    c_rim_pack,
    x_halo,
    y_halo,
    c_halo,
    x_rim,
    y_rim,
    c_rim,
    small,
    vertex_col,
    y_rows,
    sent,
    got_first,
    got_second,
    load_sem,
    halo_send,
    halo_recv,
    rim_send,
    rim_recv,
    first_send,
    first_recv,
    second_send,
    second_recv,
    hello,
):
    group = lax.axis_index("group")
    dev = lax.axis_index("dev")
    n_z = min(8, n_dev)
    n_x, n_y = n_dev // n_z, n_group // 2
    at_x, at_z = dev // n_z, dev % n_z
    at_y, core = group // 2, group % 2

    def beside(step_x, step_y):
        return (group + step_x, dev + step_y)

    def ahead(place, step, size):
        place = place + step
        return jnp.where(place >= size, place - size, place)

    def came(step_x, step_y):
        from_x, from_y = group - step_x, dev - step_y
        return (from_x >= 0) & (from_x < n_group) & (from_y >= 0) & (from_y < n_dev)

    def goes(step_x, step_y):
        return came(-step_x, -step_y)

    peers_first, peers_second = [], []
    for step in sorted(range(n_z), key=lambda step: -min(step, n_z - step)):
        for other in (1, 0):
            if step or other:
                to_z = ahead(at_z, step, n_z)
                to_core = 1 - core if other else core
                device = (2 * at_y + to_core, n_z * at_x + to_z)
                later = 2 * to_z + to_core > 2 * at_z + core
                peers_first.append((other == 0, device, later))
    pairs = [(step, other) for step in range(n_x) for other in range(n_y)]
    pairs.sort(key=lambda pair: -min(pair[0], n_x - pair[0]) - min(pair[1], n_y - pair[1]))
    for step, other in pairs:
        if step or other:
            to_x, to_y = ahead(at_x, step, n_x), ahead(at_y, other, n_y)
            device = (2 * to_y + core, n_z * to_x + at_z)
            later = n_y * to_x + to_y > n_y * at_x + at_y
            peers_second.append((other == 0, device, later))
    earlier_first = 2 * at_z + core
    earlier_second = n_y * at_x + at_y

    pairs = [
        (slot_in, slot),
        (pick_e_in, pick_e),
        (is_corner_in, is_corner),
        (residual, block.at[pl.ds(1, NX), pl.ds(0, NY), :]),
        (hat_xyt_in, hat_xyt),
        (hat_zw_in, hat_zw),
        (is_xy_in, is_xy),
        (x_local_in, x_local),
        (x_middle_in, x_middle),
        (x_top_in, x_top),
        (vectors_in, vectors_raw),
        (values_in, values_raw),
        (order_in, order),
        (pick_z_in, pick_z),
        (pick_y_in, pick_y),
        (pick_yt_in, pick_yt),
        (pick_zt_in, pick_zt),
        (hat_xy_in, hat_xy),
    ]
    loads = [
        pltpu.make_async_copy(source, target, load_sem.at[number])
        for number, (source, target) in enumerate(pairs)
    ]
    for load in loads:
        load.start()

    barrier = pltpu.get_barrier_semaphore()
    greeted = earlier_first + earlier_second
    for side in SIDES:
        greeted = greeted + goes(*side).astype(jnp.int32)

        @pl.when(goes(*side))
        def _(side=side):
            pl.semaphore_signal(barrier, inc=1, device_id=beside(*side), device_id_type=MESH)

    for _, device, later in peers_first + peers_second:

        @pl.when(later)
        def _(device=device):
            pl.semaphore_signal(barrier, inc=1, device_id=device, device_id_type=MESH)

    rows = block.reshape(PLANES * ROWS, NZ)
    total_rows = total.reshape(PLANES * ROWS, NZ)
    empty = jnp.zeros((8, NZ), F32)
    for plane in range(PLANES):
        for part in range(0 if plane in (0, PLANES - 1) else 24, ROWS, 8):
            rows[plane * ROWS + part : plane * ROWS + part + 8, :] = empty

    def send_sides(source, x_planes, y_rows_at, packs, x_into, y_into, c_into, send, recv):
        copies = []
        y_pack, c_pack = packs
        for number, (step_x, step_y) in enumerate(SIDES):
            plane = x_planes[step_x]
            row = y_rows_at[step_y]
            if step_y == 0:
                piece = source.at[pl.ds(plane * ROWS, 24), :]
                into = x_into.at[number]
            elif step_x == 0:
                for x in range(NX):
                    at = (x + 1) * ROWS + row
                    y_pack[number - 2, x : x + 1, :] = source[at : at + 1, :]
                piece = y_pack.at[number - 2]
                into = y_into.at[number - 2]
            else:
                c_pack[number - 4] = source[plane * ROWS + row : plane * ROWS + row + 1, :]
                piece = c_pack.at[number - 4]
                into = c_into.at[number - 4]
            copies.append(
                pltpu.make_async_remote_copy(
                    src_ref=piece,
                    dst_ref=into,
                    send_sem=send.at[number],
                    recv_sem=recv.at[number],
                    device_id=beside(step_x, step_y),
                    device_id_type=MESH,
                )
            )
        return copies

    pl.semaphore_wait(barrier, greeted)
    def answer(number, peers):
        for _, device, later in peers:

            @pl.when(jnp.logical_not(later))
            def _(device=device):
                pl.semaphore_signal(
                    hello.at[number], inc=1, device_id=device, device_id_type=MESH
                )

    def hear(number, count):
        @pl.when(count > 0)
        def _():
            pl.semaphore_wait(hello.at[number], count)

    answer(0, peers_first)
    for load in loads[0:3]:
        load.wait()
    slots = slot[...]
    parts = jnp.concatenate([(slots >> 5).astype(F32), (slots & 31).astype(F32)], axis=0)
    picked = mm(parts.astype(BF16), pick_e[...])
    upper = jnp.sum(picked[0:8] * is_corner[...], axis=0, keepdims=True)
    lower = jnp.sum(picked[8:16] * is_corner[...], axis=0, keepdims=True)
    upper = jnp.concatenate([parts[0:1], upper], axis=1)
    lower = jnp.concatenate([parts[8:9], lower], axis=1)
    count = lax.broadcasted_iota(jnp.int32, (32, LANES), 0).astype(F32)
    is_upper = jnp.where(count == upper, 1.0, 0.0)
    is_lower = jnp.where(count == lower, 1.0, 0.0).astype(BF16)
    loads[3].wait()
    halo = send_sides(
        rows,
        {1: 24, -1: 1, 0: 0},
        {1: 23, -1: 0, 0: 0},
        (y_halo_pack, c_halo_pack),
        x_halo,
        y_halo,
        c_halo,
        halo_send,
        halo_recv,
    )
    for side, copy in reversed(list(zip(SIDES, halo))):
        pl.when(goes(*side))(copy.start)

    for load in loads[4:10]:
        load.wait()
    own_high, own_low = split(rows[ROWS : ROWS * (NX + 1), :])
    on_xy = mm(hat_xyt[...], own_high) + mm(hat_xyt[...], own_low)
    on_vertex = mm_rows(on_xy, hat_zw[...], mm)
    at_vertex = jnp.sum(on_vertex * is_xy[...], axis=0, keepdims=True) * (1.0 / 1728.0)

    small[...] = mm_rows(is_upper * at_vertex, is_lower, mm_t)

    eye = jnp.where(
        lax.broadcasted_iota(jnp.int32, (32, 32), 0) == lax.broadcasted_iota(jnp.int32, (32, 32), 1),
        1.0,
        0.0,
    )
    y_sums = [jnp.zeros((8, 128), F32) for _ in range(3)]
    for part in range(COARSE // 32):
        column = jnp.sum(small[part : part + 1, :] * eye, axis=1, keepdims=True)
        for level, factor in enumerate((x_local, x_middle, x_top)):
            weighted = column * factor[32 * part : 32 * part + 32, :]
            y_sums[level] = y_sums[level] + (
                (weighted[0:8] + weighted[8:16]) + (weighted[16:24] + weighted[24:32])
            )
    y_local, y_middle, y_top = [jnp.sum(value, axis=0, keepdims=True) for value in y_sums]
    row_number = lax.broadcasted_iota(jnp.int32, (8, 128), 0)
    y_rows[...] = jnp.broadcast_to(y_local, (8, 128))
    sent[0] = jnp.where(row_number == 0, y_middle, y_top)[0:2]

    def sums(peers, source, into, send, recv):
        return [
            pltpu.make_async_remote_copy(
                src_ref=source,
                dst_ref=into.at[k],
                send_sem=send.at[k],
                recv_sem=recv.at[k],
                device_id=device,
                device_id_type=MESH,
            )
            for k, (_, device, _) in enumerate(peers)
        ]

    first_sums = sums(peers_first, sent.at[0], got_first, first_send, first_recv)
    second_sums = sums(peers_second, sent.at[1], got_second, second_send, second_recv)

    def take_sums(copies, peers, own, into):
        for copy in copies:
            copy.wait_recv()
        value = sent[own]
        others = jnp.zeros_like(value)
        for k, (same_row, _, _) in enumerate(peers):
            if same_row:
                value = value + into[k]
            else:
                others = others + into[k]
        return jnp.where(row_number[0:2] == 0, value, value + others)

    hear(0, len(peers_first) - earlier_first)
    for copy in first_sums:
        copy.start()
    answer(1, peers_second)

    def forward_sums():
        sent[1] = take_sums(first_sums, peers_first, 0, got_first)
        hear(1, len(peers_second) - earlier_second)
        for copy in second_sums:
            copy.start()

    for load in loads[10:]:
        load.wait()
    raw = jnp.concatenate([vectors_raw[...], values_raw[...]], axis=0)
    raw_high, raw_rest = split(raw)
    ordered = mm(raw_high, order[...]) + mm(raw_rest, order[...])
    for tile in range(3):
        vectors[tile] = ordered[0:192, 128 * tile : 128 * tile + 128]
        values[tile] = ordered[192:216, 128 * tile : 128 * tile + 128]

    for number, (step_x, step_y) in enumerate(SIDES):
        plane = {1: 0, -1: PLANES - 1}.get(step_x)
        row = {1: 24, -1: 25}.get(step_y)

        @pl.when(came(step_x, step_y))
        def _(number=number, step_x=step_x, step_y=step_y, plane=plane, row=row):
            halo[number].wait_recv()
            if step_y == 0:
                rows[plane * ROWS : plane * ROWS + 24, :] = x_halo[number]
            elif step_x == 0:
                for x in range(NX):
                    at = (x + 1) * ROWS + row
                    rows[at : at + 1, :] = y_halo[number - 2, x : x + 1, :]
            else:
                rows[plane * ROWS + row : plane * ROWS + row + 1, :] = c_halo[number - 4]

    lane = lax.broadcasted_iota(jnp.int32, (8, 128), 1)
    masks = [(lane >> (2 + bit)) & 1 == 1 for bit in range(3)]

    def make_windows(a, carry):
        planes = [
            rows[pl.ds(pl.multiple_of((6 * i + a) * ROWS, ROWS), ROWS), :] for i in range(BX)
        ]
        both = jnp.concatenate(split(jnp.concatenate(planes, axis=0)), axis=0)
        along = mm_t(pick_z[...], both).astype(BF16)
        picked = mm(along, pick_y[...])
        for tile in range(3):
            first = tile * 64
            pieces = swap_chunks(
                [picked[first + 8 * l : first + 8 * l + 8, :] for l in range(8)], masks
            )
            for b in range(8):
                window[tile, a, b] = pieces[b]
        return carry

    lax.fori_loop(0, 8, make_windows, 0, unroll=8)

    def bcast(ref, tile, row):
        return ref[tile, pl.ds(row, 8, stride=0), :]

    def solve(tile, carry):
        for b in (0, 4):
            fields = [window[tile, a, b : b + 4] for a in range(8)]
            for p in range(8):
                value = None
                for a in range(8):
                    term = bcast(vectors, tile, a * 8 + p) * fields[a]
                    value = term if value is None else value + term
                stage[p, b : b + 4] = value

        def middle(p, carry):
            fields = [stage[p, b] for b in range(8)]
            turned = []
            for q in range(8):
                value = None
                for b in range(8):
                    term = bcast(vectors, tile, 64 + b * 8 + q) * fields[b]
                    value = term if value is None else value + term
                turned.append(value)
            for q in range(8):
                spare[q] = turned[q]
            along = [vectors[tile, 128 + 8 * c : 136 + 8 * c, :] for c in range(8)]
            scale = bcast(values, tile, p) + values[tile, 16:24, :]
            divided = []
            for q in range(8):
                value = None
                for c in range(8):
                    term = along[c] * spare[q, pl.ds(c, 8, stride=0), :]
                    value = term if value is None else value + term
                below = scale + bcast(values, tile, 8 + q)
                inverse = pl.reciprocal(below, approx=True)
                divided.append(value * (inverse * (2.0 - below * inverse)))
            for q in range(8):
                spare[8 + q] = divided[q]
            across = [vectors[tile, pl.ds(128 + s, 8, stride=8), :] for s in range(8)]
            back = []
            for q in range(8):
                value = None
                for s in range(8):
                    term = across[s] * spare[8 + q, pl.ds(s, 8, stride=0), :]
                    value = term if value is None else value + term
                back.append(value)
            for b in range(8):
                value = None
                for q in range(8):
                    term = bcast(vectors, tile, 64 + b * 8 + q) * back[q]
                    value = term if value is None else value + term
                stage[p, b] = value
            return carry

        lax.fori_loop(0, 8, middle, 0, unroll=2)
        for b in (0, 4):
            fields = [stage[p, b : b + 4] for p in range(8)]
            for a in range(8):
                value = None
                for p in range(8):
                    term = bcast(vectors, tile, a * 8 + p) * fields[p]
                    value = term if value is None else value + term
                solved[tile, a, b : b + 4] = value
        return carry

    lax.fori_loop(0, 1, solve, 0)
    forward_sums()
    lax.fori_loop(1, 3, solve, 0)

    def add_up(a):
        pieces = []
        for tile in range(3):
            pieces.extend(swap_chunks([solved[tile, a, b] for b in range(8)], masks))
        both = jnp.concatenate(split(jnp.concatenate(pieces, axis=0)), axis=1)
        along = mm(pick_zt[...], both)
        along = along[:, 0:128] + along[:, 128:256]
        return mm_t(pick_yt[...], jnp.concatenate(split(along), axis=1))

    def store_sums(a, carry):
        value = add_up(a)
        for i in range(BX):
            total_rows[pl.ds(pl.multiple_of((6 * i + a) * ROWS, ROWS), ROWS), :] = value[
                32 * i : 32 * i + 32, :
            ]
        return carry

    lax.fori_loop(0, 6, store_sums, 0, unroll=6)
    for a in (6, 7):
        value = add_up(a)
        for i in range(BX):
            here = slice((6 * i + a) * ROWS, (6 * i + a + 1) * ROWS)
            piece = value[32 * i : 32 * i + 32, :]
            total_rows[here, :] = piece if i == BX - 1 else total_rows[here, :] + piece

    rim = send_sides(
        total_rows,
        {1: PLANES - 1, -1: 0, 0: 0},
        {1: 25, -1: 24, 0: 0},
        (y_rim_pack, c_rim_pack),
        x_rim,
        y_rim,
        c_rim,
        rim_send,
        rim_recv,
    )
    for side, copy in reversed(list(zip(SIDES, rim))):
        pl.when(goes(*side))(copy.start)

    for x in range(NX):
        at = (x + 1) * ROWS
        out[x] = total_rows[at : at + NY, :]

    def add_coarse():
        y_all = take_sums(second_sums, peers_second, 1, got_second)
        y_local = y_rows[0:1, :]
        y_middle = y_all[0:1, :]
        y_top = y_all[1:2, :]
        for part in range(COARSE // 32):
            here = slice(32 * part, 32 * part + 32)
            terms = x_local[here, :] * y_local + x_middle[here, :] * y_middle + x_top[here, :] * y_top
            column = jnp.sum(terms, axis=1, keepdims=True)
            vertex_col[part : part + 1, :] = jnp.sum(column * eye, axis=0, keepdims=True)
        vertex_col[20:32, :] = jnp.zeros((12, 32), F32)
        spread_out = mm_rows(vertex_col[...], is_lower, mm)
        at_vertex = jnp.sum(spread_out * is_upper, axis=0, keepdims=True) * (1.0 / 1728.0)
        on_xy = mm_rows(is_xy[...] * at_vertex, hat_zw[...], mm_t)
        field = mm(hat_xy[...], jnp.concatenate(split(on_xy), axis=0))
        for x in range(NX):
            out[x] = out[x] + field[x * ROWS : x * ROWS + NY, :]

    def add_rims():
        for number, (step_x, step_y) in enumerate(SIDES):
            x = {1: 0, -1: NX - 1}.get(step_x)
            y = {1: 0, -1: NY - 1}.get(step_y)

            @pl.when(came(step_x, step_y))
            def _(number=number, step_x=step_x, step_y=step_y, x=x, y=y):
                rim[number].wait_recv()
                if step_y == 0:
                    out[x] = out[x] + x_rim[number]
                elif step_x == 0:
                    for x in range(NX):
                        out[x, y : y + 1, :] = (
                            out[x, y : y + 1, :] + y_rim[number - 2, x : x + 1, :]
                        )
                else:
                    out[x, y : y + 1, :] = out[x, y : y + 1, :] + c_rim[number - 4]

    add_coarse()
    add_rims()

    for side, halo_copy, rim_copy in zip(SIDES, halo, rim):

        @pl.when(goes(*side))
        def _(halo_copy=halo_copy, rim_copy=rim_copy):
            halo_copy.wait_send()
            rim_copy.wait_send()

    for copy in first_sums + second_sums:
        copy.wait_send()


def local(residual, fdm_vectors, fdm_values, corner_slot, x_local, x_middle, x_top):
    n_group, n_dev = lax.axis_size("group"), lax.axis_size("dev")
    consts = tables()
    arguments = (
        residual,
        fdm_vectors.reshape(192, ELEMENTS),
        fdm_values.reshape(24, ELEMENTS),
        corner_slot,
        x_local,
        x_middle,
        x_top,
    ) + tuple(jnp.asarray(value) for value in consts)
    vmem = [pltpu.VMEM(value.shape, value.dtype) for value in arguments[1:]]
    n_sides = len(SIDES)
    scratch = (
        [pltpu.VMEM((PLANES, ROWS, NZ), F32)]
        + vmem
        + [
            pltpu.VMEM((3, 192, 128), F32),
            pltpu.VMEM((3, 24, 128), F32),
            pltpu.VMEM((3, 8, 8, 8, 128), F32),
            pltpu.VMEM((8, 8, 8, 128), F32),
            pltpu.VMEM((16, 8, 128), F32),
            pltpu.VMEM((3, 8, 8, 8, 128), F32),
            pltpu.VMEM((PLANES, ROWS, NZ), F32),
            pltpu.VMEM((2, 24, NZ), F32),
            pltpu.VMEM((4, 1, NZ), F32),
            pltpu.VMEM((2, 24, NZ), F32),
            pltpu.VMEM((4, 1, NZ), F32),
            pltpu.VMEM((2, 24, NZ), F32),
            pltpu.VMEM((2, 24, NZ), F32),
            pltpu.VMEM((4, 1, NZ), F32),
            pltpu.VMEM((2, 24, NZ), F32),
            pltpu.VMEM((2, 24, NZ), F32),
            pltpu.VMEM((4, 1, NZ), F32),
            pltpu.VMEM((32, 32), F32),
            pltpu.VMEM((32, 32), F32),
            pltpu.VMEM((8, 128), F32),
            pltpu.VMEM((2, 2, 128), F32),
            pltpu.VMEM((16, 2, 128), F32),
            pltpu.VMEM((16, 2, 128), F32),
            pltpu.SemaphoreType.DMA((len(arguments),)),
            pltpu.SemaphoreType.DMA((n_sides,)),
            pltpu.SemaphoreType.DMA((n_sides,)),
            pltpu.SemaphoreType.DMA((n_sides,)),
            pltpu.SemaphoreType.DMA((n_sides,)),
            pltpu.SemaphoreType.DMA((16,)),
            pltpu.SemaphoreType.DMA((16,)),
            pltpu.SemaphoreType.DMA((16,)),
            pltpu.SemaphoreType.DMA((16,)),
            pltpu.SemaphoreType.REGULAR((2,)),
        ]
    )
    return pl.pallas_call(
        functools.partial(kernel, n_group, n_dev),
        out_shape=pltpu.VMEM((NX, NY, NZ), F32),
        in_specs=[pl.BlockSpec(memory_space=pl.ANY)] * len(arguments),
        out_specs=pl.BlockSpec(memory_space=pltpu.VMEM),
        scratch_shapes=scratch,
        compiler_params=pltpu.CompilerParams(
            collective_id=0, has_side_effects=True, vmem_limit_bytes=40 * 1024 * 1024
        ),
    )(*[pltpu.with_memory_space_constraint(value, pltpu.HBM) for value in arguments])


def solution(mesh):
    return jax.shard_map(
        local,
        mesh=mesh,
        in_specs=(
            P("group", "dev", None),
            P(None, None, None, ("group", "dev")),
            P(None, None, ("group", "dev")),
            P(None, ("group", "dev")),
            P(("group", "dev"), None),
            P(("group", "dev"), None),
            P(("group", "dev"), None),
        ),
        out_specs=P("group", "dev", None),
        check_vma=False,
    )
```

```python
import functools

import jax
import jax.numpy as jnp
import ml_dtypes
import numpy as np
from jax import lax
from jax.experimental import pallas as pl
from jax.experimental.pallas import tpu as pltpu
from jax.sharding import PartitionSpec as P

F32 = jnp.float32
BF16 = jnp.bfloat16
MESH = pl.DeviceIdType.MESH

BX, BY, BZ = 4, 4, 24
NX, NY, NZ = 6 * BX, 6 * BY, 6 * BZ
ELEMENTS = BX * BY * BZ
ROWS = 32
PLANES = NX + 2
LANES = 640
COARSE = 640
SIDES = ((1, 0), (-1, 0), (0, 1), (0, -1), (1, 1), (1, -1), (-1, 1), (-1, -1))


def row_of(y):
    return {0: 24, 25: 25}.get(y, y - 1)


def tables():
    bf16 = ml_dtypes.bfloat16
    pick_z = np.zeros((8 * BZ, NZ), np.float32)
    for l in range(BZ):
        for c in range(8):
            z = 6 * l + c - 1
            if 0 <= z < NZ:
                pick_z[8 * l + c, z] = 1
    pick_y = np.zeros((128, 128), np.float32)
    for i in range(4):
        for b in range(8):
            for j in range(4):
                pick_y[i * 32 + row_of(6 * j + b), i * 32 + b * 4 + j] = 1
    pick_side = np.zeros((2, 2, NX, 6, 4, 8, 4), np.float32)
    for x in range(NX):
        for side, j in enumerate((0, 3)):
            pick_side[:, side, x, x % 6, x // 6, :, j] = 1
    pick_side = pick_side.reshape(96, 768)
    order = np.zeros((ELEMENTS, ELEMENTS), np.float32)
    for i in range(BX):
        for j in range(BY):
            for l in range(BZ):
                order[(i * BY + j) * BZ + l, l // 8 * 128 + i * 32 + l % 8 * 4 + j] = 1

    def hats(elements):
        weights = np.zeros((6 * elements, elements + 1), np.float32)
        for e in range(elements):
            for m in range(6):
                weights[6 * e + m, e] = 11 - 2 * m
                weights[6 * e + m, e + 1] = 2 * m + 1
        return weights

    hat_x, hat_y, hat_z = hats(BX), hats(BY), hats(BZ)
    hat_xy = np.zeros((NX, ROWS, 32), np.float32)
    hat_xy[:, :NY, :25] = np.einsum("xv,yw->xyvw", hat_x, hat_y).reshape(NX, NY, 25)
    hat_xy = hat_xy.reshape(NX * ROWS, 32)
    hat_zw = np.zeros((NZ, LANES), np.float32)
    is_xy = np.zeros((32, LANES), np.float32)
    others = LANES - ELEMENTS
    pick_e = np.zeros((ELEMENTS, others), np.float32)
    is_corner = np.zeros((8, others), np.float32)
    extra = 0
    for vx in range(5):
        for vy in range(5):
            for vz in range(25):
                i, j, l = min(vx, 3), min(vy, 3), min(vz, 23)
                corner = 4 * (vx - i) + 2 * (vy - j) + (vz - l)
                w = (i * BY + j) * BZ + l
                if corner:
                    pick_e[w, extra] = 1
                    is_corner[corner, extra] = 1
                    w = ELEMENTS + extra
                    extra += 1
                hat_zw[:, w] = hat_z[:, vz]
                is_xy[vx * 5 + vy, w] = 1
    return (
        pick_z.astype(bf16),
        pick_z.T.copy().astype(bf16),
        np.concatenate([pick_y, pick_y], axis=0).astype(bf16),
        np.concatenate([pick_y, pick_y], axis=1).astype(bf16),
        order.astype(bf16),
        pick_side.astype(bf16),
        np.concatenate([hat_xy, hat_xy], axis=1).astype(bf16),
        hat_xy.T.copy().astype(bf16),
        hat_zw.astype(bf16),
        pick_e.astype(bf16),
        is_xy,
        is_corner,
    )


def split(value):
    high = value.astype(BF16)
    return high, (value - high.astype(F32)).astype(BF16)


def mm(a, b):
    return lax.dot_general(a, b, (((1,), (0,)), ((), ())), preferred_element_type=F32)


def mm_rows(a, b, product):
    count = a.shape[0]
    value = product(jnp.concatenate(split(a), axis=0), b)
    return value[:count] + value[count:]


def mm_t(a, b):
    return lax.dot_general(a, b, (((1,), (1,)), ((), ())), preferred_element_type=F32)


def swap_chunks(pieces, masks):
    pieces = list(pieces)
    for bit in range(3):
        shift = 4 << bit
        mask = masks[bit]
        for low in range(8):
            if low >> bit & 1:
                continue
            high = low | 1 << bit
            x, y = pieces[low], pieces[high]
            pieces[low] = jnp.where(mask, pltpu.roll(y, shift, 1), x)
            pieces[high] = jnp.where(mask, y, pltpu.roll(x, 128 - shift, 1))
    return pieces


def kernel(
    n_group,
    n_dev,
    residual,
    vectors_in,
    values_in,
    slot_in,
    x_local_in,
    x_middle_in,
    x_top_in,
    pick_z_in,
    pick_zt_in,
    pick_y_in,
    pick_yt_in,
    order_in,
    pick_side_in,
    hat_xy_in,
    hat_xyt_in,
    hat_zw_in,
    pick_e_in,
    is_xy_in,
    is_corner_in,
    out,
    block,
    vectors_raw,
    values_raw,
    slot,
    x_local,
    x_middle,
    x_top,
    pick_z,
    pick_zt,
    pick_y,
    pick_yt,
    order,
    pick_side,
    hat_xy,
    hat_xyt,
    hat_zw,
    pick_e,
    is_xy,
    is_corner,
    vectors,
    values,
    window,
    stage,
    spare,
    solved,
    total,
    y_halo_pack,
    c_halo_pack,
    y_rim_pack,
    c_rim_pack,
    x_halo,
    y_halo,
    c_halo,
    x_rim,
    y_rim,
    c_rim,
    small,
    vertex_col,
    y_rows,
    sent,
    got_first,
    got_second,
    load_sem,
    halo_send,
    halo_recv,
    rim_send,
    rim_recv,
    first_send,
    first_recv,
    second_send,
    second_recv,
    hello,
):
    group = lax.axis_index("group")
    dev = lax.axis_index("dev")
    n_z = min(8, n_dev)
    n_x, n_y = n_dev // n_z, n_group // 2
    at_x, at_z = dev // n_z, dev % n_z
    at_y, core = group // 2, group % 2

    def beside(step_x, step_y):
        return (group + step_x, dev + step_y)

    def ahead(place, step, size):
        place = place + step
        return jnp.where(place >= size, place - size, place)

    def came(step_x, step_y):
        from_x, from_y = group - step_x, dev - step_y
        return (from_x >= 0) & (from_x < n_group) & (from_y >= 0) & (from_y < n_dev)

    def goes(step_x, step_y):
        return came(-step_x, -step_y)

    peers_first, peers_second = [], []
    for step in sorted(range(n_z), key=lambda step: -min(step, n_z - step)):
        for other in (1, 0):
            if step or other:
                to_z = ahead(at_z, step, n_z)
                to_core = 1 - core if other else core
                device = (2 * at_y + to_core, n_z * at_x + to_z)
                later = 2 * to_z + to_core > 2 * at_z + core
                peers_first.append((other == 0, device, later))
    pairs = [(step, other) for step in range(n_x) for other in range(n_y)]
    pairs.sort(key=lambda pair: -min(pair[0], n_x - pair[0]) - min(pair[1], n_y - pair[1]))
    for step, other in pairs:
        if step or other:
            to_x, to_y = ahead(at_x, step, n_x), ahead(at_y, other, n_y)
            device = (2 * to_y + core, n_z * to_x + at_z)
            later = n_y * to_x + to_y > n_y * at_x + at_y
            peers_second.append((other == 0, device, later))
    earlier_first = 2 * at_z + core
    earlier_second = n_y * at_x + at_y

    pairs = [
        (slot_in, slot),
        (pick_e_in, pick_e),
        (is_corner_in, is_corner),
        (residual, block.at[pl.ds(1, NX), pl.ds(0, NY), :]),
        (hat_xyt_in, hat_xyt),
        (hat_zw_in, hat_zw),
        (is_xy_in, is_xy),
        (x_local_in, x_local),
        (x_middle_in, x_middle),
        (x_top_in, x_top),
        (vectors_in, vectors_raw),
        (values_in, values_raw),
        (order_in, order),
        (pick_side_in, pick_side),
        (pick_z_in, pick_z),
        (pick_y_in, pick_y),
        (pick_yt_in, pick_yt),
        (pick_zt_in, pick_zt),
        (hat_xy_in, hat_xy),
    ]
    loads = [
        pltpu.make_async_copy(source, target, load_sem.at[number])
        for number, (source, target) in enumerate(pairs)
    ]
    for load in loads:
        load.start()

    barrier = pltpu.get_barrier_semaphore()
    greeted = earlier_first + earlier_second
    for side in SIDES:
        greeted = greeted + goes(*side).astype(jnp.int32)

        @pl.when(goes(*side))
        def _(side=side):
            pl.semaphore_signal(barrier, inc=1, device_id=beside(*side), device_id_type=MESH)

    for _, device, later in peers_first + peers_second:

        @pl.when(later)
        def _(device=device):
            pl.semaphore_signal(barrier, inc=1, device_id=device, device_id_type=MESH)

    rows = block.reshape(PLANES * ROWS, NZ)
    total_rows = total.reshape(PLANES * ROWS, NZ)
    empty = jnp.zeros((8, NZ), F32)
    for plane in range(PLANES):
        for part in range(0 if plane in (0, PLANES - 1) else 24, ROWS, 8):
            rows[plane * ROWS + part : plane * ROWS + part + 8, :] = empty

    def send_sides(source, x_planes, y_rows_at, packs, x_into, y_into, c_into, send, recv):
        copies = []
        y_pack, c_pack = packs
        for number, (step_x, step_y) in enumerate(SIDES):
            plane = x_planes[step_x]
            row = y_rows_at[step_y]
            if step_y == 0:
                piece = source.at[pl.ds(plane * ROWS, 24), :]
                into = x_into.at[number]
            elif step_x == 0:
                for x in range(NX):
                    at = (x + 1) * ROWS + row
                    y_pack[number - 2, x : x + 1, :] = source[at : at + 1, :]
                piece = y_pack.at[number - 2]
                into = y_into.at[number - 2]
            else:
                c_pack[number - 4] = source[plane * ROWS + row : plane * ROWS + row + 1, :]
                piece = c_pack.at[number - 4]
                into = c_into.at[number - 4]
            copies.append(
                pltpu.make_async_remote_copy(
                    src_ref=piece,
                    dst_ref=into,
                    send_sem=send.at[number],
                    recv_sem=recv.at[number],
                    device_id=beside(step_x, step_y),
                    device_id_type=MESH,
                )
            )
        return copies

    pl.semaphore_wait(barrier, greeted)
    def answer(number, peers):
        for _, device, later in peers:

            @pl.when(jnp.logical_not(later))
            def _(device=device):
                pl.semaphore_signal(
                    hello.at[number], inc=1, device_id=device, device_id_type=MESH
                )

    def hear(number, count):
        @pl.when(count > 0)
        def _():
            pl.semaphore_wait(hello.at[number], count)

    answer(0, peers_first)
    loads[3].wait()
    halo = send_sides(
        rows,
        {1: 24, -1: 1, 0: 0},
        {1: 23, -1: 0, 0: 0},
        (y_halo_pack, c_halo_pack),
        x_halo,
        y_halo,
        c_halo,
        halo_send,
        halo_recv,
    )
    for side, copy in reversed(list(zip(SIDES, halo))):
        pl.when(goes(*side))(copy.start)

    for load in loads[0:3]:
        load.wait()
    slots = slot[...]
    parts = jnp.concatenate([(slots >> 5).astype(F32), (slots & 31).astype(F32)], axis=0)
    picked = mm(parts.astype(BF16), pick_e[...])
    upper = jnp.sum(picked[0:8] * is_corner[...], axis=0, keepdims=True)
    lower = jnp.sum(picked[8:16] * is_corner[...], axis=0, keepdims=True)
    upper = jnp.concatenate([parts[0:1], upper], axis=1)
    lower = jnp.concatenate([parts[8:9], lower], axis=1)
    count = lax.broadcasted_iota(jnp.int32, (32, LANES), 0).astype(F32)
    is_upper = jnp.where(count == upper, 1.0, 0.0)
    is_lower = jnp.where(count == lower, 1.0, 0.0).astype(BF16)
    for load in loads[4:10]:
        load.wait()
    own_high, own_low = split(rows[ROWS : ROWS * (NX + 1), :])
    on_xy = mm(hat_xyt[...], own_high) + mm(hat_xyt[...], own_low)
    on_vertex = mm_rows(on_xy, hat_zw[...], mm)
    at_vertex = jnp.sum(on_vertex * is_xy[...], axis=0, keepdims=True) * (1.0 / 1728.0)

    small[...] = mm_rows(is_upper * at_vertex, is_lower, mm_t)

    eye = jnp.where(
        lax.broadcasted_iota(jnp.int32, (32, 32), 0) == lax.broadcasted_iota(jnp.int32, (32, 32), 1),
        1.0,
        0.0,
    )
    y_sums = [jnp.zeros((8, 128), F32) for _ in range(3)]
    for part in range(COARSE // 32):
        column = jnp.sum(small[part : part + 1, :] * eye, axis=1, keepdims=True)
        for level, factor in enumerate((x_local, x_middle, x_top)):
            weighted = column * factor[32 * part : 32 * part + 32, :]
            y_sums[level] = y_sums[level] + (
                (weighted[0:8] + weighted[8:16]) + (weighted[16:24] + weighted[24:32])
            )
    y_local, y_middle, y_top = [jnp.sum(value, axis=0, keepdims=True) for value in y_sums]
    row_number = lax.broadcasted_iota(jnp.int32, (8, 128), 0)
    y_rows[...] = jnp.broadcast_to(y_local, (8, 128))
    sent[0] = jnp.where(row_number == 0, y_middle, y_top)[0:2]

    def sums(peers, source, into, send, recv):
        return [
            pltpu.make_async_remote_copy(
                src_ref=source,
                dst_ref=into.at[k],
                send_sem=send.at[k],
                recv_sem=recv.at[k],
                device_id=device,
                device_id_type=MESH,
            )
            for k, (_, device, _) in enumerate(peers)
        ]

    first_sums = sums(peers_first, sent.at[0], got_first, first_send, first_recv)
    second_sums = sums(peers_second, sent.at[1], got_second, second_send, second_recv)

    def take_sums(copies, peers, own, into):
        for copy in copies:
            copy.wait_recv()
        value = sent[own]
        others = jnp.zeros_like(value)
        for k, (same_row, _, _) in enumerate(peers):
            if same_row:
                value = value + into[k]
            else:
                others = others + into[k]
        return jnp.where(row_number[0:2] == 0, value, value + others)

    for (_, _, later), copy in zip(peers_first, first_sums):
        pl.when(jnp.logical_not(later))(copy.start)
    answer(1, peers_second)

    def forward_sums():
        sent[1] = take_sums(first_sums, peers_first, 0, got_first)
        hear(1, len(peers_second) - earlier_second)
        for copy in second_sums:
            copy.start()

    for load in loads[10:]:
        load.wait()
    raw = jnp.concatenate([vectors_raw[...], values_raw[...]], axis=0)
    raw_high, raw_rest = split(raw)
    ordered = mm(raw_high, order[...]) + mm(raw_rest, order[...])
    for tile in range(3):
        vectors[tile] = ordered[0:192, 128 * tile : 128 * tile + 128]
        values[tile] = ordered[192:216, 128 * tile : 128 * tile + 128]

    lane = lax.broadcasted_iota(jnp.int32, (8, 128), 1)
    masks = [(lane >> (2 + bit)) & 1 == 1 for bit in range(3)]

    def make_windows(a, carry):
        planes = [
            rows[pl.ds(pl.multiple_of((6 * i + a) * ROWS, ROWS), ROWS), :] for i in range(BX)
        ]
        both = jnp.concatenate(split(jnp.concatenate(planes, axis=0)), axis=0)
        along = mm_t(pick_z[...], both).astype(BF16)
        picked = mm(along, pick_y[...])
        for tile in range(3):
            first = tile * 64
            pieces = swap_chunks(
                [picked[first + 8 * l : first + 8 * l + 8, :] for l in range(8)], masks
            )
            for b in range(8):
                window[tile, a, b] = pieces[b]
        return carry

    hear(0, len(peers_first) - earlier_first)
    for (_, _, later), copy in zip(peers_first, first_sums):
        pl.when(later)(copy.start)

    lax.fori_loop(1, 7, make_windows, 0, unroll=6)

    for number, (step_x, step_y) in enumerate(SIDES):
        plane = {1: 0, -1: PLANES - 1}.get(step_x)
        row = {1: 24, -1: 25}.get(step_y)

        @pl.when(came(step_x, step_y))
        def _(number=number, step_x=step_x, step_y=step_y, plane=plane, row=row):
            halo[number].wait_recv()
            if step_y == 0:
                rows[plane * ROWS : plane * ROWS + 24, :] = x_halo[number]
            elif step_x == 0:
                for x in range(NX):
                    at = (x + 1) * ROWS + row
                    rows[at : at + 1, :] = y_halo[number - 2, x : x + 1, :]
            else:
                rows[plane * ROWS + row : plane * ROWS + row + 1, :] = c_halo[number - 4]

    sides = [
        jnp.where(came(0, step), y_halo[number], 0.0) for number, step in enumerate((1, -1))
    ]
    both = jnp.concatenate(split(jnp.concatenate(sides, axis=0)), axis=0)
    beyond = mm(mm_t(pick_z[...], both).astype(BF16), pick_side[...])
    at_l = lane >> 2 & 7
    at_j = lane & 3
    for a in range(1, 7):
        column = slice(128 * (a - 1), 128 * a)
        for tile in range(3):
            value = jnp.zeros((8, 128), F32)
            for l in range(8):
                first = tile * 64 + 8 * l
                value = jnp.where(at_l == l, beyond[first : first + 8, column], value)
            window[tile, a, 0] = window[tile, a, 0] + jnp.where(at_j == 0, value, 0.0)
            window[tile, a, 7] = window[tile, a, 7] + jnp.where(at_j == 3, value, 0.0)
    make_windows(0, 0)
    make_windows(7, 0)

    def bcast(ref, tile, row):
        return ref[tile, pl.ds(row, 8, stride=0), :]

    def solve(tile, carry):
        for b in (0, 4):
            fields = [window[tile, a, b : b + 4] for a in range(8)]
            for p in range(8):
                value = None
                for a in range(8):
                    term = bcast(vectors, tile, a * 8 + p) * fields[a]
                    value = term if value is None else value + term
                stage[p, b : b + 4] = value

        def middle(p, carry):
            fields = [stage[p, b] for b in range(8)]
            turned = []
            for q in range(8):
                value = None
                for b in range(8):
                    term = bcast(vectors, tile, 64 + b * 8 + q) * fields[b]
                    value = term if value is None else value + term
                turned.append(value)
            for q in range(8):
                spare[q] = turned[q]
            along = [vectors[tile, 128 + 8 * c : 136 + 8 * c, :] for c in range(8)]
            scale = bcast(values, tile, p) + values[tile, 16:24, :]
            divided = []
            for q in range(8):
                value = None
                for c in range(8):
                    term = along[c] * spare[q, pl.ds(c, 8, stride=0), :]
                    value = term if value is None else value + term
                below = scale + bcast(values, tile, 8 + q)
                inverse = pl.reciprocal(below, approx=True)
                divided.append(value * (inverse * (2.0 - below * inverse)))
            for q in range(8):
                spare[8 + q] = divided[q]
            across = [vectors[tile, pl.ds(128 + s, 8, stride=8), :] for s in range(8)]
            back = []
            for q in range(8):
                value = None
                for s in range(8):
                    term = across[s] * spare[8 + q, pl.ds(s, 8, stride=0), :]
                    value = term if value is None else value + term
                back.append(value)
            for b in range(8):
                value = None
                for q in range(8):
                    term = bcast(vectors, tile, 64 + b * 8 + q) * back[q]
                    value = term if value is None else value + term
                stage[p, b] = value
            return carry

        lax.fori_loop(0, 8, middle, 0, unroll=2)
        for b in (0, 4):
            fields = [stage[p, b : b + 4] for p in range(8)]
            for a in range(8):
                value = None
                for p in range(8):
                    term = bcast(vectors, tile, a * 8 + p) * fields[p]
                    value = term if value is None else value + term
                solved[tile, a, b : b + 4] = value
        return carry

    lax.fori_loop(0, 1, solve, 0)
    forward_sums()
    lax.fori_loop(1, 3, solve, 0)

    def add_up(a):
        pieces = []
        for tile in range(3):
            pieces.extend(swap_chunks([solved[tile, a, b] for b in range(8)], masks))
        both = jnp.concatenate(split(jnp.concatenate(pieces, axis=0)), axis=1)
        along = mm(pick_zt[...], both)
        along = along[:, 0:128] + along[:, 128:256]
        return mm_t(pick_yt[...], jnp.concatenate(split(along), axis=1))

    def store_sums(a, carry):
        value = add_up(a)
        for i in range(BX):
            total_rows[pl.ds(pl.multiple_of((6 * i + a) * ROWS, ROWS), ROWS), :] = value[
                32 * i : 32 * i + 32, :
            ]
        return carry

    lax.fori_loop(0, 6, store_sums, 0, unroll=6)
    for a in (6, 7):
        value = add_up(a)
        for i in range(BX):
            here = slice((6 * i + a) * ROWS, (6 * i + a + 1) * ROWS)
            piece = value[32 * i : 32 * i + 32, :]
            total_rows[here, :] = piece if i == BX - 1 else total_rows[here, :] + piece

    rim = send_sides(
        total_rows,
        {1: PLANES - 1, -1: 0, 0: 0},
        {1: 25, -1: 24, 0: 0},
        (y_rim_pack, c_rim_pack),
        x_rim,
        y_rim,
        c_rim,
        rim_send,
        rim_recv,
    )
    for side, copy in reversed(list(zip(SIDES, rim))):
        pl.when(goes(*side))(copy.start)

    def add_coarse():
        y_all = take_sums(second_sums, peers_second, 1, got_second)
        y_local = y_rows[0:1, :]
        y_middle = y_all[0:1, :]
        y_top = y_all[1:2, :]
        for part in range(COARSE // 32):
            here = slice(32 * part, 32 * part + 32)
            terms = x_local[here, :] * y_local + x_middle[here, :] * y_middle + x_top[here, :] * y_top
            column = jnp.sum(terms, axis=1, keepdims=True)
            vertex_col[part : part + 1, :] = jnp.sum(column * eye, axis=0, keepdims=True)
        vertex_col[20:32, :] = jnp.zeros((12, 32), F32)
        spread_out = mm_rows(vertex_col[...], is_lower, mm)
        at_vertex = jnp.sum(spread_out * is_upper, axis=0, keepdims=True) * (1.0 / 1728.0)
        on_xy = mm_rows(is_xy[...] * at_vertex, hat_zw[...], mm_t)
        field = mm(hat_xy[...], jnp.concatenate(split(on_xy), axis=0))
        for x in range(NX):
            at = (x + 1) * ROWS
            out[x] = total_rows[at : at + NY, :] + field[x * ROWS : x * ROWS + NY, :]

    def add_rims():
        for number, (step_x, step_y) in enumerate(SIDES):
            x = {1: 0, -1: NX - 1}.get(step_x)
            y = {1: 0, -1: NY - 1}.get(step_y)

            @pl.when(came(step_x, step_y))
            def _(number=number, step_x=step_x, step_y=step_y, x=x, y=y):
                rim[number].wait_recv()
                if step_y == 0:
                    out[x] = out[x] + x_rim[number]
                elif step_x == 0:
                    for x in range(NX):
                        out[x, y : y + 1, :] = (
                            out[x, y : y + 1, :] + y_rim[number - 2, x : x + 1, :]
                        )
                else:
                    out[x, y : y + 1, :] = out[x, y : y + 1, :] + c_rim[number - 4]

    add_coarse()
    add_rims()

    for side, halo_copy, rim_copy in zip(SIDES, halo, rim):

        @pl.when(goes(*side))
        def _(halo_copy=halo_copy, rim_copy=rim_copy):
            halo_copy.wait_send()
            rim_copy.wait_send()

    for copy in first_sums + second_sums:
        copy.wait_send()


def local(residual, fdm_vectors, fdm_values, corner_slot, x_local, x_middle, x_top):
    n_group, n_dev = lax.axis_size("group"), lax.axis_size("dev")
    consts = tables()
    arguments = (
        residual,
        fdm_vectors.reshape(192, ELEMENTS),
        fdm_values.reshape(24, ELEMENTS),
        corner_slot,
        x_local,
        x_middle,
        x_top,
    ) + tuple(jnp.asarray(value) for value in consts)
    vmem = [pltpu.VMEM(value.shape, value.dtype) for value in arguments[1:]]
    n_sides = len(SIDES)
    scratch = (
        [pltpu.VMEM((PLANES, ROWS, NZ), F32)]
        + vmem
        + [
            pltpu.VMEM((3, 192, 128), F32),
            pltpu.VMEM((3, 24, 128), F32),
            pltpu.VMEM((3, 8, 8, 8, 128), F32),
            pltpu.VMEM((8, 8, 8, 128), F32),
            pltpu.VMEM((16, 8, 128), F32),
            pltpu.VMEM((3, 8, 8, 8, 128), F32),
            pltpu.VMEM((PLANES, ROWS, NZ), F32),
            pltpu.VMEM((2, 24, NZ), F32),
            pltpu.VMEM((4, 1, NZ), F32),
            pltpu.VMEM((2, 24, NZ), F32),
            pltpu.VMEM((4, 1, NZ), F32),
            pltpu.VMEM((2, 24, NZ), F32),
            pltpu.VMEM((2, 24, NZ), F32),
            pltpu.VMEM((4, 1, NZ), F32),
            pltpu.VMEM((2, 24, NZ), F32),
            pltpu.VMEM((2, 24, NZ), F32),
            pltpu.VMEM((4, 1, NZ), F32),
            pltpu.VMEM((32, 32), F32),
            pltpu.VMEM((32, 32), F32),
            pltpu.VMEM((8, 128), F32),
            pltpu.VMEM((2, 2, 128), F32),
            pltpu.VMEM((16, 2, 128), F32),
            pltpu.VMEM((16, 2, 128), F32),
            pltpu.SemaphoreType.DMA((len(arguments),)),
            pltpu.SemaphoreType.DMA((n_sides,)),
            pltpu.SemaphoreType.DMA((n_sides,)),
            pltpu.SemaphoreType.DMA((n_sides,)),
            pltpu.SemaphoreType.DMA((n_sides,)),
            pltpu.SemaphoreType.DMA((16,)),
            pltpu.SemaphoreType.DMA((16,)),
            pltpu.SemaphoreType.DMA((16,)),
            pltpu.SemaphoreType.DMA((16,)),
            pltpu.SemaphoreType.REGULAR((2,)),
        ]
    )
    return pl.pallas_call(
        functools.partial(kernel, n_group, n_dev),
        out_shape=pltpu.VMEM((NX, NY, NZ), F32),
        in_specs=[pl.BlockSpec(memory_space=pl.ANY)] * len(arguments),
        out_specs=pl.BlockSpec(memory_space=pltpu.VMEM),
        scratch_shapes=scratch,
        compiler_params=pltpu.CompilerParams(
            collective_id=0, has_side_effects=True, vmem_limit_bytes=40 * 1024 * 1024
        ),
    )(*[pltpu.with_memory_space_constraint(value, pltpu.HBM) for value in arguments])


def solution(mesh):
    return jax.shard_map(
        local,
        mesh=mesh,
        in_specs=(
            P("group", "dev", None),
            P(None, None, None, ("group", "dev")),
            P(None, None, ("group", "dev")),
            P(None, ("group", "dev")),
            P(("group", "dev"), None),
            P(("group", "dev"), None),
            P(("group", "dev"), None),
        ),
        out_specs=P("group", "dev", None),
        check_vma=False,
    )
```

```python
import functools

import jax
import jax.numpy as jnp
import ml_dtypes
import numpy as np
from jax import lax
from jax.experimental import pallas as pl
from jax.experimental.pallas import tpu as pltpu
from jax.sharding import PartitionSpec as P

F32 = jnp.float32
BF16 = jnp.bfloat16
MESH = pl.DeviceIdType.MESH

BX, BY, BZ = 4, 4, 24
NX, NY, NZ = 6 * BX, 6 * BY, 6 * BZ
ELEMENTS = BX * BY * BZ
ROWS = 32
PLANES = NX + 2
LANES = 640
COARSE = 640
SIDES = ((1, 0), (-1, 0), (0, 1), (0, -1), (1, 1), (1, -1), (-1, 1), (-1, -1))


def row_of(y):
    return {0: 24, 25: 25}.get(y, y - 1)


def tables():
    bf16 = ml_dtypes.bfloat16
    pick_z = np.zeros((8 * BZ, NZ), np.float32)
    for l in range(BZ):
        for c in range(8):
            z = 6 * l + c - 1
            if 0 <= z < NZ:
                pick_z[8 * l + c, z] = 1
    pick_y = np.zeros((128, 128), np.float32)
    for i in range(4):
        for b in range(8):
            for j in range(4):
                pick_y[i * 32 + row_of(6 * j + b), i * 32 + b * 4 + j] = 1
    pick_side = np.zeros((2, 2, NX, 6, 4, 8, 4), np.float32)
    for x in range(NX):
        for side, j in enumerate((0, 3)):
            pick_side[:, side, x, x % 6, x // 6, :, j] = 1
    pick_side = pick_side.reshape(96, 768)
    order = np.zeros((ELEMENTS, ELEMENTS), np.float32)
    for i in range(BX):
        for j in range(BY):
            for l in range(BZ):
                order[(i * BY + j) * BZ + l, l // 8 * 128 + i * 32 + l % 8 * 4 + j] = 1

    def hats(elements):
        weights = np.zeros((6 * elements, elements + 1), np.float32)
        for e in range(elements):
            for m in range(6):
                weights[6 * e + m, e] = 11 - 2 * m
                weights[6 * e + m, e + 1] = 2 * m + 1
        return weights

    hat_x, hat_y, hat_z = hats(BX), hats(BY), hats(BZ)
    hat_xy = np.zeros((NX, ROWS, 32), np.float32)
    hat_xy[:, :NY, :25] = np.einsum("xv,yw->xyvw", hat_x, hat_y).reshape(NX, NY, 25)
    hat_xy = hat_xy.reshape(NX * ROWS, 32)
    hat_zw = np.zeros((NZ, LANES), np.float32)
    is_xy = np.zeros((32, LANES), np.float32)
    others = LANES - ELEMENTS
    pick_e = np.zeros((ELEMENTS, others), np.float32)
    is_corner = np.zeros((8, others), np.float32)
    extra = 0
    for vx in range(5):
        for vy in range(5):
            for vz in range(25):
                i, j, l = min(vx, 3), min(vy, 3), min(vz, 23)
                corner = 4 * (vx - i) + 2 * (vy - j) + (vz - l)
                w = (i * BY + j) * BZ + l
                if corner:
                    pick_e[w, extra] = 1
                    is_corner[corner, extra] = 1
                    w = ELEMENTS + extra
                    extra += 1
                hat_zw[:, w] = hat_z[:, vz]
                is_xy[vx * 5 + vy, w] = 1
    return (
        pick_z.astype(bf16),
        pick_z.T.copy().astype(bf16),
        np.concatenate([pick_y, pick_y], axis=0).astype(bf16),
        np.concatenate([pick_y, pick_y], axis=1).astype(bf16),
        order.astype(bf16),
        pick_side.astype(bf16),
        np.concatenate([hat_xy, hat_xy], axis=1).astype(bf16),
        hat_xy.T.copy().astype(bf16),
        hat_zw.astype(bf16),
        pick_e.astype(bf16),
        is_xy,
        is_corner,
    )


def split(value):
    high = value.astype(BF16)
    return high, (value - high.astype(F32)).astype(BF16)


def mm(a, b):
    return lax.dot_general(a, b, (((1,), (0,)), ((), ())), preferred_element_type=F32)


def mm_rows(a, b, product):
    count = a.shape[0]
    value = product(jnp.concatenate(split(a), axis=0), b)
    return value[:count] + value[count:]


def mm_t(a, b):
    return lax.dot_general(a, b, (((1,), (1,)), ((), ())), preferred_element_type=F32)


def swap_chunks(pieces, masks):
    pieces = list(pieces)
    for bit in range(3):
        shift = 4 << bit
        mask = masks[bit]
        for low in range(8):
            if low >> bit & 1:
                continue
            high = low | 1 << bit
            x, y = pieces[low], pieces[high]
            pieces[low] = jnp.where(mask, pltpu.roll(y, shift, 1), x)
            pieces[high] = jnp.where(mask, y, pltpu.roll(x, 128 - shift, 1))
    return pieces


def kernel(
    n_group,
    n_dev,
    residual,
    vectors_in,
    values_in,
    slot_in,
    x_local_in,
    x_middle_in,
    x_top_in,
    pick_z_in,
    pick_zt_in,
    pick_y_in,
    pick_yt_in,
    order_in,
    pick_side_in,
    hat_xy_in,
    hat_xyt_in,
    hat_zw_in,
    pick_e_in,
    is_xy_in,
    is_corner_in,
    out,
    block,
    vectors_raw,
    values_raw,
    slot,
    x_local,
    x_middle,
    x_top,
    pick_z,
    pick_zt,
    pick_y,
    pick_yt,
    order,
    pick_side,
    hat_xy,
    hat_xyt,
    hat_zw,
    pick_e,
    is_xy,
    is_corner,
    vectors,
    values,
    window,
    stage,
    spare,
    solved,
    total,
    y_halo_pack,
    c_halo_pack,
    y_rim_pack,
    c_rim_pack,
    x_halo,
    y_halo,
    c_halo,
    x_rim,
    y_rim,
    c_rim,
    small,
    vertex_col,
    y_rows,
    sent,
    got_first,
    got_second,
    load_sem,
    halo_send,
    halo_recv,
    rim_send,
    rim_recv,
    first_send,
    first_recv,
    second_send,
    second_recv,
    hello,
):
    group = lax.axis_index("group")
    dev = lax.axis_index("dev")
    n_z = min(8, n_dev)
    n_x, n_y = n_dev // n_z, n_group // 2
    at_x, at_z = dev // n_z, dev % n_z
    at_y, core = group // 2, group % 2

    def beside(step_x, step_y):
        return (group + step_x, dev + step_y)

    def ahead(place, step, size):
        place = place + step
        return jnp.where(place >= size, place - size, place)

    def came(step_x, step_y):
        from_x, from_y = group - step_x, dev - step_y
        return (from_x >= 0) & (from_x < n_group) & (from_y >= 0) & (from_y < n_dev)

    def goes(step_x, step_y):
        return came(-step_x, -step_y)

    peers_first, peers_second = [], []
    for step in sorted(range(n_z), key=lambda step: -min(step, n_z - step)):
        for other in (1, 0):
            if step or other:
                to_z = ahead(at_z, step, n_z)
                to_core = 1 - core if other else core
                device = (2 * at_y + to_core, n_z * at_x + to_z)
                later = 2 * to_z + to_core > 2 * at_z + core
                peers_first.append((other == 0, device, later))
    pairs = [(step, other) for step in range(n_x) for other in range(n_y)]
    pairs.sort(key=lambda pair: -min(pair[0], n_x - pair[0]) - min(pair[1], n_y - pair[1]))
    for step, other in pairs:
        if step or other:
            to_x, to_y = ahead(at_x, step, n_x), ahead(at_y, other, n_y)
            device = (2 * to_y + core, n_z * to_x + at_z)
            later = n_y * to_x + to_y > n_y * at_x + at_y
            peers_second.append((other == 0, device, later))
    earlier_first = 2 * at_z + core
    earlier_second = n_y * at_x + at_y

    pairs = [
        (slot_in, slot),
        (pick_e_in, pick_e),
        (is_corner_in, is_corner),
        (residual, block.at[pl.ds(1, NX), pl.ds(0, NY), :]),
        (hat_xyt_in, hat_xyt),
        (hat_zw_in, hat_zw),
        (is_xy_in, is_xy),
        (x_local_in, x_local),
        (x_middle_in, x_middle),
        (x_top_in, x_top),
        (vectors_in, vectors_raw),
        (values_in, values_raw),
        (order_in, order),
        (pick_side_in, pick_side),
        (pick_z_in, pick_z),
        (pick_y_in, pick_y),
        (pick_yt_in, pick_yt),
        (pick_zt_in, pick_zt),
        (hat_xy_in, hat_xy),
    ]
    loads = [
        pltpu.make_async_copy(source, target, load_sem.at[number])
        for number, (source, target) in enumerate(pairs)
    ]
    for load in loads:
        load.start()

    barrier = pltpu.get_barrier_semaphore()
    greeted = earlier_first + earlier_second
    for side in SIDES:
        greeted = greeted + goes(*side).astype(jnp.int32)

        @pl.when(goes(*side))
        def _(side=side):
            pl.semaphore_signal(barrier, inc=1, device_id=beside(*side), device_id_type=MESH)

    for _, device, later in peers_first + peers_second:

        @pl.when(later)
        def _(device=device):
            pl.semaphore_signal(barrier, inc=1, device_id=device, device_id_type=MESH)

    rows = block.reshape(PLANES * ROWS, NZ)
    total_rows = total.reshape(PLANES * ROWS, NZ)
    empty = jnp.zeros((8, NZ), F32)
    for plane in range(PLANES):
        for part in range(0 if plane in (0, PLANES - 1) else 24, ROWS, 8):
            rows[plane * ROWS + part : plane * ROWS + part + 8, :] = empty

    def send_sides(source, x_planes, y_rows_at, packs, x_into, y_into, c_into, send, recv):
        copies = []
        y_pack, c_pack = packs
        for number, (step_x, step_y) in enumerate(SIDES):
            plane = x_planes[step_x]
            row = y_rows_at[step_y]
            if step_y == 0:
                piece = source.at[pl.ds(plane * ROWS, 24), :]
                into = x_into.at[number]
            elif step_x == 0:
                for x in range(NX):
                    at = (x + 1) * ROWS + row
                    y_pack[number - 2, x : x + 1, :] = source[at : at + 1, :]
                piece = y_pack.at[number - 2]
                into = y_into.at[number - 2]
            else:
                c_pack[number - 4] = source[plane * ROWS + row : plane * ROWS + row + 1, :]
                piece = c_pack.at[number - 4]
                into = c_into.at[number - 4]
            copies.append(
                pltpu.make_async_remote_copy(
                    src_ref=piece,
                    dst_ref=into,
                    send_sem=send.at[number],
                    recv_sem=recv.at[number],
                    device_id=beside(step_x, step_y),
                    device_id_type=MESH,
                )
            )
        return copies

    pl.semaphore_wait(barrier, greeted)
    def answer(number, peers):
        for _, device, later in peers:

            @pl.when(jnp.logical_not(later))
            def _(device=device):
                pl.semaphore_signal(
                    hello.at[number], inc=1, device_id=device, device_id_type=MESH
                )

    def hear(number, count):
        @pl.when(count > 0)
        def _():
            pl.semaphore_wait(hello.at[number], count)

    answer(0, peers_first)
    loads[3].wait()
    halo = send_sides(
        rows,
        {1: 24, -1: 1, 0: 0},
        {1: 23, -1: 0, 0: 0},
        (y_halo_pack, c_halo_pack),
        x_halo,
        y_halo,
        c_halo,
        halo_send,
        halo_recv,
    )
    for side, copy in reversed(list(zip(SIDES, halo))):
        pl.when(goes(*side))(copy.start)

    for load in loads[0:3]:
        load.wait()
    slots = slot[...]
    parts = jnp.concatenate([(slots >> 5).astype(F32), (slots & 31).astype(F32)], axis=0)
    picked = mm(parts.astype(BF16), pick_e[...])
    upper = jnp.sum(picked[0:8] * is_corner[...], axis=0, keepdims=True)
    lower = jnp.sum(picked[8:16] * is_corner[...], axis=0, keepdims=True)
    upper = jnp.concatenate([parts[0:1], upper], axis=1)
    lower = jnp.concatenate([parts[8:9], lower], axis=1)
    count = lax.broadcasted_iota(jnp.int32, (32, LANES), 0).astype(F32)
    is_upper = jnp.where(count == upper, 1.0, 0.0)
    is_lower = jnp.where(count == lower, 1.0, 0.0).astype(BF16)
    for load in loads[4:10]:
        load.wait()
    own_high, own_low = split(rows[ROWS : ROWS * (NX + 1), :])
    on_xy = mm(hat_xyt[...], own_high) + mm(hat_xyt[...], own_low)
    on_vertex = mm_rows(on_xy, hat_zw[...], mm)
    at_vertex = jnp.sum(on_vertex * is_xy[...], axis=0, keepdims=True) * (1.0 / 1728.0)

    small[...] = mm_rows(is_upper * at_vertex, is_lower, mm_t)

    eye = jnp.where(
        lax.broadcasted_iota(jnp.int32, (32, 32), 0) == lax.broadcasted_iota(jnp.int32, (32, 32), 1),
        1.0,
        0.0,
    )
    y_sums = [jnp.zeros((8, 128), F32) for _ in range(3)]
    for part in range(COARSE // 32):
        column = jnp.sum(small[part : part + 1, :] * eye, axis=1, keepdims=True)
        for level, factor in enumerate((x_local, x_middle, x_top)):
            weighted = column * factor[32 * part : 32 * part + 32, :]
            y_sums[level] = y_sums[level] + (
                (weighted[0:8] + weighted[8:16]) + (weighted[16:24] + weighted[24:32])
            )
    y_local, y_middle, y_top = [jnp.sum(value, axis=0, keepdims=True) for value in y_sums]
    row_number = lax.broadcasted_iota(jnp.int32, (8, 128), 0)
    y_rows[...] = jnp.broadcast_to(y_local, (8, 128))
    sent[0] = jnp.where(row_number == 0, y_middle, y_top)[0:2]

    def sums(peers, source, into, send, recv):
        return [
            pltpu.make_async_remote_copy(
                src_ref=source,
                dst_ref=into.at[k],
                send_sem=send.at[k],
                recv_sem=recv.at[k],
                device_id=device,
                device_id_type=MESH,
            )
            for k, (_, device, _) in enumerate(peers)
        ]

    first_sums = sums(peers_first, sent.at[0], got_first, first_send, first_recv)
    second_sums = sums(peers_second, sent.at[1], got_second, second_send, second_recv)

    def take_sums(copies, peers, own, into):
        for copy in copies:
            copy.wait_recv()
        value = sent[own]
        others = jnp.zeros_like(value)
        for k, (same_row, _, _) in enumerate(peers):
            if same_row:
                value = value + into[k]
            else:
                others = others + into[k]
        return jnp.where(row_number[0:2] == 0, value, value + others)

    for (_, _, later), copy in zip(peers_first, first_sums):
        pl.when(jnp.logical_not(later))(copy.start)
    answer(1, peers_second)

    def forward_sums():
        sent[1] = take_sums(first_sums, peers_first, 0, got_first)
        hear(1, len(peers_second) - earlier_second)
        for copy in second_sums:
            copy.start()

    for load in loads[10:]:
        load.wait()
    raw = jnp.concatenate([vectors_raw[...], values_raw[...]], axis=0)
    raw_high, raw_rest = split(raw)
    ordered = mm(raw_high, order[...]) + mm(raw_rest, order[...])
    for tile in range(3):
        vectors[tile] = ordered[0:192, 128 * tile : 128 * tile + 128]
        values[tile] = ordered[192:216, 128 * tile : 128 * tile + 128]

    lane = lax.broadcasted_iota(jnp.int32, (8, 128), 1)
    masks = [(lane >> (2 + bit)) & 1 == 1 for bit in range(3)]

    def make_windows(a, carry):
        planes = [
            rows[pl.ds(pl.multiple_of((6 * i + a) * ROWS, ROWS), ROWS), :] for i in range(BX)
        ]
        both = jnp.concatenate(split(jnp.concatenate(planes, axis=0)), axis=0)
        along = mm_t(pick_z[...], both).astype(BF16)
        picked = mm(along, pick_y[...])
        for tile in range(3):
            first = tile * 64
            pieces = swap_chunks(
                [picked[first + 8 * l : first + 8 * l + 8, :] for l in range(8)], masks
            )
            for b in range(8):
                window[tile, a, b] = pieces[b]
        return carry

    hear(0, len(peers_first) - earlier_first)
    for (_, _, later), copy in zip(peers_first, first_sums):
        pl.when(later)(copy.start)

    lax.fori_loop(1, 7, make_windows, 0, unroll=6)

    for number, (step_x, step_y) in enumerate(SIDES):
        plane = {1: 0, -1: PLANES - 1}.get(step_x)
        row = {1: 24, -1: 25}.get(step_y)

        @pl.when(came(step_x, step_y))
        def _(number=number, step_x=step_x, step_y=step_y, plane=plane, row=row):
            halo[number].wait_recv()
            if step_y == 0:
                rows[plane * ROWS : plane * ROWS + 24, :] = x_halo[number]
            elif step_x == 0:
                for x in range(NX):
                    at = (x + 1) * ROWS + row
                    rows[at : at + 1, :] = y_halo[number - 2, x : x + 1, :]
            else:
                rows[plane * ROWS + row : plane * ROWS + row + 1, :] = c_halo[number - 4]

    sides = [
        jnp.where(came(0, step), y_halo[number], 0.0) for number, step in enumerate((1, -1))
    ]
    both = jnp.concatenate(split(jnp.concatenate(sides, axis=0)), axis=0)
    beyond = mm(mm_t(pick_z[...], both).astype(BF16), pick_side[...])
    at_l = lane >> 2 & 7
    at_j = lane & 3
    for a in range(1, 7):
        column = slice(128 * (a - 1), 128 * a)
        for tile in range(3):
            value = jnp.zeros((8, 128), F32)
            for l in range(8):
                first = tile * 64 + 8 * l
                value = jnp.where(at_l == l, beyond[first : first + 8, column], value)
            window[tile, a, 0] = window[tile, a, 0] + jnp.where(at_j == 0, value, 0.0)
            window[tile, a, 7] = window[tile, a, 7] + jnp.where(at_j == 3, value, 0.0)
    make_windows(0, 0)
    make_windows(7, 0)

    def bcast(ref, tile, row):
        return ref[tile, pl.ds(row, 8, stride=0), :]

    def solve(tile, carry):
        for b in (0, 4):
            fields = [window[tile, a, b : b + 4] for a in range(8)]
            for p in range(8):
                value = None
                for a in range(8):
                    term = bcast(vectors, tile, a * 8 + p) * fields[a]
                    value = term if value is None else value + term
                stage[p, b : b + 4] = value

        def middle(p, carry):
            fields = [stage[p, b] for b in range(8)]
            turned = []
            for q in range(8):
                value = None
                for b in range(8):
                    term = bcast(vectors, tile, 64 + b * 8 + q) * fields[b]
                    value = term if value is None else value + term
                turned.append(value)
            for q in range(8):
                spare[q, 0:8, :] = turned[q]
            along = [vectors[tile, 128 + 8 * c : 136 + 8 * c, :] for c in range(8)]
            scale = bcast(values, tile, p) + values[tile, 16:24, :]
            divided = []
            for q in range(8):
                value = None
                for c in range(8):
                    term = along[c] * spare[q, pl.ds(c, 8, stride=0), :]
                    value = term if value is None else value + term
                below = scale + bcast(values, tile, 8 + q)
                inverse = pl.reciprocal(below, approx=True)
                divided.append(value * (inverse * (2.0 - below * inverse)))
            for q in range(8):
                spare[8 + q, 0:8, :] = divided[q]
            across = [vectors[tile, pl.ds(128 + s, 8, stride=8), :] for s in range(8)]
            back = []
            for q in range(8):
                value = None
                for s in range(8):
                    term = across[s] * spare[8 + q, pl.ds(s, 8, stride=0), :]
                    value = term if value is None else value + term
                back.append(value)
            for b in range(8):
                value = None
                for q in range(8):
                    term = bcast(vectors, tile, 64 + b * 8 + q) * back[q]
                    value = term if value is None else value + term
                stage[p, b] = value
            return carry

        lax.fori_loop(0, 8, middle, 0, unroll=2)
        for b in (0, 4):
            fields = [stage[p, b : b + 4] for p in range(8)]
            for a in range(8):
                value = None
                for p in range(8):
                    term = bcast(vectors, tile, a * 8 + p) * fields[p]
                    value = term if value is None else value + term
                solved[tile, a, b : b + 4] = value
        return carry

    lax.fori_loop(0, 1, solve, 0)
    forward_sums()
    lax.fori_loop(1, 3, solve, 0)

    def add_up(a):
        pieces = []
        for tile in range(3):
            pieces.extend(swap_chunks([solved[tile, a, b] for b in range(8)], masks))
        both = jnp.concatenate(split(jnp.concatenate(pieces, axis=0)), axis=1)
        along = mm(pick_zt[...], both)
        along = along[:, 0:128] + along[:, 128:256]
        return mm_t(pick_yt[...], jnp.concatenate(split(along), axis=1))

    def store_sums(a, carry):
        value = add_up(a)
        for i in range(BX):
            total_rows[pl.ds(pl.multiple_of((6 * i + a) * ROWS, ROWS), ROWS), :] = value[
                32 * i : 32 * i + 32, :
            ]
        return carry

    lax.fori_loop(0, 6, store_sums, 0, unroll=6)
    for a in (6, 7):
        value = add_up(a)
        for i in range(BX):
            here = slice((6 * i + a) * ROWS, (6 * i + a + 1) * ROWS)
            piece = value[32 * i : 32 * i + 32, :]
            total_rows[here, :] = piece if i == BX - 1 else total_rows[here, :] + piece

    rim = send_sides(
        total_rows,
        {1: PLANES - 1, -1: 0, 0: 0},
        {1: 25, -1: 24, 0: 0},
        (y_rim_pack, c_rim_pack),
        x_rim,
        y_rim,
        c_rim,
        rim_send,
        rim_recv,
    )
    for side, copy in reversed(list(zip(SIDES, rim))):
        pl.when(goes(*side))(copy.start)

    def add_coarse():
        y_all = take_sums(second_sums, peers_second, 1, got_second)
        y_local = y_rows[0:1, :]
        y_middle = y_all[0:1, :]
        y_top = y_all[1:2, :]
        for part in range(COARSE // 32):
            here = slice(32 * part, 32 * part + 32)
            terms = x_local[here, :] * y_local + x_middle[here, :] * y_middle + x_top[here, :] * y_top
            column = jnp.sum(terms, axis=1, keepdims=True)
            vertex_col[part : part + 1, :] = jnp.sum(column * eye, axis=0, keepdims=True)
        vertex_col[20:32, :] = jnp.zeros((12, 32), F32)
        spread_out = mm_rows(vertex_col[...], is_lower, mm)
        at_vertex = jnp.sum(spread_out * is_upper, axis=0, keepdims=True) * (1.0 / 1728.0)
        on_xy = mm_rows(is_xy[...] * at_vertex, hat_zw[...], mm_t)
        field = mm(hat_xy[...], jnp.concatenate(split(on_xy), axis=0))
        for x in range(NX):
            at = (x + 1) * ROWS
            out[x] = total_rows[at : at + NY, :] + field[x * ROWS : x * ROWS + NY, :]

    def add_rims():
        for number, (step_x, step_y) in enumerate(SIDES):
            x = {1: 0, -1: NX - 1}.get(step_x)
            y = {1: 0, -1: NY - 1}.get(step_y)

            @pl.when(came(step_x, step_y))
            def _(number=number, step_x=step_x, step_y=step_y, x=x, y=y):
                rim[number].wait_recv()
                if step_y == 0:
                    out[x] = out[x] + x_rim[number]
                elif step_x == 0:
                    for x in range(NX):
                        out[x, y : y + 1, :] = (
                            out[x, y : y + 1, :] + y_rim[number - 2, x : x + 1, :]
                        )
                else:
                    out[x, y : y + 1, :] = out[x, y : y + 1, :] + c_rim[number - 4]

    add_coarse()
    add_rims()

    for side, halo_copy, rim_copy in zip(SIDES, halo, rim):

        @pl.when(goes(*side))
        def _(halo_copy=halo_copy, rim_copy=rim_copy):
            halo_copy.wait_send()
            rim_copy.wait_send()

    for copy in first_sums + second_sums:
        copy.wait_send()


def local(residual, fdm_vectors, fdm_values, corner_slot, x_local, x_middle, x_top):
    n_group, n_dev = lax.axis_size("group"), lax.axis_size("dev")
    consts = tables()
    arguments = (
        residual,
        fdm_vectors.reshape(192, ELEMENTS),
        fdm_values.reshape(24, ELEMENTS),
        corner_slot,
        x_local,
        x_middle,
        x_top,
    ) + tuple(jnp.asarray(value) for value in consts)
    vmem = [pltpu.VMEM(value.shape, value.dtype) for value in arguments[1:]]
    n_sides = len(SIDES)
    scratch = (
        [pltpu.VMEM((PLANES, ROWS, NZ), F32)]
        + vmem
        + [
            pltpu.VMEM((3, 192, 128), F32),
            pltpu.VMEM((3, 24, 128), F32),
            pltpu.VMEM((3, 8, 8, 8, 128), F32),
            pltpu.VMEM((8, 8, 8, 128), F32),
            pltpu.VMEM((16, 16, 128), F32),
            pltpu.VMEM((3, 8, 8, 8, 128), F32),
            pltpu.VMEM((PLANES, ROWS, NZ), F32),
            pltpu.VMEM((2, 24, NZ), F32),
            pltpu.VMEM((4, 1, NZ), F32),
            pltpu.VMEM((2, 24, NZ), F32),
            pltpu.VMEM((4, 1, NZ), F32),
            pltpu.VMEM((2, 24, NZ), F32),
            pltpu.VMEM((2, 24, NZ), F32),
            pltpu.VMEM((4, 1, NZ), F32),
            pltpu.VMEM((2, 24, NZ), F32),
            pltpu.VMEM((2, 24, NZ), F32),
            pltpu.VMEM((4, 1, NZ), F32),
            pltpu.VMEM((32, 32), F32),
            pltpu.VMEM((32, 32), F32),
            pltpu.VMEM((8, 128), F32),
            pltpu.VMEM((2, 2, 128), F32),
            pltpu.VMEM((16, 2, 128), F32),
            pltpu.VMEM((16, 2, 128), F32),
            pltpu.SemaphoreType.DMA((len(arguments),)),
            pltpu.SemaphoreType.DMA((n_sides,)),
            pltpu.SemaphoreType.DMA((n_sides,)),
            pltpu.SemaphoreType.DMA((n_sides,)),
            pltpu.SemaphoreType.DMA((n_sides,)),
            pltpu.SemaphoreType.DMA((16,)),
            pltpu.SemaphoreType.DMA((16,)),
            pltpu.SemaphoreType.DMA((16,)),
            pltpu.SemaphoreType.DMA((16,)),
            pltpu.SemaphoreType.REGULAR((2,)),
        ]
    )
    return pl.pallas_call(
        functools.partial(kernel, n_group, n_dev),
        out_shape=pltpu.VMEM((NX, NY, NZ), F32),
        in_specs=[pl.BlockSpec(memory_space=pl.ANY)] * len(arguments),
        out_specs=pl.BlockSpec(memory_space=pltpu.VMEM),
        scratch_shapes=scratch,
        compiler_params=pltpu.CompilerParams(
            collective_id=0, has_side_effects=True, vmem_limit_bytes=40 * 1024 * 1024
        ),
    )(*[pltpu.with_memory_space_constraint(value, pltpu.HBM) for value in arguments])


def solution(mesh):
    return jax.shard_map(
        local,
        mesh=mesh,
        in_specs=(
            P("group", "dev", None),
            P(None, None, None, ("group", "dev")),
            P(None, None, ("group", "dev")),
            P(None, ("group", "dev")),
            P(("group", "dev"), None),
            P(("group", "dev"), None),
            P(("group", "dev"), None),
        ),
        out_specs=P("group", "dev", None),
        check_vma=False,
    )
```
